1024 devices in a mesh: region: 32 (over x, y, core), span: 32 (over z).
Axes of the slice: x: 4, y: 4, z: 32, core: 2. Of those that a mesh axis runs over, the one named last changes fastest.
Arguments:
- column_state: bfloat16 [65536, 288], P(('region', 'span')), may hold values from -5 to 5
- crm_fields: bfloat16 [65536, 5568], P(('region', 'span')), may hold values from -5 to 5
- span_map: int32 [65536], P(('region', 'span')), may hold values from 0 to 31, as said below
- active: int32 [65536], P(('region', 'span')), may hold values from 0 to 1
- density: float32 [58], replicated, may hold values from 0.3 to 1
- nbr_elem: int32 [16384, 4], P(('region', 'span')), may hold values from 0 to 16383, as said below
- nbr_side: int32 [16384, 4], P(('region', 'span')), may hold values from 0 to 3
Outputs:
- column_tendency: bfloat16 [65536, 288], P(('region', 'span'))
- crm_next: bfloat16 [65536, 5568], P(('region', 'span'))
- span_precip: float32 [24576], P(('region', 'span'))
- edge_sums: float32 [16384, 4, 288], P(('region', 'span'))
The draws below stay inside these ranges and needn't reach their ends.
Inputs may be any that keep to these rules, and one draw needn't show every extreme that they name: `span_map`: among the active columns of one device at most 2 name the same span, and the devices of a region send at most 24 active columns to one span; both bounds are reached in every draw. `nbr_elem`: the neighbour across a side of element e lies within 8 of e in the element order wrapped at 16384, never e itself; distance 8 occurs in both directions.
All inputs are finite; a program needn't handle non-finite values.
Results may differ from the reference program's by a relative error of at most 0.0035.
Values may be sent and summed in bfloat16 or wider, within the bound.
A program may use at most 64 MiB of HBM per device.

```python
import math
import jax
import jax.numpy as jnp
from jax import lax

NLEV = 72
NZC = 58
NXC = 32
COLS_DEV = 64
RECV_MOST = 24
CAP = 2
REACH = 8
COLUMNS = 65536
ELEMS = 16384
SPAN_ROWS = 24576
N_SPAN = 32
DEVICES = 1024


def span_plan(key):
    key = jax.random.fold_in(key, 11)
    key_rate, key_coin, key_load, key_region, key_target, key_spare, key_order = jax.random.split(key, 7)
    regions = DEVICES // N_SPAN
    keep_rate = jax.random.randint(key_rate, (DEVICES, 1), 5, 9)
    coin_flip = jax.random.randint(key_coin, (DEVICES, N_SPAN), 0, 8)
    pair_load = jax.random.randint(key_load, (DEVICES, N_SPAN), 1, CAP + 1) * (coin_flip < keep_rate).astype(jnp.int32)
    chosen_region = jax.random.randint(key_region, (), 0, regions)
    chosen_target = jax.random.randint(key_target, (), 0, N_SPAN)
    owning_devices = jnp.arange(DEVICES) // N_SPAN
    targets = jnp.arange(N_SPAN)
    forced = (owning_devices == chosen_region)[:, None] & (targets == chosen_target)[None, :]
    pair_load = jnp.where(forced, CAP, pair_load)
    turned = (targets[None, :] - chosen_target) % N_SPAN
    order_hot = (turned[:, :, None] < turned[:, None, :]).astype(jnp.int32)
    sender_before = jnp.sum(pair_load[:, :, None] * order_hot, 1)
    pair_load = jnp.minimum(jnp.maximum(COLS_DEV - sender_before, 0), pair_load)
    pair_grid = pair_load.reshape(regions, N_SPAN, N_SPAN)
    receiver_before = jnp.cumsum(pair_grid, 1) - pair_grid
    pair_grid = jnp.minimum(jnp.maximum(RECV_MOST - receiver_before, 0), pair_grid)
    pair_load = pair_grid.reshape(DEVICES, N_SPAN)
    bounds = jnp.cumsum(pair_load, 1)
    positions = jnp.arange(COLS_DEV)
    ordered_dest = jnp.sum((bounds[:, None, :] <= positions[None, :, None]).astype(jnp.int32), 2)
    ordered_active = (positions[None, :] < bounds[:, -1:]).astype(jnp.int32)
    spare_dest = jax.random.randint(key_spare, (DEVICES, COLS_DEV), 0, N_SPAN)
    ordered_dest = jnp.where(ordered_active > 0, ordered_dest, spare_dest)
    scores = jax.random.randint(key_order, (DEVICES, COLS_DEV), 0, 2 ** 20) * COLS_DEV + positions[None, :]
    shuffle = jnp.argsort(scores, axis=1)
    dest = jnp.take_along_axis(ordered_dest, shuffle, 1).reshape(COLUMNS)
    flags = jnp.take_along_axis(ordered_active, shuffle, 1).reshape(COLUMNS)
    return (dest.astype(jnp.int32), flags.astype(jnp.int32))


def draw_span_map(key, part):
    return span_plan(key)[0]


def draw_active(key, part):
    return span_plan(key)[1]


def draw_nbr_elem(key, part):
    key = jax.random.fold_in(key, 7)
    key_size, key_sign, key_first, key_second = jax.random.split(key, 4)
    magnitude = jax.random.randint(key_size, (ELEMS, 4), 1, REACH + 1)
    direction = jax.random.randint(key_sign, (ELEMS, 4), 0, 2) * 2 - 1
    offset = magnitude * direction
    first_elem = jax.random.randint(key_first, (), 0, ELEMS)
    second_elem = jax.random.randint(key_second, (), 0, ELEMS)
    indices = jnp.arange(ELEMS)[:, None]
    sides = jnp.arange(4)[None, :]
    offset = jnp.where((indices == first_elem) & (sides == 0), REACH, offset)
    offset = jnp.where((indices == second_elem) & (sides == 1), -REACH, offset)
    return ((indices + offset) % ELEMS).astype(jnp.int32)


def plant(array, stream_key, low, largest):
    place = [jax.random.randint(jax.random.fold_in(stream_key, axis), (), 0, length) for axis, length in enumerate(array.shape)]
    main_axis = array.shape.index(max(array.shape))
    next_to = place[:main_axis] + [(place[main_axis] + 1) % array.shape[main_axis]] + place[main_axis + 1:]
    return array.at[tuple(place)].set(low).at[tuple(next_to)].set(largest)


def block_scale(stream_key, extent, cuts, smallest, high):
    def one(dim, shards_of):
        draws = jax.random.uniform(jax.random.fold_in(jax.random.fold_in(stream_key, 6), dim), (shards_of,), jnp.float32, smallest / len(cuts), high / len(cuts))
        return jnp.repeat(jnp.exp(draws), extent[dim] // shards_of).reshape((-1,) + (1,) * (len(extent) - dim - 1))

    loudness = one(*cuts[0])
    for cut in cuts[1:]:
        loudness = loudness * one(*cut)
    return loudness


def centred(own_key, dims, deviation, limit, cuts=(), kind=jnp.bfloat16):
    array = deviation * jax.random.normal(own_key, dims, jnp.float32)
    if cuts:
        array = array * block_scale(own_key, dims, cuts, -0.22, 0.18)
    return jnp.clip(array, -limit, limit).astype(kind)


def setup_inputs(seed: int = 0) -> dict:
    keys = jax.random.split(jax.random.key(seed), 8)
    column_state = centred(keys[0], (COLUMNS, 4 * NLEV), 1.0, 5.0, ((0, 1024),))
    crm_fields = centred(keys[1], (COLUMNS, 3 * NZC * NXC), 1.0, 5.0, ((0, 1024),))
    span_map = draw_span_map(jax.random.fold_in(keys[7], 71), 0)
    active = draw_active(jax.random.fold_in(keys[7], 71), 0)
    density = jnp.clip(jnp.exp(jax.random.uniform(keys[4], (NZC,), jnp.float32, math.log(0.3), math.log(1.0))), 0.3, 1.0)
    nbr_elem = draw_nbr_elem(jax.random.fold_in(keys[7], 71), 0)
    nbr_side = plant(jax.random.randint(keys[6], (ELEMS, 4), 0, 4), jax.random.fold_in(keys[6], 1), 0, 3).astype(jnp.int32)
    return dict(column_state=column_state, crm_fields=crm_fields, span_map=span_map, active=active, density=density, nbr_elem=nbr_elem, nbr_side=nbr_side)


HIGH = lax.Precision.HIGHEST

def level_map(count_to, count_from):
    indices = jnp.arange(count_to, dtype=jnp.int32)
    numerator = (2 * indices + 1) * count_from - count_to
    denominator = 2 * count_to
    lower_index = jnp.clip(numerator // denominator, 0, count_from - 2)
    fraction = jnp.clip((numerator - lower_index * denominator).astype(jnp.float32) / denominator, 0.0, 1.0)
    targets = jnp.arange(count_from, dtype=jnp.int32)[None, :]
    return (1.0 - fraction)[:, None] * (targets == lower_index[:, None]) + fraction[:, None] * (targets == lower_index[:, None] + 1)

def make_tables(density, levels, height, crm_width):
    up_map = level_map(height, levels)
    down_map = level_map(levels, height)
    midpoint = crm_width // 2
    modes = jnp.arange(crm_width, dtype=jnp.int32)
    wavenumber = jnp.where(modes <= midpoint, modes, modes - midpoint)
    points = jnp.arange(crm_width, dtype=jnp.int32)
    phases = 2.0 * jnp.pi * (wavenumber[:, None] * points[None, :] % crm_width).astype(jnp.float32) / crm_width
    norms = jnp.where((modes == 0) | (modes == midpoint), jnp.sqrt(1.0 / crm_width), jnp.sqrt(2.0 / crm_width))
    fourier = norms[:, None] * jnp.where((modes <= midpoint)[:, None], jnp.cos(phases), jnp.sin(phases))
    eigenvalue = 2.0 - 2.0 * jnp.cos(2.0 * jnp.pi * wavenumber.astype(jnp.float32) / crm_width)
    faces = 0.5 * (density[1:] + density[:-1])
    upper_face = jnp.concatenate([faces, density[-1:]])
    lower_face = jnp.concatenate([density[:1], faces])
    empty = jnp.zeros((1,), density.dtype)
    main_diag = -eigenvalue[:, None] - ((upper_face + lower_face) / density)[None, :]
    upper_diag = jnp.broadcast_to(jnp.concatenate([faces / density[:-1], empty])[None, :], main_diag.shape)
    lower_diag = jnp.broadcast_to(jnp.concatenate([empty, faces / density[1:]])[None, :], main_diag.shape)
    return (up_map, down_map, fourier, lower_diag, main_diag, upper_diag, density)

def diff_x(field):
    return 0.5 * (jnp.roll(field, -1, 2) - jnp.roll(field, 1, 2))

def diff_z(field):
    padded = jnp.pad(field, ((0, 0), (1, 1), (0, 0)))
    return 0.5 * (padded[:, 2:] - padded[:, :-2])

def crm_step(gcm_state, fields, tables, levels, height, crm_width):
    up_map, down_map, fourier, lower_diag, main_diag, upper_diag, density = tables
    column_count = gcm_state.shape[0]
    gcm = gcm_state.astype(jnp.float32).reshape(column_count, 4, levels)
    vertical_profile = jnp.einsum('nfl,kl->nfk', gcm, up_map, precision=HIGH)
    crm_state = fields.astype(jnp.float32).reshape(column_count, 3, height, crm_width)
    wind_x, wind_z, water = (crm_state[:, 0], crm_state[:, 1], crm_state[:, 2])
    force_u = vertical_profile[:, 2] - lax.optimization_barrier(jnp.mean(wind_x, 2))
    force_q = vertical_profile[:, 1] + vertical_profile[:, 3] - lax.optimization_barrier(jnp.mean(water, 2))
    buoyant = 0.5 * (water - lax.optimization_barrier(jnp.mean(water, 2, keepdims=True)))
    wind_x1 = wind_x - 0.25 * (wind_x * diff_x(wind_x) + wind_z * diff_z(wind_x)) + 0.25 * force_u[:, :, None]
    wind_z1 = wind_z - 0.25 * (wind_x * diff_x(wind_z) + wind_z * diff_z(wind_z)) + 0.25 * buoyant
    water1 = water - 0.25 * (wind_x * diff_x(water) + wind_z * diff_z(water)) + 0.25 * force_q[:, :, None]
    rho_cells = density[None, :, None]
    divergence = diff_x(wind_x1) + diff_z(rho_cells * wind_z1) / rho_cells
    spectrum = jnp.einsum('nzx,mx->mzn', divergence, fourier, precision=HIGH)
    solved = lax.linalg.tridiagonal_solve(lower_diag, main_diag, upper_diag, spectrum)
    pressure = jnp.einsum('mzn,mx->nzx', solved, fourier, precision=HIGH)
    wind_x2 = wind_x1 - diff_x(pressure)
    wind_z2 = wind_z1 - diff_z(pressure)
    condensate = jax.nn.softplus(water1 - jnp.exp(0.3 * vertical_profile[:, 0])[:, :, None])
    water2 = water1 - 0.5 * condensate
    cond_mean = lax.optimization_barrier(jnp.mean(condensate, 2))
    crm_tend = jnp.stack([2.0 * cond_mean, (lax.optimization_barrier(jnp.mean(water2, 2)) - lax.optimization_barrier(jnp.mean(water, 2))) / 0.25, (lax.optimization_barrier(jnp.mean(wind_x2, 2)) - lax.optimization_barrier(jnp.mean(wind_x, 2))) / 0.25, 0.5 * cond_mean], 1)
    tendency = jnp.einsum('nfk,lk->nfl', crm_tend, down_map, precision=HIGH)
    tendency = tendency.reshape(column_count, 4 * levels).astype(jnp.bfloat16)
    fresh = jnp.stack([wind_x2, wind_z2, water2], 1).reshape(column_count, 3 * height * crm_width).astype(jnp.bfloat16)
    precip = 2.0 * lax.optimization_barrier(jnp.mean(density[None, :] * cond_mean, 1))
    return (tendency, fresh, precip)

def edge_means(by_element):
    return 0.5 * jnp.stack([by_element[:, 0] + by_element[:, 1], by_element[:, 1] + by_element[:, 3], by_element[:, 2] + by_element[:, 3], by_element[:, 0] + by_element[:, 2]], 1)

def reference(column_state, crm_fields, span_map, active, density, nbr_elem, nbr_side):
    tables = make_tables(density, NLEV, NZC, NXC)
    running = active > 0

    def one_device(column_block):
        gcm_state, fields, run_flags = column_block
        tendency, fresh, precip = crm_step(gcm_state, fields, tables, NLEV, NZC, NXC)
        tendency = jnp.where(run_flags[:, None], tendency, jnp.zeros_like(tendency))
        fresh = jnp.where(run_flags[:, None], fresh, fields)
        return (tendency, fresh, precip)
    blocks = (column_state.reshape(DEVICES, COLS_DEV, 4 * NLEV), crm_fields.reshape(DEVICES, COLS_DEV, 3 * NZC * NXC), running.reshape(DEVICES, COLS_DEV))
    tendency, fresh, precip = lax.map(one_device, blocks)
    tendency = tendency.reshape(COLUMNS, 4 * NLEV)
    fresh = fresh.reshape(COLUMNS, 3 * NZC * NXC)
    precip = precip.reshape(COLUMNS)
    dest_hot = ((span_map[:, None] == jnp.arange(N_SPAN, dtype=jnp.int32)[None, :]) & running[:, None]).astype(jnp.int32)
    dest_hot = dest_hot.reshape(DEVICES, COLS_DEV, N_SPAN)
    ranking = lax.optimization_barrier(jnp.sum((jnp.cumsum(dest_hot, 1).astype(jnp.int32) - dest_hot) * dest_hot, 2)).astype(jnp.int32).reshape(COLUMNS)
    pair_counts = lax.optimization_barrier(jnp.sum(dest_hot, 1)).astype(jnp.int32).reshape(DEVICES // N_SPAN, N_SPAN, N_SPAN)
    earlier_counts = (jnp.cumsum(pair_counts, 1).astype(jnp.int32) - pair_counts).astype(jnp.int32)
    owner = jnp.arange(COLUMNS, dtype=jnp.int32) // COLS_DEV
    region_index = owner // N_SPAN
    source = owner % N_SPAN
    position = earlier_counts[region_index, source, span_map] + ranking
    table_row = jnp.where(running, (region_index * N_SPAN + span_map) * RECV_MOST + position, SPAN_ROWS)
    span_precip = jnp.zeros((SPAN_ROWS,), jnp.float32).at[table_row].set(precip, mode='drop')
    by_element = tendency.astype(jnp.float32).reshape(ELEMS, 4, 4 * NLEV)
    edge_value = edge_means(by_element)
    neighbour = edge_value[nbr_elem, nbr_side]
    edge_sums = edge_value + neighbour
    return (tendency, fresh, span_precip, edge_sums)
```

```python
import functools

import jax
import jax.numpy as jnp
import ml_dtypes
import numpy as np
from jax import lax
from jax.experimental import pallas as pl
from jax.experimental.pallas import tpu as pltpu
from jax.sharding import PartitionSpec as P

HIGH = lax.Precision.HIGHEST
LEV, NZ, NX, COLS = 72, 58, 32, 64
G, R, LANES = 4, 16, 128
ROWS = NZ * R
PAD = (NZ + 2) * R
F32, BF16 = jnp.float32, jnp.bfloat16


def split(a):
    high = a.astype(ml_dtypes.bfloat16)
    return high, (a - high.astype(np.float64)).astype(ml_dtypes.bfloat16)


def level_map(count_to, count_from):
    index = np.arange(count_to)
    numerator = (2 * index + 1) * count_from - count_to
    lower = np.clip(numerator // (2 * count_to), 0, count_from - 2)
    fraction = np.clip((numerator - lower * 2 * count_to) / (2 * count_to), 0.0, 1.0)
    target = np.arange(count_from)[None, :]
    return (1 - fraction)[:, None] * (target == lower[:, None]) + fraction[:, None] * (
        target == lower[:, None] + 1
    )


@functools.cache
def tables():
    eye = np.eye(G)
    step = 0.5 * (np.roll(np.eye(NX), 1, 0) - np.roll(np.eye(NX), -1, 0))
    dxm = np.concatenate(
        [np.kron(eye, 0.25 * step), np.kron(eye, np.full((NX, NX), 0.25 / NX))], 1
    ).astype(ml_dtypes.bfloat16)
    mode = np.arange(NX)
    wave = np.where(mode <= NX // 2, mode, mode - NX // 2)
    phase = 2 * np.pi * (wave[:, None] * np.arange(NX)[None, :] % NX) / NX
    norm = np.where((mode == 0) | (mode == NX // 2), np.sqrt(1 / NX), np.sqrt(2 / NX))
    four = norm[:, None] * np.where((mode <= NX // 2)[:, None], np.cos(phase), np.sin(phase))
    eigen = np.tile(2 - 2 * np.cos(2 * np.pi * wave / NX), G)[None, :]
    eigen = np.broadcast_to(eigen, (R, LANES)).astype(np.float32)

    def doubled(a):
        return np.concatenate(split(a), 1)

    to_mode = -four.T
    forward = np.concatenate(
        [doubled(np.kron(eye, a)) for a in (step @ to_mode, step @ to_mode, to_mode, to_mode)], 0
    )
    back = np.concatenate([np.kron(eye, 0.5 * four), np.kron(eye, four @ step)], 1)
    back = np.concatenate([doubled(back)] * 2, 0)
    up = level_map(NZ, LEV)
    zero = np.zeros_like(up)
    blocks = [
        [0.3 * up, zero, zero, zero],
        [zero, 0.25 * up, zero, 0.25 * up],
        [zero, zero, 0.25 * up, zero],
    ]
    rise = np.zeros((192, 4 * LEV))
    for i, row in enumerate(blocks):
        rise[64 * i : 64 * i + NZ] = np.concatenate(row, 1)
    rise = np.stack(split(rise))
    column, lane = np.arange(LANES) % COLS, np.arange(LANES)
    spread = (column[:, None] // R == lane[None, :] // NX).astype(ml_dtypes.bfloat16)
    gather = (lane[:, None] // NX == column[None, :] // R) / NX
    gather = np.concatenate([gather, gather], 0).astype(ml_dtypes.bfloat16)
    tally = np.zeros((64, ROWS))
    for z in range(NZ):
        tally[z, R * z : R * z + R] = 1
    tally = tally.astype(ml_dtypes.bfloat16)
    down = level_map(LEV, NZ)
    fall = np.zeros((4 * LEV, 192))
    for f, (source, gain) in enumerate(((0, 2.0), (1, 4.0), (2, 4.0), (0, 0.5))):
        fall[LEV * f : LEV * f + LEV, 64 * source : 64 * source + NZ] = gain * down
    fall = fall.astype(np.float32)
    return dxm, forward, back, eigen, rise, spread, gather, tally, fall


def dot(a, b, dims=((1,), (0,)), precision=None):
    return lax.dot_general(a, b, (dims, ((), ())), precision=precision, preferred_element_type=F32)


def halves(a):
    high = a.astype(BF16)
    return high, (a - high.astype(F32)).astype(BF16)


def regroup(parts):
    lane = lax.broadcasted_iota(jnp.int32, (R, LANES), 1)
    low, even = lane < 64, (lane & 32) == 0
    a, b, c, d = parts
    a, c = jnp.where(low, a, pltpu.roll(c, 64, 1)), jnp.where(low, pltpu.roll(a, 64, 1), c)
    b, d = jnp.where(low, b, pltpu.roll(d, 64, 1)), jnp.where(low, pltpu.roll(b, 64, 1), d)
    a, b = jnp.where(even, a, pltpu.roll(b, 32, 1)), jnp.where(even, pltpu.roll(a, 96, 1), b)
    c, d = jnp.where(even, c, pltpu.roll(d, 32, 1)), jnp.where(even, pltpu.roll(c, 96, 1), d)
    return a, b, c, d


def at(z):
    return pl.ds(pl.multiple_of(z * R, R), R)


def crm_kernel(
    state_ref, fields_ref, active_ref, density_ref, density_row_ref,
    dxm_ref, forward_ref, back_ref, eigen_ref, rise_ref, spread_ref, gather_ref, tally_ref, fall_ref,
    tend_ref, fresh_ref, precip_ref,
    raw, dxm, prof, prof_wide, prof_rows, inv, coupling, u1, w1, left, sol, sol_low, pres, means, fresh,
):
    lane = lax.broadcasted_iota(jnp.int32, (R, LANES), 1)
    row = lax.broadcasted_iota(jnp.int32, (R, LANES), 0)
    own = (lane & (R - 1)) == row

    zero16 = jnp.zeros((R, LANES), BF16)
    for f in range(3):
        raw[f, :R] = zero16
        raw[f, R * (NZ + 1) :] = zero16
    for j in range(44):
        if j < 43:
            parts = [fields_ref[R * g : R * g + R, LANES * j : LANES * j + LANES] for g in range(G)]
        else:
            parts = [
                jnp.concatenate(
                    [fields_ref[R * g : R * g + R, LANES * j :], jnp.zeros((R, 64), BF16)], 1
                )
                for g in range(G)
            ]
        for part, level in zip(regroup(parts), range(4 * j, min(4 * j + 4, 3 * NZ))):
            f, z = divmod(level, NZ)
            raw[f, R * (z + 1) : R * (z + 2)] = part
    for f in range(3):
        dxm[f] = dot(raw[f, R : R + ROWS], dxm_ref[...])

    state = state_ref[...]
    profile = dot(rise_ref[0], state, ((1,), (1,))) + dot(rise_ref[1], state, ((1,), (1,)))
    prof[:64] = jnp.exp(profile[:64])
    prof[64:] = profile[64:]
    flags = active_ref[...].reshape(1, COLS).astype(F32)
    prof[63:64] = flags
    p_high, p_low = halves(prof[...])
    prof_wide[...] = jnp.concatenate([p_high, p_low], 1).astype(F32)

    @pl.loop(0, 192, unroll=4)
    def _(i):
        line = jnp.broadcast_to(prof_wide[pl.ds(i, 1)], (R, LANES))
        prof_rows[at(i)] = jnp.where(own, line, 0.0).astype(BF16)

    for f in range(3):
        block = dot(prof_rows[64 * R * f : 64 * R * (f + 1)], spread_ref[...])
        means[f] = block
    mask = means[0, 63 * R :] > 0.5

    eigen = eigen_ref[...]

    def factor(z, last):
        rho = density_ref[z]
        above = jnp.where(z < NZ - 1, density_ref[jnp.minimum(z + 1, NZ - 1)], rho)
        below = jnp.where(z > 0, density_ref[jnp.maximum(z - 1, 0)], rho)
        f_up, f_down = 0.5 * (rho + above), 0.5 * (rho + below)
        before = jnp.where(z > 0, f_down, 0.0)
        i = 1.0 / ((eigen * rho + (f_up + f_down)) - before * last)
        e = jnp.where(z < NZ - 1, f_up, 0.0) * i
        inv[at(z)] = i
        coupling[at(z + 1)] = e
        return e

    coupling[:R] = jnp.zeros((R, LANES), F32)
    lax.fori_loop(0, NZ, factor, coupling[:R])

    def load(f, z):
        return raw[f, at(z)].astype(F32)

    zero = coupling[:R]

    def advect(z, carry):
        (u_m, u), (w_m, w), (q_m, q), (rw_mm, rw_m) = carry
        here = at(z)
        u_p, w_p, q_p = load(0, z + 2), load(1, z + 2), load(2, z + 2)
        rho = density_ref[z]
        half = 0.125 * w
        mean_u, mean_q = dxm[0, here, LANES:], dxm[2, here, LANES:]
        new_u = u - u * dxm[0, here, :LANES] - half * (u_p - u_m) + (means[2, here] - mean_u)
        new_w = w - u * dxm[1, here, :LANES] - half * (w_p - w_m) + (0.125 * q - 0.5 * mean_q)
        new_q = q - u * dxm[2, here, :LANES] - half * (q_p - q_m) + (means[1, here] - mean_q)
        x = new_q - means[0, here]
        cond = jnp.maximum(x, 0.0) + jnp.log(1.0 + jnp.exp(-jnp.abs(x)))
        q2 = new_q - 0.5 * cond
        u1[here] = new_u
        w1[at(z + 1)] = new_w
        fresh[at(2 * NZ + z)] = jnp.where(mask, q2, q).astype(BF16)
        high, low = halves(cond)
        sol_low[0, here, :LANES], sol_low[0, here, LANES:] = high, low
        high, low = halves(q2 - q)
        sol_low[1, here, :LANES], sol_low[1, here, LANES:] = high, low
        high, low = halves(rho * new_u)
        left[at(z + 1), :LANES], left[at(z + 1), LANES : 2 * LANES] = high, low
        rw = rho * new_w
        high, low = halves(0.5 * (rw - rw_mm))
        left[at(z), 2 * LANES : 3 * LANES], left[at(z), 3 * LANES :] = high, low
        return (u, u_p), (w, w_p), (q, q_p), (rw_m, rw)

    first = tuple((zero, load(f, 1)) for f in range(3)) + ((zero, zero),)
    *_, (rw_m, _) = lax.fori_loop(0, NZ, advect, first)
    high, low = halves(-0.5 * rw_m)
    left[at(NZ), 2 * LANES : 3 * LANES], left[at(NZ), 3 * LANES :] = high, low

    right = dot(left[R:], forward_ref[...])
    sol[...] = right[:, :LANES] + right[:, LANES:]

    def sweep_up(z, last):
        last = sol[at(z)] + coupling[at(z)] * last
        sol[at(z)] = last
        return last

    lax.fori_loop(0, NZ, sweep_up, zero, unroll=2)

    def sweep_down(i, last):
        z = NZ - 1 - i
        last = inv[at(z)] * sol[at(z)] + coupling[at(z + 1)] * last
        high, low = halves(last)
        left[at(z), :LANES], left[at(z), LANES : 2 * LANES] = high, low
        return last

    lax.fori_loop(0, NZ, sweep_down, zero, unroll=2)
    both = dot(left[:ROWS, : 2 * LANES], back_ref[...])
    pres[:R] = zero
    pres[R * (NZ + 1) :] = zero
    pres[R : R + ROWS] = both[:, :LANES] + both[:, 2 * LANES : 3 * LANES]
    sol[...] = both[:, LANES : 2 * LANES] + both[:, 3 * LANES :]

    @pl.loop(0, NZ)
    def _(z):
        here = at(z)
        u, w = load(0, z + 1), load(1, z + 1)
        u2 = u1[here] - sol[here]
        w2 = w1[at(z + 1)] - (pres[at(z + 2)] - pres[here])
        fresh[here] = jnp.where(mask, u2, u).astype(BF16)
        fresh[at(NZ + z)] = jnp.where(mask, w2, w).astype(BF16)
        high, low = halves(u2 - u)
        sol_low[2, here, :LANES], sol_low[2, here, LANES:] = high, low

    lane_high = lane < COLS
    sums = []
    for f in range(3):
        means[f, :ROWS] = dot(sol_low[f], gather_ref[...])

        @pl.loop(0, NZ)
        def _(z):
            value = jnp.where(own, means[f, at(z)], 0.0)
            high = value.astype(BF16)
            low = (value - high.astype(F32)).astype(BF16)
            left[at(z), :LANES] = jnp.where(lane_high, high, low)

        total = dot(tally_ref[...], left[:ROWS, :LANES])
        sums.append(total[:, :COLS] + total[:, COLS:])
    tend = dot(fall_ref[...], jnp.concatenate(sums, 0), precision=HIGH)
    tend = jnp.where(flags > 0.5, tend, 0.0)
    tend_ref[...] = tend.T.astype(BF16)
    weights = density_row_ref[...] * (2.0 / NZ)
    precip_ref[...] = dot(weights, sums[0][:NZ], precision=HIGH)

    for j in range(44):
        parts = [
            fresh[R * level : R * level + R] if level < 3 * NZ else zero16
            for level in range(4 * j, 4 * j + 4)
        ]
        for g, part in enumerate(regroup(parts)):
            if j < 43:
                fresh_ref[R * g : R * g + R, LANES * j : LANES * j + LANES] = part
            else:
                fresh_ref[R * g : R * g + R, LANES * j :] = part[:, :64]


def crm_call(column_state, crm_fields, active, density):
    constants = [jnp.asarray(a) for a in tables()]
    vmem = pl.BlockSpec(memory_space=pltpu.VMEM)
    smem = pl.BlockSpec(memory_space=pltpu.SMEM)
    return pl.pallas_call(
        crm_kernel,
        out_shape=(
            jax.ShapeDtypeStruct((COLS, 4 * LEV), BF16),
            jax.ShapeDtypeStruct((COLS, 3 * NZ * NX), BF16),
            jax.ShapeDtypeStruct((1, COLS), F32),
        ),
        in_specs=[vmem, vmem, vmem, smem, vmem] + [vmem] * len(constants),
        out_specs=(vmem, vmem, vmem),
        scratch_shapes=[
            pltpu.VMEM((3, PAD, LANES), BF16),
            pltpu.VMEM((3, ROWS, 2 * LANES), F32),
            pltpu.VMEM((192, COLS), F32),
            pltpu.VMEM((192, LANES), F32),
            pltpu.VMEM((192 * R, LANES), BF16),
            pltpu.VMEM((ROWS, LANES), F32),
            pltpu.VMEM((PAD, LANES), F32),
            pltpu.VMEM((ROWS, LANES), F32),
            pltpu.VMEM((PAD, LANES), F32),
            pltpu.VMEM((ROWS + R, 4 * LANES), BF16),
            pltpu.VMEM((ROWS, LANES), F32),
            pltpu.VMEM((3, ROWS, 2 * LANES), BF16),
            pltpu.VMEM((PAD, LANES), F32),
            pltpu.VMEM((3, 64 * R, LANES), F32),
            pltpu.VMEM((3 * ROWS, LANES), BF16),
        ],
        compiler_params=pltpu.CompilerParams(vmem_limit_bytes=48 * 2**20),
    )(column_state, crm_fields, active, density, density.reshape(1, NZ), *constants)


def edge_part(tendency, nbr_elem, nbr_side):
    axes = ("region", "span")
    count = lax.axis_size(axes)
    up = [(i, (i + 1) % count) for i in range(count)]
    down = [((i + 1) % count, i) for i in range(count)]
    half = COLS // 2
    table = jnp.concatenate(
        [
            lax.ppermute(tendency[half:], axes, up),
            tendency,
            lax.ppermute(tendency[:half], axes, down),
        ],
        0,
    )
    elems = COLS // 4
    first = lax.axis_index(axes) * elems
    near = (nbr_elem - first + elems // 2 + elems * count) % (elems * count)
    sides = jnp.arange(4, dtype=jnp.int32)
    corner = jnp.array([[1, 1, 0, 0], [0, 1, 0, 1], [0, 0, 1, 1], [1, 0, 1, 0]], F32)
    place = jnp.arange(2 * elems, dtype=jnp.int32)
    side_hot = (nbr_side[:, :, None] == sides).astype(F32) @ corner
    theirs = (near[:, :, None] == place).astype(F32)[..., None] * side_hot[:, :, None, :]
    home = (jnp.arange(elems, dtype=jnp.int32)[:, None] + elems // 2 == place).astype(F32)
    ours = home[:, None, :, None] * corner[None, :, None, :]
    pick = (0.5 * (theirs + ours)).astype(BF16).reshape(COLS, 2 * COLS)
    return dot(pick, table).reshape(elems, 4, 4 * LEV)


def precip_part(precip, span_map, active):
    spans, rows = 32, 24
    hot = ((span_map[:, None] == jnp.arange(spans, dtype=jnp.int32)) & (active[:, None] > 0)).astype(F32)
    earlier = jnp.cumsum(hot, 0) - hot
    cast = precip[:, None]
    first = jnp.sum(jnp.where(earlier == 0, hot, 0) * cast, 0)
    second = jnp.sum(jnp.where(earlier == 1, hot, 0) * cast, 0)
    sent = jnp.stack([first, second, jnp.sum(hot, 0)], 1)
    got = lax.all_to_all(sent, "span", split_axis=0, concat_axis=0, tiled=True)
    load = got[:, 2]
    start = (jnp.cumsum(load) - load)[:, None]
    place = jnp.arange(rows, dtype=F32)[None, :]
    one = jnp.where((start == place) & (load[:, None] > 0.5), got[:, 0:1], 0.0)
    two = jnp.where((start + 1 == place) & (load[:, None] > 1.5), got[:, 1:2], 0.0)
    return jnp.sum(one + two, 0)


def body(column_state, crm_fields, span_map, active, density, nbr_elem, nbr_side):
    tendency, fresh, precip = crm_call(column_state, crm_fields, active, density)
    edge_sums = edge_part(tendency, nbr_elem, nbr_side)
    span_precip = precip_part(precip[0], span_map, active)
    return (tendency, fresh, span_precip, edge_sums)


def solution(mesh):
    rows = P(("region", "span"), None)
    line = P(("region", "span"))
    return jax.shard_map(
        body,
        mesh=mesh,
        in_specs=(rows, rows, line, line, P(), rows, rows),
        out_specs=(rows, rows, line, P(("region", "span"), None, None)),
        check_vma=False,
    )
```

```python
import functools

import jax
import jax.numpy as jnp
import ml_dtypes
import numpy as np
from jax import lax
from jax.experimental import pallas as pl
from jax.experimental.pallas import tpu as pltpu
from jax.sharding import PartitionSpec as P

HIGH = lax.Precision.HIGHEST
MESH = pl.DeviceIdType.MESH
LEV, NZ, NX, COLS = 72, 58, 32, 64
G, R, LANES = 4, 16, 128
ROWS = NZ * R
WIDE, CHUNKS = 512, 11
F32, BF16 = jnp.float32, jnp.bfloat16


def split(a):
    high = a.astype(ml_dtypes.bfloat16)
    return high, (a - high.astype(np.float64)).astype(ml_dtypes.bfloat16)


def level_map(count_to, count_from):
    index = np.arange(count_to)
    numerator = (2 * index + 1) * count_from - count_to
    lower = np.clip(numerator // (2 * count_to), 0, count_from - 2)
    fraction = np.clip((numerator - lower * 2 * count_to) / (2 * count_to), 0.0, 1.0)
    target = np.arange(count_from)[None, :]
    return (1 - fraction)[:, None] * (target == lower[:, None]) + fraction[:, None] * (
        target == lower[:, None] + 1
    )


@functools.cache
def tables():
    eye = np.eye(G)
    step = 0.5 * (np.roll(np.eye(NX), 1, 0) - np.roll(np.eye(NX), -1, 0))
    dxm = np.concatenate(
        [np.kron(eye, 0.25 * step), np.kron(eye, np.full((NX, NX), 0.25 / NX))], 1
    ).astype(ml_dtypes.bfloat16)
    mode = np.arange(NX)
    wave = np.where(mode <= NX // 2, mode, mode - NX // 2)
    phase = 2 * np.pi * (wave[:, None] * np.arange(NX)[None, :] % NX) / NX
    norm = np.where((mode == 0) | (mode == NX // 2), np.sqrt(1 / NX), np.sqrt(2 / NX))
    four = norm[:, None] * np.where((mode <= NX // 2)[:, None], np.cos(phase), np.sin(phase))
    eigen = np.tile(2 - 2 * np.cos(2 * np.pi * wave / NX), G)[None, :]
    eigen = np.broadcast_to(eigen, (R, LANES)).astype(np.float32)

    def doubled(a):
        return np.concatenate(split(a), 1)

    to_mode = -four.T
    forward = np.concatenate(
        [doubled(np.kron(eye, a)) for a in (step @ to_mode, step @ to_mode, to_mode, to_mode)], 0
    )
    back = np.concatenate([np.kron(eye, 0.5 * four), np.kron(eye, four @ step)], 1)
    back = np.concatenate([doubled(back)] * 2, 0)
    up = level_map(NZ, LEV)
    zero = np.zeros_like(up)
    blocks = [
        [0.3 * up, zero, zero, zero],
        [zero, 0.25 * up, zero, 0.25 * up],
        [zero, zero, 0.25 * up, zero],
    ]
    rise = np.zeros((192, 4 * LEV))
    for i, row in enumerate(blocks):
        rise[64 * i : 64 * i + NZ] = np.concatenate(row, 1)
    rise = np.stack(split(rise))
    column, lane = np.arange(LANES) % COLS, np.arange(LANES)
    spread = (column[:, None] // R == lane[None, :] // NX).astype(ml_dtypes.bfloat16)
    gather = (lane[:, None] // NX == column[None, :] // R) / NX
    gather = np.concatenate([gather, gather], 0).astype(ml_dtypes.bfloat16)
    tally = np.zeros((64, ROWS))
    for z in range(NZ):
        tally[z, R * z : R * z + R] = 1
    tally = tally.astype(ml_dtypes.bfloat16)
    down = level_map(LEV, NZ)
    fall = np.zeros((4 * LEV, 192))
    for f, (source, gain) in enumerate(((0, 2.0), (1, 4.0), (2, 4.0), (0, 0.5))):
        fall[LEV * f : LEV * f + LEV, 64 * source : 64 * source + NZ] = gain * down
    fall = np.stack(split(fall.T))
    return dxm, forward, back, eigen, rise, spread, gather, tally, fall


def dot(a, b, dims=((1,), (0,)), precision=None):
    return lax.dot_general(a, b, (dims, ((), ())), precision=precision, preferred_element_type=F32)


def halves(a):
    high = a.astype(BF16)
    return high, (a - high.astype(F32)).astype(BF16)


def regroup(parts):
    lane = lax.broadcasted_iota(jnp.int32, (R, LANES), 1)
    low, even = lane < 64, (lane & 32) == 0
    a, b, c, d = parts
    a, c = jnp.where(low, a, pltpu.roll(c, 64, 1)), jnp.where(low, pltpu.roll(a, 64, 1), c)
    b, d = jnp.where(low, b, pltpu.roll(d, 64, 1)), jnp.where(low, pltpu.roll(b, 64, 1), d)
    a, b = jnp.where(even, a, pltpu.roll(b, 32, 1)), jnp.where(even, pltpu.roll(a, 96, 1), b)
    c, d = jnp.where(even, c, pltpu.roll(d, 32, 1)), jnp.where(even, pltpu.roll(c, 96, 1), d)
    return a, b, c, d


def crm_kernel(
    state_hbm, fields_hbm, active_hbm, density_hbm,
    dxm_hbm, forward_hbm, back_hbm, eigen_hbm, rise_hbm, spread_hbm, gather_hbm, tally_hbm, fall_hbm,
    tend_hbm, fresh_hbm, precip_hbm,
    state_ref, fields_ref, active_ref, density_ref, density_row_ref,
    dxm_ref, forward_ref, back_ref, eigen_ref, rise_ref, spread_ref, gather_ref, tally_ref, fall_ref,
    tend_ref, fresh_ref, precip_ref,
    raw, dxm, prof_wide, prof_rows, inv, coup, u1, w1, left, sol, cells, pres, means, fresh,
    in_sem, field_sem, out_sem, fresh_sem,
):
    copies = {}
    pairs = dict(
        state=(state_hbm, state_ref), rise=(rise_hbm, rise_ref), active=(active_hbm, active_ref),
        spread=(spread_hbm, spread_ref), dxm=(dxm_hbm, dxm_ref), density=(density_hbm, density_ref),
        eigen=(eigen_hbm, eigen_ref), forward=(forward_hbm, forward_ref), back=(back_hbm, back_ref),
        gather=(gather_hbm, gather_ref), tally=(tally_hbm, tally_ref), fall=(fall_hbm, fall_ref),
        density_row=(density_hbm, density_row_ref),
    )
    for n, (name, (source, target)) in enumerate(pairs.items()):
        copies[name] = pltpu.make_async_copy(source, target, in_sem.at[n])
        if n == 6:
            for k in range(CHUNKS):
                cut = slice(WIDE * k, min(WIDE * k + WIDE, NZ * NX * 3))
                copies[k] = pltpu.make_async_copy(
                    fields_hbm.at[:, cut], fields_ref.at[:, cut], field_sem.at[k]
                )
                copies[k].start()
        copies[name].start()

    lane = lax.broadcasted_iota(jnp.int32, (R, LANES), 1)
    row = lax.broadcasted_iota(jnp.int32, (R, LANES), 0)
    own = (lane & (R - 1)) == row
    zero16 = jnp.zeros((R, LANES), BF16)

    copies["state"].wait()
    copies["rise"].wait()
    copies["active"].wait()
    state = state_ref[...]
    profile = dot(rise_ref[0], state, ((1,), (1,))) + dot(rise_ref[1], state, ((1,), (1,)))
    flags = active_ref[...].reshape(1, COLS).astype(F32)
    p_high, p_low = halves(jnp.concatenate([jnp.exp(profile[:64]), profile[64:]], 0))
    prof_wide[...] = jnp.concatenate([p_high, p_low], 1).astype(F32)
    keep = jnp.concatenate([flags, flags], 1)
    prof_wide[63:64] = jnp.where(lane[:1] < COLS, keep, 0.0)
    wanted = [64 * f + z for f in range(3) for z in range(NZ)] + [63]
    for k in range(0, len(wanted), 8):
        lines = [prof_wide[i : i + 1] for i in wanted[k : k + 8]]
        lines = [jnp.where(own, jnp.broadcast_to(v, (R, LANES)), 0.0).astype(BF16) for v in lines]
        for i, v in zip(wanted[k : k + 8], lines):
            prof_rows[i] = v
    copies["spread"].wait()
    for f in range(3):
        top = 64 if f == 0 else NZ
        block = dot(prof_rows[64 * f : 64 * f + top].reshape(top * R, LANES), spread_ref[...])
        means[f, :top] = block.reshape(top, R, LANES)
    mask = means[0, 63] > 0.5

    for f in range(3):
        raw[f, 0] = zero16
        raw[f, NZ + 1] = zero16
    for k in range(CHUNKS):
        copies[k].wait()
        blocks = []
        for j in range(4 * k, 4 * k + 4):
            if j < 43:
                tiles = [fields_ref[R * g : R * g + R, LANES * j : LANES * j + LANES] for g in range(G)]
            else:
                tiles = [
                    jnp.concatenate([fields_ref[R * g : R * g + R, LANES * j :], zero16[:, :64]], 1)
                    for g in range(G)
                ]
            blocks.append(regroup(tiles))
        for j, block in enumerate(blocks):
            for part, level in zip(block, range(16 * k + 4 * j, min(16 * k + 4 * j + 4, 3 * NZ))):
                f, z = divmod(level, NZ)
                raw[f, z + 1] = part
    copies["dxm"].wait()
    for f in range(3):
        block = dot(raw[f, 1 : NZ + 1].reshape(ROWS, LANES), dxm_ref[...])
        dxm[f] = block.reshape(NZ, R, 2 * LANES)

    copies["density"].wait()
    copies["eigen"].wait()
    eigen = eigen_ref[...]
    inv[0] = jnp.zeros((R, LANES), F32)
    zero = inv[0]

    def factor(t, last):
        low, high, _ = last
        z = NZ - 1 - t
        rho, above = density_ref[t], density_ref[t + 1]
        below = jnp.where(t > 0, density_ref[jnp.maximum(t - 1, 0)], rho)
        f_up, f_down = 0.5 * (rho + above), 0.5 * (rho + below)
        i_low = 1.0 / ((eigen * rho + (f_up + f_down)) - f_down * low)
        e_low = f_up * i_low
        rho, below = density_ref[z], density_ref[z - 1]
        above = jnp.where(t > 0, density_ref[jnp.minimum(z + 1, NZ - 1)], rho)
        f_up, f_down = 0.5 * (rho + above), 0.5 * (rho + below)
        diag = (eigen * rho + (f_up + f_down)) - f_up * high
        i_high = 1.0 / diag
        e_high = f_down * i_high
        stores = [(inv, t, i_low), (coup, t, e_low), (inv, z, i_high), (coup, z, e_high)]
        return stores, (e_low, e_high, diag)

    def advect(z, carry):
        (u_m, u), (w_m, w), (q_m, q), (rw_mm, rw_m) = carry
        u_p, w_p, q_p = [raw[f, z + 2].astype(F32) for f in range(3)]
        rho = density_ref[z]
        half = 0.125 * w
        du, mean_u = dxm[0, z, :, :LANES], dxm[0, z, :, LANES:]
        dw = dxm[1, z, :, :LANES]
        dq, mean_q = dxm[2, z, :, :LANES], dxm[2, z, :, LANES:]
        new_u = u - u * du - half * (u_p - u_m) + (means[2, z] - mean_u)
        new_w = w - u * dw - half * (w_p - w_m) + (0.125 * q - 0.5 * mean_q)
        new_q = q - u * dq - half * (q_p - q_m) + (means[1, z] - mean_q)
        x = new_q - means[0, z]
        cond = jnp.maximum(x, 0.0) + jnp.log(1.0 + jnp.exp(-jnp.abs(x)))
        q2 = new_q - 0.5 * cond
        rw = rho * new_w
        stores = [
            (u1, z, new_u),
            (w1, z, new_w),
            (fresh, 2 * NZ + z, jnp.where(mask, q2, q).astype(BF16)),
            (cells.at[0], z, jnp.concatenate(halves(cond), 1)),
            (cells.at[1], z, jnp.concatenate(halves(q2 - q), 1)),
            (left.at[:, :, : 2 * LANES], z + 1, jnp.concatenate(halves(rho * new_u), 1)),
            (left.at[:, :, 2 * LANES :], z, jnp.concatenate(halves(0.5 * (rw - rw_mm)), 1)),
        ]
        return stores, ((u, u_p), (w, w_p), (q, q_p), (rw_m, rw))

    def both_passes(t, carry):
        stores, last = factor(t, carry[0])
        more, levels = advect(2 * t, carry[1])
        most, levels = advect(2 * t + 1, levels)
        for ref, z, value in stores + more + most:
            ref[z] = value
        return last, levels

    first = tuple((zero, raw[f, 1].astype(F32)) for f in range(3)) + ((zero, zero),)
    last, levels = lax.fori_loop(0, NZ // 2, both_passes, ((zero, zero, zero), first))
    left[NZ, :, 2 * LANES :] = jnp.concatenate(halves(-0.5 * levels[3][0]), 1)
    mid = NZ // 2
    centre = 1.0 / (last[2] - 0.5 * (density_ref[mid - 1] + density_ref[mid]) * last[0])

    def give_back(k):
        blocks = []
        for j in range(4 * k, 4 * k + 4):
            blocks.append(
                regroup([fresh[v] if v < 3 * NZ else zero16 for v in range(4 * j, 4 * j + 4)])
            )
        for j, block in enumerate(blocks):
            j += 4 * k
            for g, part in enumerate(block):
                if j < 43:
                    fresh_ref[R * g : R * g + R, LANES * j : LANES * j + LANES] = part
                else:
                    fresh_ref[R * g : R * g + R, LANES * j :] = part[:, :64]
        cut = slice(WIDE * k, min(WIDE * k + WIDE, NZ * NX * 3))
        copy = pltpu.make_async_copy(fresh_ref.at[:, cut], fresh_hbm.at[:, cut], fresh_sem.at[k])
        copy.start()
        return copy

    leaving = [give_back(k) for k in range(8, CHUNKS)]

    copies["forward"].wait()
    right = dot(left[1:].reshape(ROWS, 4 * LANES), forward_ref[...])
    sol[...] = (right[:, :LANES] + right[:, LANES:]).reshape(NZ, R, LANES)
    low, high = sol[0], sol[NZ - 1]
    for t in range(1, mid):
        z = NZ - 1 - t
        low = sol[t] + coup[t - 1] * low
        high = sol[z] + coup[z + 1] * high
        sol[t], sol[z] = low, high
    high = centre * (high + coup[mid - 1] * low)
    low = inv[mid - 1] * low + coup[mid - 1] * high
    left[mid - 1, :, : 2 * LANES] = jnp.concatenate(halves(low), 1)
    left[mid, :, : 2 * LANES] = jnp.concatenate(halves(high), 1)
    for t in range(mid - 2, -1, -1):
        z = NZ - 1 - t
        low = inv[t] * sol[t] + coup[t] * low
        high = inv[z] * sol[z] + coup[z] * high
        left[t, :, : 2 * LANES] = jnp.concatenate(halves(low), 1)
        left[z, :, : 2 * LANES] = jnp.concatenate(halves(high), 1)
    copies["back"].wait()
    both = dot(left[:NZ, :, : 2 * LANES].reshape(ROWS, 2 * LANES), back_ref[...])
    pres[0] = zero
    pres[NZ + 1] = zero
    pres[1 : NZ + 1] = (both[:, :LANES] + both[:, 2 * LANES : 3 * LANES]).reshape(NZ, R, LANES)
    sol[...] = (both[:, LANES : 2 * LANES] + both[:, 3 * LANES :]).reshape(NZ, R, LANES)

    @pl.loop(0, NZ // 2)
    def _(t):
        z = 2 * t
        here = pl.ds(z, 2)
        u, w = raw[0, pl.ds(z + 1, 2)].astype(F32), raw[1, pl.ds(z + 1, 2)].astype(F32)
        u2 = u1[here] - sol[here]
        w2 = w1[here] - (pres[pl.ds(z + 2, 2)] - pres[here])
        u_out = jnp.where(mask[None], u2, u).astype(BF16)
        w_out = jnp.where(mask[None], w2, w).astype(BF16)
        change = jnp.concatenate(halves(u2 - u), 2)
        fresh[here] = u_out
        fresh[pl.ds(NZ + z, 2)] = w_out
        cells[2, here] = change

    copies["gather"].wait()
    for f in range(3):
        total = dot(cells[f].reshape(ROWS, 2 * LANES), gather_ref[...])
        means[f, :NZ] = total.reshape(NZ, R, LANES)
    lane_high = lane < COLS

    @pl.loop(0, NZ // 2)
    def _(t):
        here = pl.ds(2 * t, 2)
        values = []
        for f in range(3):
            value = jnp.where(own[None], means[f, here], 0.0)
            high = value.astype(BF16).astype(F32)
            values.append(jnp.where(lane_high[None], high, value - high).astype(BF16))
        left[here, :, : 3 * LANES] = jnp.concatenate(values, 2)

    copies["tally"].wait()
    total = dot(tally_ref[...], left[:NZ, :, : 3 * LANES].reshape(ROWS, 3 * LANES))
    copies["density_row"].wait()
    weights = density_row_ref[...].reshape(1, NZ) * (2.0 / NZ)
    precip = dot(weights, total[:NZ, :LANES], precision=HIGH)
    precip_ref[...] = precip[:, :COLS] + precip[:, COLS:]
    total = jnp.concatenate([total[:, LANES * f : LANES * f + LANES] for f in range(3)], 0)
    t_high, t_low = halves(jnp.where(keep > 0.5, total, 0.0).T)
    copies["fall"].wait()
    tend = dot(t_high, fall_ref[0]) + dot(t_low, fall_ref[0]) + dot(t_high, fall_ref[1])
    tend_ref[...] = (tend[:COLS] + tend[COLS:]).astype(BF16)
    leaving.append(pltpu.make_async_copy(tend_ref, tend_hbm, out_sem.at[0]))
    leaving[-1].start()
    leaving.append(pltpu.make_async_copy(precip_ref, precip_hbm, out_sem.at[1]))
    leaving[-1].start()
    leaving += [give_back(k) for k in range(8)]
    for copy in leaving:
        copy.wait()


def crm_call(column_state, crm_fields, active, density):
    constants = [jnp.asarray(a) for a in tables()]
    hbm = pl.BlockSpec(memory_space=pltpu.HBM)
    levels = (NZ, R, LANES)
    return pl.pallas_call(
        crm_kernel,
        out_shape=(
            jax.ShapeDtypeStruct((COLS, 4 * LEV), BF16),
            jax.ShapeDtypeStruct((COLS, 3 * NZ * NX), BF16),
            jax.ShapeDtypeStruct((1, COLS), F32),
        ),
        in_specs=[hbm] * (4 + len(constants)),
        out_specs=(hbm, hbm, hbm),
        scratch_shapes=[
            pltpu.VMEM((COLS, 4 * LEV), BF16),
            pltpu.VMEM((COLS, 3 * NZ * NX), BF16),
            pltpu.VMEM((COLS,), jnp.int32),
            pltpu.SMEM((NZ,), F32),
            pltpu.VMEM((NZ,), F32),
            *[pltpu.VMEM(a.shape, a.dtype) for a in constants],
            pltpu.VMEM((COLS, 4 * LEV), BF16),
            pltpu.VMEM((COLS, 3 * NZ * NX), BF16),
            pltpu.VMEM((1, COLS), F32),
            pltpu.VMEM((3, NZ + 2, R, LANES), BF16),
            pltpu.VMEM((3, NZ, R, 2 * LANES), F32),
            pltpu.VMEM((192, LANES), F32),
            pltpu.VMEM((192, R, LANES), BF16),
            pltpu.VMEM(levels, F32),
            pltpu.VMEM(levels, F32),
            pltpu.VMEM(levels, F32),
            pltpu.VMEM(levels, F32),
            pltpu.VMEM((NZ + 1, R, 4 * LANES), BF16),
            pltpu.VMEM(levels, F32),
            pltpu.VMEM((3, NZ, R, 2 * LANES), BF16),
            pltpu.VMEM((NZ + 2, R, LANES), F32),
            pltpu.VMEM((3, 64, R, LANES), F32),
            pltpu.VMEM((3 * NZ, R, LANES), BF16),
            pltpu.SemaphoreType.DMA((13,)),
            pltpu.SemaphoreType.DMA((CHUNKS,)),
            pltpu.SemaphoreType.DMA((2,)),
            pltpu.SemaphoreType.DMA((CHUNKS,)),
        ],
        compiler_params=pltpu.CompilerParams(vmem_limit_bytes=63 * 2**20),
    )(column_state, crm_fields, active, density, *constants)


def exchange_kernel(
    shape, tend_ref, precip_ref, span_map_ref, active_ref, nbr_elem_ref, nbr_side_ref,
    edge_ref, rows_ref,
    from_left, from_right, sent, got, flat, send_sem, recv_sem, halo_send, halo_recv,
):
    regions, spans = shape
    region, span = lax.axis_index("region"), lax.axis_index("span")
    me = region * spans + span
    total = regions * spans
    right, left = lax.rem(me + 1, total), lax.rem(me + total - 1, total)
    right, left = (lax.div(right, spans), lax.rem(right, spans)), (lax.div(left, spans), lax.rem(left, spans))

    barrier = pltpu.get_barrier_semaphore()

    def greet(i, _):
        pl.semaphore_signal(
            barrier, inc=1, device_id=(region, lax.rem(span + i, spans)), device_id_type=MESH
        )
        return _

    lax.fori_loop(1, spans, greet, 0)
    for other in (left, right):
        pl.semaphore_signal(barrier, inc=1, device_id=other, device_id_type=MESH)

    target = lax.broadcasted_iota(jnp.int32, (spans, COLS), 0)
    hot = jnp.where(
        (span_map_ref[...].reshape(1, COLS) == target) & (active_ref[...].reshape(1, COLS) > 0), 1.0, 0.0
    )
    upper = lax.broadcasted_iota(jnp.int32, (COLS, COLS), 0) < lax.broadcasted_iota(jnp.int32, (COLS, COLS), 1)
    before = dot(hot.astype(BF16), jnp.where(upper, 1.0, 0.0).astype(BF16))
    precip = precip_ref[...]
    one = jnp.sum(jnp.where(before < 0.5, hot, 0.0) * precip, 1, keepdims=True)
    two = jnp.sum(jnp.where(before > 0.5, hot, 0.0) * precip, 1, keepdims=True)
    load = jnp.sum(hot, 1, keepdims=True)
    lane = lax.broadcasted_iota(jnp.int32, (spans, LANES), 1)
    block = jnp.where(lane == 0, one, jnp.where(lane == 1, two, jnp.where(lane == 2, load, 0.0)))
    for i in range(spans):
        sent[i] = block[i : i + 1]
    got[span] = sent[span]

    pl.semaphore_wait(barrier, spans + 1)
    half = COLS // 2
    halos = [
        pltpu.make_async_remote_copy(
            src_ref=tend_ref.at[part], dst_ref=place, send_sem=halo_send.at[n], recv_sem=halo_recv.at[n],
            device_id=other, device_id_type=MESH,
        )
        for n, (part, place, other) in enumerate(
            ((pl.ds(half, half), from_left, right), (pl.ds(0, half), from_right, left))
        )
    ]
    for halo in halos:
        halo.start()

    def give(i, _):
        there = lax.rem(span + i, spans)
        pltpu.make_async_remote_copy(
            src_ref=sent.at[there], dst_ref=got.at[span], send_sem=send_sem, recv_sem=recv_sem,
            device_id=(region, there), device_id_type=MESH,
        ).start()
        return _

    lax.fori_loop(1, spans, give, 0)

    cell = lax.broadcasted_iota(jnp.int32, (COLS // 4, 2 * COLS), 1)
    elem, corner = cell >> 2, cell & 3
    c_low, c_high = corner & 1, corner >> 1
    home = lax.broadcasted_iota(jnp.int32, (COLS // 4, 2 * COLS), 0) + COLS // 8
    faces = (1 - c_high, c_low, c_high, 1 - c_low)
    everyone = total * (COLS // 4)
    picks = []
    for side in range(4):
        near = nbr_elem_ref[:, side : side + 1] - (me * (COLS // 4) - COLS // 8)
        near = jnp.where(near < 0, near + everyone, near)
        near = jnp.where(near >= everyone, near - everyone, near)
        theirs = nbr_side_ref[:, side : side + 1]
        face = jnp.where(
            theirs < 2, jnp.where(theirs == 0, faces[0], faces[1]), jnp.where(theirs == 2, faces[2], faces[3])
        )
        pick = jnp.where(near == elem, face, 0) + jnp.where(home == elem, faces[side], 0)
        picks.append((0.5 * pick.astype(F32)).astype(BF16))

    for halo in halos:
        halo.wait()
    own = tend_ref[...]
    table = jnp.concatenate([from_left[...], own, from_right[...]], 0)
    for side in range(4):
        edge_ref[:, side, :] = dot(picks[side], table)

    others = pl.ds(0, spans - 1)
    pltpu.make_async_copy(got.at[others], got.at[others], recv_sem).wait()
    for i in range(spans):
        flat[i : i + 1] = got[i]
    table = flat[...]
    lower = lax.broadcasted_iota(jnp.int32, (spans, spans), 0) > lax.broadcasted_iota(jnp.int32, (spans, spans), 1)
    load = table[:, 2:3]
    start = dot(
        jnp.where(lower, 1.0, 0.0).astype(BF16), jnp.broadcast_to(load, (spans, LANES)).astype(BF16)
    )
    place = lane.astype(F32)
    rows = jnp.where((start == place) & (load > 0.5), table[:, 0:1], 0.0)
    rows += jnp.where((start + 1.0 == place) & (load > 1.5), table[:, 1:2], 0.0)
    rows_ref[...] = jnp.sum(rows, 0, keepdims=True)[:, : rows_ref.shape[1]]
    pltpu.make_async_copy(sent.at[others], sent.at[others], send_sem).wait()


def exchange_call(shape, slots, tendency, precip, span_map, active, nbr_elem, nbr_side):
    spans = shape[1]
    vmem = pl.BlockSpec(memory_space=pltpu.VMEM)
    return pl.pallas_call(
        functools.partial(exchange_kernel, shape),
        out_shape=(
            jax.ShapeDtypeStruct((COLS // 4, 4, 4 * LEV), F32),
            jax.ShapeDtypeStruct((1, slots), F32),
        ),
        in_specs=[vmem] * 6,
        out_specs=(vmem, vmem),
        scratch_shapes=[
            pltpu.VMEM((COLS // 2, 4 * LEV), BF16),
            pltpu.VMEM((COLS // 2, 4 * LEV), BF16),
            pltpu.VMEM((spans, 1, LANES), F32),
            pltpu.VMEM((spans, 1, LANES), F32),
            pltpu.VMEM((spans, LANES), F32),
            pltpu.SemaphoreType.DMA,
            pltpu.SemaphoreType.DMA,
            pltpu.SemaphoreType.DMA((2,)),
            pltpu.SemaphoreType.DMA((2,)),
        ],
        compiler_params=pltpu.CompilerParams(
            collective_id=0, has_side_effects=True, vmem_limit_bytes=16 * 2**20
        ),
    )(tendency, precip, span_map, active, nbr_elem, nbr_side)


def body(shape, column_state, crm_fields, span_map, active, density, nbr_elem, nbr_side):
    tendency, fresh, precip = crm_call(column_state, crm_fields, active, density)
    edge_sums, rows = exchange_call(
        shape, COLS * 3 // 8, tendency, precip, span_map, active, nbr_elem, nbr_side
    )
    return (tendency, fresh, rows[0], edge_sums)


def solution(mesh):
    rows = P(("region", "span"), None)
    line = P(("region", "span"))
    return jax.shard_map(
        functools.partial(body, (mesh.shape["region"], mesh.shape["span"])),
        mesh=mesh,
        in_specs=(rows, rows, line, line, P(), rows, rows),
        out_specs=(rows, rows, line, P(("region", "span"), None, None)),
        check_vma=False,
    )
```

```python
import functools

import jax
import jax.numpy as jnp
import ml_dtypes
import numpy as np
from jax import lax
from jax.experimental import pallas as pl
from jax.experimental.pallas import tpu as pltpu
from jax.sharding import PartitionSpec as P

MESH = pl.DeviceIdType.MESH
LEV, NZ, NX, COLS = 72, 58, 32, 64
G, R, LANES = 4, 16, 128
ROWS = NZ * R
WIDE, CHUNKS = 512, 11
F32, BF16 = jnp.float32, jnp.bfloat16


def split(a):
    high = a.astype(ml_dtypes.bfloat16)
    return high, (a - high.astype(np.float64)).astype(ml_dtypes.bfloat16)


def level_map(count_to, count_from):
    index = np.arange(count_to)
    numerator = (2 * index + 1) * count_from - count_to
    lower = np.clip(numerator // (2 * count_to), 0, count_from - 2)
    fraction = np.clip((numerator - lower * 2 * count_to) / (2 * count_to), 0.0, 1.0)
    target = np.arange(count_from)[None, :]
    return (1 - fraction)[:, None] * (target == lower[:, None]) + fraction[:, None] * (
        target == lower[:, None] + 1
    )


@functools.cache
def tables():
    eye = np.eye(G)
    step = 0.5 * (np.roll(np.eye(NX), 1, 0) - np.roll(np.eye(NX), -1, 0))
    dxm = np.concatenate(
        [np.kron(eye, 0.25 * step), np.kron(eye, np.full((NX, NX), 0.25 / NX))], 1
    ).astype(ml_dtypes.bfloat16)
    mode = np.arange(NX)
    wave = np.where(mode <= NX // 2, mode, mode - NX // 2)
    phase = 2 * np.pi * (wave[:, None] * np.arange(NX)[None, :] % NX) / NX
    norm = np.where((mode == 0) | (mode == NX // 2), np.sqrt(1 / NX), np.sqrt(2 / NX))
    four = norm[:, None] * np.where((mode <= NX // 2)[:, None], np.cos(phase), np.sin(phase))
    eigen = np.tile(2 - 2 * np.cos(2 * np.pi * wave / NX), G)[None, :]
    eigen = np.broadcast_to(eigen, (R, LANES)).astype(np.float32)

    def doubled(a):
        return np.concatenate(split(a), 1)

    to_mode = -four.T
    forward = np.concatenate(
        [doubled(np.kron(eye, a)) for a in (step @ to_mode, step @ to_mode, to_mode, to_mode)], 0
    )
    back = np.concatenate([np.kron(eye, 0.5 * four), np.kron(eye, four @ step)], 1)
    back = np.concatenate([doubled(back)] * 2, 0)
    up = level_map(NZ, LEV)
    zero = np.zeros_like(up)
    blocks = [
        [0.3 * up, zero, zero, zero],
        [zero, 0.25 * up, zero, 0.25 * up],
        [zero, zero, 0.25 * up, zero],
    ]
    rise = np.zeros((192, 4 * LEV))
    for i, row in enumerate(blocks):
        rise[64 * i : 64 * i + NZ] = np.concatenate(row, 1)
    rise = np.stack(split(rise))
    column, lane = np.arange(LANES) % COLS, np.arange(LANES)
    spread = (column[:, None] // R == lane[None, :] // NX).astype(ml_dtypes.bfloat16)
    gather = (lane[:, None] // NX == column[None, :] // R) / NX
    gather = np.concatenate([gather, gather], 0).astype(ml_dtypes.bfloat16)
    tally = np.zeros((64, ROWS))
    for z in range(NZ):
        tally[z, R * z : R * z + R] = 1
    tally = tally.astype(ml_dtypes.bfloat16)
    down = level_map(LEV, NZ)
    fall = np.zeros((4 * LEV, 192))
    for f, (source, gain) in enumerate(((0, 2.0), (1, 4.0), (2, 4.0), (0, 0.5))):
        fall[LEV * f : LEV * f + LEV, 64 * source : 64 * source + NZ] = gain * down
    fall = np.stack(split(fall.T))
    return dxm, forward, back, eigen, rise, spread, gather, tally, fall


def dot(a, b, dims=((1,), (0,)), precision=None):
    return lax.dot_general(a, b, (dims, ((), ())), precision=precision, preferred_element_type=F32)


def halves(a):
    high = a.astype(BF16)
    return high, (a - high.astype(F32)).astype(BF16)


def regroup(parts):
    lane = lax.broadcasted_iota(jnp.int32, (R, LANES), 1)
    low, even = lane < 64, (lane & 32) == 0
    a, b, c, d = parts
    a, c = jnp.where(low, a, pltpu.roll(c, 64, 1)), jnp.where(low, pltpu.roll(a, 64, 1), c)
    b, d = jnp.where(low, b, pltpu.roll(d, 64, 1)), jnp.where(low, pltpu.roll(b, 64, 1), d)
    a, b = jnp.where(even, a, pltpu.roll(b, 32, 1)), jnp.where(even, pltpu.roll(a, 96, 1), b)
    c, d = jnp.where(even, c, pltpu.roll(d, 32, 1)), jnp.where(even, pltpu.roll(c, 96, 1), d)
    return a, b, c, d


def crm_kernel(
    shape,
    state_hbm, fields_hbm, active_hbm, density_hbm, span_map_hbm, nbr_elem_hbm, nbr_side_hbm,
    dxm_hbm, forward_hbm, back_hbm, eigen_hbm, rise_hbm, spread_hbm, gather_hbm, tally_hbm, fall_hbm,
    tend_hbm, fresh_hbm, rows_hbm, edge_hbm,
    state_ref, fields_ref, active_ref, density_ref, span_map_ref, nbr_elem_ref, nbr_side_ref,
    dxm_ref, forward_ref, back_ref, eigen_ref, rise_ref, spread_ref, gather_ref, tally_ref, fall_ref,
    tend_ref, fresh_ref, rows_ref, edge_ref,
    raw, dxm, prof_wide, prof_rows, inv, coup, u1, w1, left, sol, cells, pres, means, fresh,
    from_left, from_right, sent, got, from_lower, from_upper, flat,
    in_sem, field_sem, out_sem, fresh_sem, send_sem, recv_sem, halo_send, halo_recv, relay_send, relay_recv,
):
    regions, spans = shape
    reach = spans // 4
    region, span = lax.axis_index("region"), lax.axis_index("span")
    me = region * spans + span
    total = regions * spans
    next_device, left_device = lax.rem(me + 1, total), lax.rem(me + total - 1, total)
    next_device = (lax.div(next_device, spans), lax.rem(next_device, spans))
    left_device = (lax.div(left_device, spans), lax.rem(left_device, spans))

    def along(offset):
        return (region, lax.rem(span + offset, spans))

    copies = {}
    pairs = dict(
        state=(state_hbm, state_ref), rise=(rise_hbm, rise_ref), active=(active_hbm, active_ref),
        spread=(spread_hbm, spread_ref), dxm=(dxm_hbm, dxm_ref), density=(density_hbm, density_ref),
        eigen=(eigen_hbm, eigen_ref), forward=(forward_hbm, forward_ref), back=(back_hbm, back_ref),
        gather=(gather_hbm, gather_ref), tally=(tally_hbm, tally_ref), fall=(fall_hbm, fall_ref),
        span_map=(span_map_hbm, span_map_ref), nbr_elem=(nbr_elem_hbm, nbr_elem_ref),
        nbr_side=(nbr_side_hbm, nbr_side_ref),
    )
    for n, (name, (source, target)) in enumerate(pairs.items()):
        copies[name] = pltpu.make_async_copy(source, target, in_sem.at[n])
        if n == 6:
            for k in range(CHUNKS):
                cut = slice(WIDE * k, min(WIDE * k + WIDE, NZ * NX * 3))
                copies[k] = pltpu.make_async_copy(
                    fields_hbm.at[:, cut], fields_ref.at[:, cut], field_sem.at[k]
                )
                copies[k].start()
        copies[name].start()

    barrier = pltpu.get_barrier_semaphore()

    def greet(i, _):
        for offset in (i, spans - i):
            pl.semaphore_signal(barrier, inc=1, device_id=along(offset), device_id_type=MESH)
        return _

    lax.fori_loop(1, reach + 1, greet, 0)
    for other in (left_device, next_device):
        pl.semaphore_signal(barrier, inc=1, device_id=other, device_id_type=MESH)

    lane = lax.broadcasted_iota(jnp.int32, (R, LANES), 1)
    row = lax.broadcasted_iota(jnp.int32, (R, LANES), 0)
    own = (lane & (R - 1)) == row
    zero16 = jnp.zeros((R, LANES), BF16)

    copies["state"].wait()
    copies["rise"].wait()
    copies["active"].wait()
    state = state_ref[...]
    profile = dot(rise_ref[0], state, ((1,), (1,))) + dot(rise_ref[1], state, ((1,), (1,)))
    flags = active_ref[...].reshape(1, COLS).astype(F32)
    p_high, p_low = halves(jnp.concatenate([jnp.exp(profile[:64]), profile[64:]], 0))
    prof_wide[...] = jnp.concatenate([p_high, p_low], 1).astype(F32)
    keep = jnp.concatenate([flags, flags], 1)
    prof_wide[63:64] = jnp.where(lane[:1] < COLS, keep, 0.0)
    wanted = [64 * f + z for f in range(3) for z in range(NZ)] + [63]
    for k in range(0, len(wanted), 8):
        lines = [prof_wide[i : i + 1] for i in wanted[k : k + 8]]
        lines = [jnp.where(own, jnp.broadcast_to(v, (R, LANES)), 0.0).astype(BF16) for v in lines]
        for i, v in zip(wanted[k : k + 8], lines):
            prof_rows[i] = v
    copies["spread"].wait()
    for f in range(3):
        top = 64 if f == 0 else NZ
        block = dot(prof_rows[64 * f : 64 * f + top].reshape(top * R, LANES), spread_ref[...])
        means[f, :top] = block.reshape(top, R, LANES)
    mask = means[0, 63] > 0.5

    for f in range(3):
        raw[f, 0] = zero16
        raw[f, NZ + 1] = zero16
    for k in range(CHUNKS):
        copies[k].wait()
        blocks = []
        for j in range(4 * k, 4 * k + 4):
            if j < 43:
                tiles = [fields_ref[R * g : R * g + R, LANES * j : LANES * j + LANES] for g in range(G)]
            else:
                tiles = [
                    jnp.concatenate([fields_ref[R * g : R * g + R, LANES * j :], zero16[:, :64]], 1)
                    for g in range(G)
                ]
            blocks.append(regroup(tiles))
        for j, block in enumerate(blocks):
            for part, level in zip(block, range(16 * k + 4 * j, min(16 * k + 4 * j + 4, 3 * NZ))):
                f, z = divmod(level, NZ)
                raw[f, z + 1] = part
    copies["dxm"].wait()
    for f in range(3):
        block = dot(raw[f, 1 : NZ + 1].reshape(ROWS, LANES), dxm_ref[...])
        dxm[f] = block.reshape(NZ, R, 2 * LANES)

    copies["density"].wait()
    copies["eigen"].wait()
    eigen = eigen_ref[...]
    inv[0] = jnp.zeros((R, LANES), F32)
    zero = inv[0]

    def factor(t, last):
        low, high, _ = last
        z = NZ - 1 - t
        rho, above = density_ref[t], density_ref[t + 1]
        below = jnp.where(t > 0, density_ref[jnp.maximum(t - 1, 0)], rho)
        f_up, f_down = 0.5 * (rho + above), 0.5 * (rho + below)
        i_low = 1.0 / ((eigen * rho + (f_up + f_down)) - f_down * low)
        e_low = f_up * i_low
        rho, below = density_ref[z], density_ref[z - 1]
        above = jnp.where(t > 0, density_ref[jnp.minimum(z + 1, NZ - 1)], rho)
        f_up, f_down = 0.5 * (rho + above), 0.5 * (rho + below)
        diag = (eigen * rho + (f_up + f_down)) - f_up * high
        i_high = 1.0 / diag
        e_high = f_down * i_high
        stores = [(inv, t, i_low), (coup, t, e_low), (inv, z, i_high), (coup, z, e_high)]
        return stores, (e_low, e_high, diag)

    def advect(z, carry):
        (u_m, u), (w_m, w), (q_m, q), (rw_mm, rw_m), rain = carry
        u_p, w_p, q_p = [raw[f, z + 2].astype(F32) for f in range(3)]
        rho = density_ref[z]
        half = 0.125 * w
        du, mean_u = dxm[0, z, :, :LANES], dxm[0, z, :, LANES:]
        dw = dxm[1, z, :, :LANES]
        dq, mean_q = dxm[2, z, :, :LANES], dxm[2, z, :, LANES:]
        new_u = u - u * du - half * (u_p - u_m) + (means[2, z] - mean_u)
        new_w = w - u * dw - half * (w_p - w_m) + (0.125 * q - 0.5 * mean_q)
        new_q = q - u * dq - half * (q_p - q_m) + (means[1, z] - mean_q)
        x = new_q - means[0, z]
        cond = jnp.maximum(x, 0.0) + jnp.log(1.0 + jnp.exp(-jnp.abs(x)))
        q2 = new_q - 0.5 * cond
        rw = rho * new_w
        stores = [
            (u1, z, new_u),
            (w1, z, new_w),
            (fresh, 2 * NZ + z, jnp.where(mask, q2, q).astype(BF16)),
            (cells.at[0], z, jnp.concatenate(halves(cond), 1)),
            (cells.at[1], z, jnp.concatenate(halves(q2 - q), 1)),
            (left.at[:, :, : 2 * LANES], z + 1, jnp.concatenate(halves(rho * new_u), 1)),
            (left.at[:, :, 2 * LANES :], z, jnp.concatenate(halves(0.5 * (rw - rw_mm)), 1)),
        ]
        return stores, ((u, u_p), (w, w_p), (q, q_p), (rw_m, rw), rain + rho * cond)

    def both_passes(t, carry):
        stores, last = factor(t, carry[0])
        more, levels = advect(2 * t, carry[1])
        most, levels = advect(2 * t + 1, levels)
        for ref, z, value in stores + more + most:
            ref[z] = value
        return last, levels

    first = tuple((zero, raw[f, 1].astype(F32)) for f in range(3)) + ((zero, zero), zero)
    last, levels = lax.fori_loop(0, NZ // 2, both_passes, ((zero, zero, zero), first))
    left[NZ, :, 2 * LANES :] = jnp.concatenate(halves(-0.5 * levels[3][0]), 1)
    mid = NZ // 2
    centre = 1.0 / (last[2] - 0.5 * (density_ref[mid - 1] + density_ref[mid]) * last[0])

    copies["gather"].wait()
    parts = dot(jnp.concatenate(halves(levels[4] * (2.0 / NZ)), 1), gather_ref[...])
    precip = jnp.sum(jnp.where(own, parts, 0.0), 0, keepdims=True)[:, :COLS]
    copies["span_map"].wait()
    order = lax.broadcasted_iota(jnp.int32, (spans, COLS), 0) + span
    target = jnp.where(order >= spans, order - spans, order)
    hot = jnp.where((span_map_ref[...].reshape(1, COLS) == target) & (flags > 0.5), 1.0, 0.0)
    upper = lax.broadcasted_iota(jnp.int32, (COLS, COLS), 0) < lax.broadcasted_iota(jnp.int32, (COLS, COLS), 1)
    before = dot(hot.astype(BF16), jnp.where(upper, 1.0, 0.0).astype(BF16))
    one = jnp.sum(jnp.where(before < 0.5, hot, 0.0) * precip, 1, keepdims=True)
    two = jnp.sum(jnp.where(before > 0.5, hot, 0.0) * precip, 1, keepdims=True)
    load = jnp.sum(hot, 1, keepdims=True)
    place = lax.broadcasted_iota(jnp.int32, (spans, LANES), 1)
    block = jnp.where(place == 0, one, jnp.where(place == 1, two, jnp.where(place == 2, load, 0.0)))
    for i in range(spans):
        sent[i] = block[i : i + 1]
    got[span] = block[:1]

    pl.semaphore_wait(barrier, 2 * reach + 2)
    relays = [
        pltpu.make_async_remote_copy(
            src_ref=sent.at[pl.ds(first_row, count)], dst_ref=slot, send_sem=relay_send.at[n],
            recv_sem=relay_recv.at[n], device_id=along(offset), device_id_type=MESH,
        )
        for n, (first_row, count, slot, offset) in enumerate(
            (
                (reach + 1, reach, from_lower, reach),
                (2 * reach + 1, reach - 1, from_upper, spans - reach),
            )
        )
    ]
    for relay in relays:
        relay.start()

    def give(source, slot, offset):
        pltpu.make_async_remote_copy(
            src_ref=source, dst_ref=got.at[slot], send_sem=send_sem, recv_sem=recv_sem,
            device_id=along(offset), device_id_type=MESH,
        ).start()

    def give_near(i, _):
        for offset in (i, spans - i):
            give(sent.at[offset], span, offset)
        return _

    lax.fori_loop(1, reach + 1, give_near, 0)

    def give_back(k):
        blocks = []
        for j in range(4 * k, 4 * k + 4):
            blocks.append(
                regroup([fresh[v] if v < 3 * NZ else zero16 for v in range(4 * j, 4 * j + 4)])
            )
        for j, block in enumerate(blocks):
            j += 4 * k
            for g, part in enumerate(block):
                if j < 43:
                    fresh_ref[R * g : R * g + R, LANES * j : LANES * j + LANES] = part
                else:
                    fresh_ref[R * g : R * g + R, LANES * j :] = part[:, :64]
        cut = slice(WIDE * k, min(WIDE * k + WIDE, NZ * NX * 3))
        copy = pltpu.make_async_copy(fresh_ref.at[:, cut], fresh_hbm.at[:, cut], fresh_sem.at[k])
        copy.start()
        return copy

    leaving = [give_back(k) for k in range(8, CHUNKS)]

    copies["forward"].wait()
    right = dot(left[1:].reshape(ROWS, 4 * LANES), forward_ref[...])
    sol[...] = (right[:, :LANES] + right[:, LANES:]).reshape(NZ, R, LANES)
    low, high = sol[0], sol[NZ - 1]
    for t in range(1, mid):
        z = NZ - 1 - t
        low = sol[t] + coup[t - 1] * low
        high = sol[z] + coup[z + 1] * high
        sol[t], sol[z] = low, high
    high = centre * (high + coup[mid - 1] * low)
    low = inv[mid - 1] * low + coup[mid - 1] * high
    left[mid - 1, :, : 2 * LANES] = jnp.concatenate(halves(low), 1)
    left[mid, :, : 2 * LANES] = jnp.concatenate(halves(high), 1)
    for t in range(mid - 2, -1, -1):
        z = NZ - 1 - t
        low = inv[t] * sol[t] + coup[t] * low
        high = inv[z] * sol[z] + coup[z] * high
        left[t, :, : 2 * LANES] = jnp.concatenate(halves(low), 1)
        left[z, :, : 2 * LANES] = jnp.concatenate(halves(high), 1)
    copies["back"].wait()
    both = dot(left[:NZ, :, : 2 * LANES].reshape(ROWS, 2 * LANES), back_ref[...])
    pres[0] = zero
    pres[NZ + 1] = zero
    pres[1 : NZ + 1] = (both[:, :LANES] + both[:, 2 * LANES : 3 * LANES]).reshape(NZ, R, LANES)
    sol[...] = (both[:, LANES : 2 * LANES] + both[:, 3 * LANES :]).reshape(NZ, R, LANES)

    @pl.loop(0, NZ // 2)
    def _(t):
        z = 2 * t
        here = pl.ds(z, 2)
        u, w = raw[0, pl.ds(z + 1, 2)].astype(F32), raw[1, pl.ds(z + 1, 2)].astype(F32)
        u2 = u1[here] - sol[here]
        w2 = w1[here] - (pres[pl.ds(z + 2, 2)] - pres[here])
        u_out = jnp.where(mask[None], u2, u).astype(BF16)
        w_out = jnp.where(mask[None], w2, w).astype(BF16)
        change = jnp.concatenate(halves(u2 - u), 2)
        fresh[here] = u_out
        fresh[pl.ds(NZ + z, 2)] = w_out
        cells[2, here] = change

    for f in range(3):
        block = dot(cells[f].reshape(ROWS, 2 * LANES), gather_ref[...])
        means[f, :NZ] = block.reshape(NZ, R, LANES)
    lane_high = lane < COLS

    @pl.loop(0, NZ // 2)
    def _(t):
        here = pl.ds(2 * t, 2)
        values = []
        for f in range(3):
            value = jnp.where(own[None], means[f, here], 0.0)
            high = value.astype(BF16).astype(F32)
            values.append(jnp.where(lane_high[None], high, value - high).astype(BF16))
        left[here, :, : 3 * LANES] = jnp.concatenate(values, 2)

    copies["tally"].wait()
    sums = dot(tally_ref[...], left[:NZ, :, : 3 * LANES].reshape(ROWS, 3 * LANES))
    sums = jnp.concatenate([sums[:, LANES * f : LANES * f + LANES] for f in range(3)], 0)
    t_high, t_low = halves(jnp.where(keep > 0.5, sums, 0.0).T)
    copies["fall"].wait()
    tend = dot(t_high, fall_ref[0]) + dot(t_low, fall_ref[0]) + dot(t_high, fall_ref[1])
    tend_ref[...] = (tend[:COLS] + tend[COLS:]).astype(BF16)
    half = COLS // 2
    halos = [
        pltpu.make_async_remote_copy(
            src_ref=tend_ref.at[part], dst_ref=slot, send_sem=halo_send.at[n], recv_sem=halo_recv.at[n],
            device_id=other, device_id_type=MESH,
        )
        for n, (part, slot, other) in enumerate(
            ((pl.ds(half, half), from_left, next_device), (pl.ds(0, half), from_right, left_device))
        )
    ]
    for halo in halos:
        halo.start()
    leaving.append(pltpu.make_async_copy(tend_ref, tend_hbm, out_sem.at[0]))
    leaving[-1].start()

    for relay in relays:
        relay.wait_recv()

    def pass_up(i, _):
        give(from_lower.at[i], lax.rem(span + spans - reach, spans), i + 1)
        return _

    def pass_down(i, _):
        give(from_upper.at[i], lax.rem(span + reach, spans), spans - reach + 1 + i)
        return _

    lax.fori_loop(0, reach, pass_up, 0)
    lax.fori_loop(0, reach - 1, pass_down, 0)

    leaving += [give_back(k) for k in range(8)]

    copies["nbr_elem"].wait()
    copies["nbr_side"].wait()
    elems = COLS // 4
    cell = lax.broadcasted_iota(jnp.int32, (2 * COLS, elems), 0)
    elem, corner = cell >> 2, cell & 3
    c_low, c_high = corner & 1, corner >> 1
    home = lax.broadcasted_iota(jnp.int32, (2 * COLS, elems), 1) + elems // 2
    faces = (1 - c_high, c_low, c_high, 1 - c_low)
    everyone = total * elems
    picks = []
    for side in range(4):
        near = nbr_elem_ref[side : side + 1, :] - (me * elems - elems // 2)
        near = jnp.where(near < 0, near + everyone, near)
        near = jnp.where(near >= everyone, near - everyone, near)
        theirs = nbr_side_ref[side : side + 1, :]
        face = jnp.where(
            theirs < 2, jnp.where(theirs == 0, faces[0], faces[1]), jnp.where(theirs == 2, faces[2], faces[3])
        )
        pick = jnp.where(near == elem, face, 0) + jnp.where(home == elem, faces[side], 0)
        picks.append((0.5 * pick.astype(F32)).T.astype(BF16))

    for halo in halos:
        halo.wait()
    table = jnp.concatenate([from_left[...], tend_ref[...], from_right[...]], 0)
    for side in range(4):
        edge_ref[:, side, :] = dot(picks[side], table)
    leaving.append(pltpu.make_async_copy(edge_ref, edge_hbm, out_sem.at[1]))
    leaving[-1].start()
    for relay in relays:
        relay.wait_send()

    lower = lax.broadcasted_iota(jnp.int32, (spans, spans), 0) > lax.broadcasted_iota(jnp.int32, (spans, spans), 1)
    lower = jnp.where(lower, 1.0, 0.0).astype(BF16)
    others = pl.ds(0, spans - 1)
    pltpu.make_async_copy(got.at[others], got.at[others], recv_sem).wait()
    for i in range(spans):
        flat[i : i + 1] = got[i]
    table = flat[...]
    load = jnp.broadcast_to(table[:, 2:3], (spans, LANES))
    start = dot(lower, load.astype(BF16))
    slot = place.astype(F32)
    rows = jnp.where((start == slot) & (load > 0.5), table[:, 0:1], 0.0)
    rows += jnp.where((start + 1.0 == slot) & (load > 1.5), table[:, 1:2], 0.0)
    rows_ref[...] = jnp.sum(rows, 0, keepdims=True)[:, : rows_ref.shape[1]]
    leaving.append(pltpu.make_async_copy(rows_ref, rows_hbm, out_sem.at[2]))
    leaving[-1].start()
    pltpu.make_async_copy(sent.at[others], sent.at[others], send_sem).wait()
    for copy in leaving:
        copy.wait()


def crm_call(shape, slots, column_state, crm_fields, active, density, span_map, nbr_elem, nbr_side):
    constants = [jnp.asarray(a) for a in tables()]
    hbm = pl.BlockSpec(memory_space=pltpu.HBM)
    levels = (NZ, R, LANES)
    spans = shape[1]
    return pl.pallas_call(
        functools.partial(crm_kernel, shape),
        out_shape=(
            jax.ShapeDtypeStruct((COLS, 4 * LEV), BF16),
            jax.ShapeDtypeStruct((COLS, 3 * NZ * NX), BF16),
            jax.ShapeDtypeStruct((1, slots), F32),
            jax.ShapeDtypeStruct((COLS // 4, 4, 4 * LEV), F32),
        ),
        in_specs=[hbm] * (7 + len(constants)),
        out_specs=(hbm,) * 4,
        scratch_shapes=[
            pltpu.VMEM((COLS, 4 * LEV), BF16),
            pltpu.VMEM((COLS, 3 * NZ * NX), BF16),
            pltpu.VMEM((COLS,), jnp.int32),
            pltpu.SMEM((NZ,), F32),
            pltpu.VMEM((COLS,), jnp.int32),
            pltpu.VMEM((4, COLS // 4), jnp.int32),
            pltpu.VMEM((4, COLS // 4), jnp.int32),
            *[pltpu.VMEM(a.shape, a.dtype) for a in constants],
            pltpu.VMEM((COLS, 4 * LEV), BF16),
            pltpu.VMEM((COLS, 3 * NZ * NX), BF16),
            pltpu.VMEM((1, slots), F32),
            pltpu.VMEM((COLS // 4, 4, 4 * LEV), F32),
            pltpu.VMEM((3, NZ + 2, R, LANES), BF16),
            pltpu.VMEM((3, NZ, R, 2 * LANES), F32),
            pltpu.VMEM((192, LANES), F32),
            pltpu.VMEM((192, R, LANES), BF16),
            pltpu.VMEM(levels, F32),
            pltpu.VMEM(levels, F32),
            pltpu.VMEM(levels, F32),
            pltpu.VMEM(levels, F32),
            pltpu.VMEM((NZ + 1, R, 4 * LANES), BF16),
            pltpu.VMEM(levels, F32),
            pltpu.VMEM((3, NZ, R, 2 * LANES), BF16),
            pltpu.VMEM((NZ + 2, R, LANES), F32),
            pltpu.VMEM((3, 64, R, LANES), F32),
            pltpu.VMEM((3 * NZ, R, LANES), BF16),
            pltpu.VMEM((COLS // 2, 4 * LEV), BF16),
            pltpu.VMEM((COLS // 2, 4 * LEV), BF16),
            pltpu.VMEM((spans, 1, LANES), F32),
            pltpu.VMEM((spans, 1, LANES), F32),
            pltpu.VMEM((spans // 4, 1, LANES), F32),
            pltpu.VMEM((spans // 4 - 1, 1, LANES), F32),
            pltpu.VMEM((spans, LANES), F32),
            pltpu.SemaphoreType.DMA((15,)),
            pltpu.SemaphoreType.DMA((CHUNKS,)),
            pltpu.SemaphoreType.DMA((3,)),
            pltpu.SemaphoreType.DMA((CHUNKS,)),
            pltpu.SemaphoreType.DMA,
            pltpu.SemaphoreType.DMA,
            pltpu.SemaphoreType.DMA((2,)),
            pltpu.SemaphoreType.DMA((2,)),
            pltpu.SemaphoreType.DMA((2,)),
            pltpu.SemaphoreType.DMA((2,)),
        ],
        compiler_params=pltpu.CompilerParams(
            collective_id=0, has_side_effects=True, vmem_limit_bytes=63 * 2**20
        ),
    )(column_state, crm_fields, active, density, span_map, nbr_elem.T, nbr_side.T, *constants)


def hand_over_kernel(*refs):
    count = (len(refs) - 2) // 3
    came, went = refs[-2:]
    pieces = []
    for source, target, stage in zip(refs[:count], refs[count:], refs[2 * count :]):
        rows = source.shape[0]
        step = rows // 4 if rows == COLS and source.shape[1] > 4 * LEV else rows
        for top in range(0, rows, step):
            cut = pl.ds(top, step)
            pieces.append((source.at[cut], stage.at[cut], target.at[cut]))
    inward = [pltpu.make_async_copy(a, b, came.at[n]) for n, (a, b, _) in enumerate(pieces)]
    outward = [pltpu.make_async_copy(b, c, went.at[n]) for n, (_, b, c) in enumerate(pieces)]
    for copy in inward:
        copy.start()
    for first, second in zip(inward, outward):
        first.wait()
        second.start()
    for copy in outward:
        copy.wait()


def hand_over(*arrays):
    hbm = pl.BlockSpec(memory_space=pltpu.HBM)
    return pl.pallas_call(
        hand_over_kernel,
        out_shape=tuple(jax.ShapeDtypeStruct(a.shape, a.dtype) for a in arrays),
        in_specs=[hbm] * len(arrays),
        out_specs=(hbm,) * len(arrays),
        scratch_shapes=[pltpu.VMEM(a.shape, a.dtype) for a in arrays]
        + [pltpu.SemaphoreType.DMA((len(arrays) + 3,))] * 2,
        compiler_params=pltpu.CompilerParams(vmem_limit_bytes=63 * 2**20),
    )(*arrays)


def body(shape, column_state, crm_fields, span_map, active, density, nbr_elem, nbr_side):
    results = crm_call(
        shape, COLS * 3 // 8, column_state, crm_fields, active, density, span_map, nbr_elem, nbr_side
    )
    tendency, fresh, rows, edge_sums = hand_over(*results)
    return (tendency, fresh, rows[0], edge_sums)


def solution(mesh):
    rows = P(("region", "span"), None)
    line = P(("region", "span"))
    return jax.shard_map(
        functools.partial(body, (mesh.shape["region"], mesh.shape["span"])),
        mesh=mesh,
        in_specs=(rows, rows, line, line, P(), rows, rows),
        out_specs=(rows, rows, line, P(("region", "span"), None, None)),
        check_vma=False,
    )
```

```python
import functools

import jax
import jax.numpy as jnp
import ml_dtypes
import numpy as np
from jax import lax
from jax.experimental import pallas as pl
from jax.experimental.pallas import tpu as pltpu
from jax.sharding import PartitionSpec as P

MESH = pl.DeviceIdType.MESH
LEV, NZ, NX, COLS = 72, 58, 32, 64
G, R, LANES = 4, 16, 128
ROWS = NZ * R
WIDE, CHUNKS = 512, 11
F32, BF16 = jnp.float32, jnp.bfloat16


def split(a):
    high = a.astype(ml_dtypes.bfloat16)
    return high, (a - high.astype(np.float64)).astype(ml_dtypes.bfloat16)


def level_map(count_to, count_from):
    index = np.arange(count_to)
    numerator = (2 * index + 1) * count_from - count_to
    lower = np.clip(numerator // (2 * count_to), 0, count_from - 2)
    fraction = np.clip((numerator - lower * 2 * count_to) / (2 * count_to), 0.0, 1.0)
    target = np.arange(count_from)[None, :]
    return (1 - fraction)[:, None] * (target == lower[:, None]) + fraction[:, None] * (
        target == lower[:, None] + 1
    )


@functools.cache
def tables():
    eye = np.eye(G)
    step = 0.5 * (np.roll(np.eye(NX), 1, 0) - np.roll(np.eye(NX), -1, 0))
    dxm = np.concatenate(
        [np.kron(eye, 0.25 * step), np.kron(eye, np.full((NX, NX), 0.25 / NX))], 1
    ).astype(ml_dtypes.bfloat16)
    mode = np.arange(NX)
    wave = np.where(mode <= NX // 2, mode, mode - NX // 2)
    phase = 2 * np.pi * (wave[:, None] * np.arange(NX)[None, :] % NX) / NX
    norm = np.where((mode == 0) | (mode == NX // 2), np.sqrt(1 / NX), np.sqrt(2 / NX))
    four = norm[:, None] * np.where((mode <= NX // 2)[:, None], np.cos(phase), np.sin(phase))
    eigen = np.tile(2 - 2 * np.cos(2 * np.pi * wave / NX), G)[None, :]
    eigen = np.broadcast_to(eigen, (R, LANES)).astype(np.float32)

    def doubled(a):
        return np.concatenate(split(a), 1)

    to_mode = -four.T
    forward = np.concatenate(
        [doubled(np.kron(eye, a)) for a in (step @ to_mode, step @ to_mode, to_mode, to_mode)], 0
    )
    back = np.concatenate([np.kron(eye, 0.5 * four), np.kron(eye, four @ step)], 1)
    back = np.concatenate([doubled(back)] * 2, 0)
    up = level_map(NZ, LEV)
    zero = np.zeros_like(up)
    blocks = [
        [0.3 * up, zero, zero, zero],
        [zero, 0.25 * up, zero, 0.25 * up],
        [zero, zero, 0.25 * up, zero],
    ]
    rise = np.zeros((192, 4 * LEV))
    for i, row in enumerate(blocks):
        rise[64 * i : 64 * i + NZ] = np.concatenate(row, 1)
    rise = np.stack(split(rise))
    column, lane = np.arange(LANES) % COLS, np.arange(LANES)
    spread = (column[:, None] // R == lane[None, :] // NX).astype(ml_dtypes.bfloat16)
    gather = (lane[:, None] // NX == column[None, :] // R) / NX
    gather = np.concatenate([gather, gather], 0).astype(ml_dtypes.bfloat16)
    tally = np.zeros((64, ROWS))
    for z in range(NZ):
        tally[z, R * z : R * z + R] = 1
    tally = tally.astype(ml_dtypes.bfloat16)
    down = level_map(LEV, NZ)
    fall = np.zeros((4 * LEV, 192))
    for f, (source, gain) in enumerate(((0, 2.0), (1, 4.0), (2, 4.0), (0, 0.5))):
        fall[LEV * f : LEV * f + LEV, 64 * source : 64 * source + NZ] = gain * down
    fall = np.stack(split(fall.T))
    return dxm, forward, back, eigen, rise, spread, gather, tally, fall


def dot(a, b, dims=((1,), (0,)), precision=None):
    return lax.dot_general(a, b, (dims, ((), ())), precision=precision, preferred_element_type=F32)


def halves(a):
    high = a.astype(BF16)
    return high, (a - high.astype(F32)).astype(BF16)


def regroup(parts):
    lane = lax.broadcasted_iota(jnp.int32, (R, LANES), 1)
    low, even = lane < 64, (lane & 32) == 0
    a, b, c, d = parts
    a, c = jnp.where(low, a, pltpu.roll(c, 64, 1)), jnp.where(low, pltpu.roll(a, 64, 1), c)
    b, d = jnp.where(low, b, pltpu.roll(d, 64, 1)), jnp.where(low, pltpu.roll(b, 64, 1), d)
    a, b = jnp.where(even, a, pltpu.roll(b, 32, 1)), jnp.where(even, pltpu.roll(a, 96, 1), b)
    c, d = jnp.where(even, c, pltpu.roll(d, 32, 1)), jnp.where(even, pltpu.roll(c, 96, 1), d)
    return a, b, c, d


def crm_kernel(
    shape,
    state_hbm, fields_hbm, active_hbm, density_hbm, span_map_hbm, nbr_elem_hbm, nbr_side_hbm,
    dxm_hbm, forward_hbm, back_hbm, eigen_hbm, rise_hbm, spread_hbm, gather_hbm, tally_hbm, fall_hbm,
    tend_ref, fresh_ref, got, edge_ref,
    state_ref, fields_ref, active_ref, density_ref, span_map_ref, nbr_elem_ref, nbr_side_ref,
    dxm_ref, forward_ref, back_ref, eigen_ref, rise_ref, spread_ref, gather_ref, tally_ref, fall_ref,
    raw, dxm, prof_wide, prof_rows, inv, coup, u1, w1, left, sol, cells, pres, means, fresh,
    from_left, from_right, sent, from_lower, from_upper,
    in_sem, field_sem, out_sem, send_sem, recv_sem, halo_send, halo_recv, relay_send, relay_recv,
):
    regions, spans = shape
    reach = spans // 4
    region, span = lax.axis_index("region"), lax.axis_index("span")
    me = region * spans + span
    total = regions * spans
    next_device, left_device = lax.rem(me + 1, total), lax.rem(me + total - 1, total)
    next_device = (lax.div(next_device, spans), lax.rem(next_device, spans))
    left_device = (lax.div(left_device, spans), lax.rem(left_device, spans))

    def along(offset):
        return (region, lax.rem(span + offset, spans))

    barrier = pltpu.get_barrier_semaphore()

    def greet(i, _):
        for offset in (reach - i, spans - reach + i):
            pl.semaphore_signal(barrier, inc=1, device_id=along(offset), device_id_type=MESH)
        return _

    lax.fori_loop(0, reach, greet, 0)
    for other in (left_device, next_device):
        pl.semaphore_signal(barrier, inc=1, device_id=other, device_id_type=MESH)

    copies = {}
    pairs = dict(
        state=(state_hbm, state_ref), rise=(rise_hbm, rise_ref), active=(active_hbm, active_ref),
        spread=(spread_hbm, spread_ref), dxm=(dxm_hbm, dxm_ref), density=(density_hbm, density_ref),
        eigen=(eigen_hbm, eigen_ref), forward=(forward_hbm, forward_ref), back=(back_hbm, back_ref),
        gather=(gather_hbm, gather_ref), tally=(tally_hbm, tally_ref), fall=(fall_hbm, fall_ref),
        span_map=(span_map_hbm, span_map_ref), nbr_elem=(nbr_elem_hbm, nbr_elem_ref),
        nbr_side=(nbr_side_hbm, nbr_side_ref),
    )
    for n, (name, (source, target)) in enumerate(pairs.items()):
        copies[name] = pltpu.make_async_copy(source, target, in_sem.at[n])
        if n == 6:
            for k in range(CHUNKS):
                cut = slice(WIDE * k, min(WIDE * k + WIDE, NZ * NX * 3))
                copies[k] = pltpu.make_async_copy(
                    fields_hbm.at[:, cut], fields_ref.at[:, cut], field_sem.at[k]
                )
                copies[k].start()
        copies[name].start()

    lane = lax.broadcasted_iota(jnp.int32, (R, LANES), 1)
    row = lax.broadcasted_iota(jnp.int32, (R, LANES), 0)
    own = (lane & (R - 1)) == row
    zero16 = jnp.zeros((R, LANES), BF16)

    copies["state"].wait()
    copies["rise"].wait()
    copies["active"].wait()
    state = state_ref[...]
    profile = dot(rise_ref[0], state, ((1,), (1,))) + dot(rise_ref[1], state, ((1,), (1,)))
    flags = active_ref[...].reshape(1, COLS).astype(F32)
    p_high, p_low = halves(jnp.concatenate([jnp.exp(profile[:64]), profile[64:]], 0))
    prof_wide[...] = jnp.concatenate([p_high, p_low], 1).astype(F32)
    keep = jnp.concatenate([flags, flags], 1)
    prof_wide[63:64] = jnp.where(lane[:1] < COLS, keep, 0.0)
    wanted = [64 * f + z for f in range(3) for z in range(NZ)] + [63]
    for k in range(0, len(wanted), 8):
        lines = [prof_wide[i : i + 1] for i in wanted[k : k + 8]]
        lines = [jnp.where(own, jnp.broadcast_to(v, (R, LANES)), 0.0).astype(BF16) for v in lines]
        for i, v in zip(wanted[k : k + 8], lines):
            prof_rows[i] = v
    copies["spread"].wait()
    for f in range(3):
        top = 64 if f == 0 else NZ
        block = dot(prof_rows[64 * f : 64 * f + top].reshape(top * R, LANES), spread_ref[...])
        means[f, :top] = block.reshape(top, R, LANES)
    mask = means[0, 63] > 0.5

    for f in range(3):
        raw[f, 0] = zero16
        raw[f, NZ + 1] = zero16
    for k in range(CHUNKS):
        copies[k].wait()
        blocks = []
        for j in range(4 * k, 4 * k + 4):
            if j < 43:
                tiles = [fields_ref[R * g : R * g + R, LANES * j : LANES * j + LANES] for g in range(G)]
            else:
                tiles = [
                    jnp.concatenate([fields_ref[R * g : R * g + R, LANES * j :], zero16[:, :64]], 1)
                    for g in range(G)
                ]
            blocks.append(regroup(tiles))
        for j, block in enumerate(blocks):
            for part, level in zip(block, range(16 * k + 4 * j, min(16 * k + 4 * j + 4, 3 * NZ))):
                f, z = divmod(level, NZ)
                raw[f, z + 1] = part
    copies["dxm"].wait()
    for f in range(3):
        block = dot(raw[f, 1 : NZ + 1].reshape(ROWS, LANES), dxm_ref[...])
        dxm[f] = block.reshape(NZ, R, 2 * LANES)

    copies["density"].wait()
    copies["eigen"].wait()
    eigen = eigen_ref[...]
    inv[0] = jnp.zeros((R, LANES), F32)
    zero = inv[0]

    def factor(t, last):
        low, high, _ = last
        z = NZ - 1 - t
        rho, above = density_ref[t], density_ref[t + 1]
        below = jnp.where(t > 0, density_ref[jnp.maximum(t - 1, 0)], rho)
        f_up, f_down = 0.5 * (rho + above), 0.5 * (rho + below)
        i_low = 1.0 / ((eigen * rho + (f_up + f_down)) - f_down * low)
        e_low = f_up * i_low
        rho, below = density_ref[z], density_ref[z - 1]
        above = jnp.where(t > 0, density_ref[jnp.minimum(z + 1, NZ - 1)], rho)
        f_up, f_down = 0.5 * (rho + above), 0.5 * (rho + below)
        diag = (eigen * rho + (f_up + f_down)) - f_up * high
        i_high = 1.0 / diag
        e_high = f_down * i_high
        stores = [(inv, t, i_low), (coup, t, e_low), (inv, z, i_high), (coup, z, e_high)]
        return stores, (e_low, e_high, diag)

    def advect(z, carry):
        (u_m, u), (w_m, w), (q_m, q), (rw_mm, rw_m), rain = carry
        u_p, w_p, q_p = [raw[f, z + 2].astype(F32) for f in range(3)]
        rho = density_ref[z]
        half = 0.125 * w
        du, mean_u = dxm[0, z, :, :LANES], dxm[0, z, :, LANES:]
        dw = dxm[1, z, :, :LANES]
        dq, mean_q = dxm[2, z, :, :LANES], dxm[2, z, :, LANES:]
        new_u = u - u * du - half * (u_p - u_m) + (means[2, z] - mean_u)
        new_w = w - u * dw - half * (w_p - w_m) + (0.125 * q - 0.5 * mean_q)
        new_q = q - u * dq - half * (q_p - q_m) + (means[1, z] - mean_q)
        x = new_q - means[0, z]
        cond = jnp.maximum(x, 0.0) + jnp.log(1.0 + jnp.exp(-jnp.abs(x)))
        q2 = new_q - 0.5 * cond
        rw = rho * new_w
        stores = [
            (u1, z, new_u),
            (w1, z, new_w),
            (fresh, 2 * NZ + z, jnp.where(mask, q2, q).astype(BF16)),
            (cells.at[0], z, jnp.concatenate(halves(cond), 1)),
            (cells.at[1], z, jnp.concatenate(halves(q2 - q), 1)),
            (left.at[:, :, : 2 * LANES], z + 1, jnp.concatenate(halves(rho * new_u), 1)),
            (left.at[:, :, 2 * LANES :], z, jnp.concatenate(halves(0.5 * (rw - rw_mm)), 1)),
        ]
        return stores, ((u, u_p), (w, w_p), (q, q_p), (rw_m, rw), rain + rho * cond)

    def both_passes(t, carry):
        stores, last = factor(t, carry[0])
        more, levels = advect(2 * t, carry[1])
        most, levels = advect(2 * t + 1, levels)
        for ref, z, value in stores + more + most:
            ref[z] = value
        return last, levels

    first = tuple((zero, raw[f, 1].astype(F32)) for f in range(3)) + ((zero, zero), zero)
    last, levels = lax.fori_loop(0, NZ // 2, both_passes, ((zero, zero, zero), first))
    left[NZ, :, 2 * LANES :] = jnp.concatenate(halves(-0.5 * levels[3][0]), 1)
    mid = NZ // 2
    centre = 1.0 / (last[2] - 0.5 * (density_ref[mid - 1] + density_ref[mid]) * last[0])

    copies["gather"].wait()
    parts = dot(jnp.concatenate(halves(levels[4] * (2.0 / NZ)), 1), gather_ref[...])
    precip = jnp.sum(jnp.where(own, parts, 0.0), 0, keepdims=True)[:, :COLS]
    copies["span_map"].wait()
    order = lax.broadcasted_iota(jnp.int32, (spans, COLS), 0) + span
    target = jnp.where(order >= spans, order - spans, order)
    hot = jnp.where((span_map_ref[...].reshape(1, COLS) == target) & (flags > 0.5), 1.0, 0.0)
    upper = lax.broadcasted_iota(jnp.int32, (COLS, COLS), 0) < lax.broadcasted_iota(jnp.int32, (COLS, COLS), 1)
    before = dot(hot.astype(BF16), jnp.where(upper, 1.0, 0.0).astype(BF16))
    one = jnp.sum(jnp.where(before < 0.5, hot, 0.0) * precip, 1, keepdims=True)
    two = jnp.sum(jnp.where(before > 0.5, hot, 0.0) * precip, 1, keepdims=True)
    load = jnp.sum(hot, 1, keepdims=True)
    place = lax.broadcasted_iota(jnp.int32, (spans, LANES), 1)
    block = jnp.where(place < 32, load, jnp.where(place < 64, one, two))
    for i in range(spans):
        sent[i] = block[i : i + 1]
    mine = pltpu.make_async_copy(sent.at[0], got.at[span], out_sem)
    mine.start()

    pl.semaphore_wait(barrier, 2 * reach + 2)
    relays = [
        pltpu.make_async_remote_copy(
            src_ref=sent.at[pl.ds(first_row, count)], dst_ref=slot, send_sem=relay_send.at[n],
            recv_sem=relay_recv.at[n], device_id=along(offset), device_id_type=MESH,
        )
        for n, (first_row, count, slot, offset) in enumerate(
            (
                (reach + 1, reach, from_lower, reach),
                (2 * reach + 1, reach - 1, from_upper, spans - reach),
            )
        )
    ]
    for relay in relays:
        relay.start()

    def give(source, slot, offset):
        pltpu.make_async_remote_copy(
            src_ref=source, dst_ref=got.at[slot], send_sem=send_sem, recv_sem=recv_sem,
            device_id=along(offset), device_id_type=MESH,
        ).start()

    def give_near(i, _):
        for offset in (reach - i, spans - reach + i):
            give(sent.at[offset], span, offset)
        return _

    lax.fori_loop(0, reach, give_near, 0)

    def give_back(k):
        blocks = []
        for j in range(4 * k, 4 * k + 4):
            blocks.append(
                regroup([fresh[v] if v < 3 * NZ else zero16 for v in range(4 * j, 4 * j + 4)])
            )
        for j, block in enumerate(blocks):
            j += 4 * k
            for g, part in enumerate(block):
                if j < 43:
                    fresh_ref[R * g : R * g + R, LANES * j : LANES * j + LANES] = part
                else:
                    fresh_ref[R * g : R * g + R, LANES * j :] = part[:, :64]

    for k in range(8, CHUNKS):
        give_back(k)

    copies["forward"].wait()
    right = dot(left[1:].reshape(ROWS, 4 * LANES), forward_ref[...])
    sol[...] = (right[:, :LANES] + right[:, LANES:]).reshape(NZ, R, LANES)
    low, high = sol[0], sol[NZ - 1]
    for t in range(1, mid):
        z = NZ - 1 - t
        low = sol[t] + coup[t - 1] * low
        high = sol[z] + coup[z + 1] * high
        sol[t], sol[z] = low, high
    high = centre * (high + coup[mid - 1] * low)
    low = inv[mid - 1] * low + coup[mid - 1] * high
    left[mid - 1, :, : 2 * LANES] = jnp.concatenate(halves(low), 1)
    left[mid, :, : 2 * LANES] = jnp.concatenate(halves(high), 1)
    for t in range(mid - 2, -1, -1):
        z = NZ - 1 - t
        low = inv[t] * sol[t] + coup[t] * low
        high = inv[z] * sol[z] + coup[z] * high
        left[t, :, : 2 * LANES] = jnp.concatenate(halves(low), 1)
        left[z, :, : 2 * LANES] = jnp.concatenate(halves(high), 1)
    copies["back"].wait()
    both = dot(left[:NZ, :, : 2 * LANES].reshape(ROWS, 2 * LANES), back_ref[...])
    pres[0] = zero
    pres[NZ + 1] = zero
    pres[1 : NZ + 1] = (both[:, :LANES] + both[:, 2 * LANES : 3 * LANES]).reshape(NZ, R, LANES)
    sol[...] = (both[:, LANES : 2 * LANES] + both[:, 3 * LANES :]).reshape(NZ, R, LANES)

    @pl.loop(0, NZ // 2)
    def _(t):
        z = 2 * t
        here = pl.ds(z, 2)
        u, w = raw[0, pl.ds(z + 1, 2)].astype(F32), raw[1, pl.ds(z + 1, 2)].astype(F32)
        u2 = u1[here] - sol[here]
        w2 = w1[here] - (pres[pl.ds(z + 2, 2)] - pres[here])
        u_out = jnp.where(mask[None], u2, u).astype(BF16)
        w_out = jnp.where(mask[None], w2, w).astype(BF16)
        change = jnp.concatenate(halves(u2 - u), 2)
        fresh[here] = u_out
        fresh[pl.ds(NZ + z, 2)] = w_out
        cells[2, here] = change

    for f in range(3):
        block = dot(cells[f].reshape(ROWS, 2 * LANES), gather_ref[...])
        means[f, :NZ] = block.reshape(NZ, R, LANES)
    lane_high = lane < COLS

    @pl.loop(0, NZ // 2)
    def _(t):
        here = pl.ds(2 * t, 2)
        values = []
        for f in range(3):
            value = jnp.where(own[None], means[f, here], 0.0)
            high = value.astype(BF16).astype(F32)
            values.append(jnp.where(lane_high[None], high, value - high).astype(BF16))
        left[here, :, : 3 * LANES] = jnp.concatenate(values, 2)

    copies["tally"].wait()
    sums = dot(tally_ref[...], left[:NZ, :, : 3 * LANES].reshape(ROWS, 3 * LANES))
    sums = jnp.concatenate([sums[:, LANES * f : LANES * f + LANES] for f in range(3)], 0)
    t_high, t_low = halves(jnp.where(keep > 0.5, sums, 0.0).T)
    copies["fall"].wait()
    tend = dot(t_high, fall_ref[0]) + dot(t_low, fall_ref[0]) + dot(t_high, fall_ref[1])
    tend_ref[...] = (tend[:COLS] + tend[COLS:]).astype(BF16)
    half = COLS // 2
    halos = [
        pltpu.make_async_remote_copy(
            src_ref=tend_ref.at[part], dst_ref=slot, send_sem=halo_send.at[n], recv_sem=halo_recv.at[n],
            device_id=other, device_id_type=MESH,
        )
        for n, (part, slot, other) in enumerate(
            ((pl.ds(half, half), from_left, next_device), (pl.ds(0, half), from_right, left_device))
        )
    ]
    for halo in halos:
        halo.start()

    for relay in relays:
        relay.wait_recv()

    def pass_up(i):
        give(from_lower.at[i], lax.rem(span + spans - reach, spans), i + 1)

    def pass_on(i, _):
        pass_up(reach - 1 - i)
        give(from_upper.at[i], lax.rem(span + reach, spans), spans - reach + 1 + i)
        return _

    lax.fori_loop(0, reach - 1, pass_on, 0)
    pass_up(0)

    for k in range(8):
        give_back(k)

    copies["nbr_elem"].wait()
    copies["nbr_side"].wait()
    elems = COLS // 4
    cell = lax.broadcasted_iota(jnp.int32, (2 * COLS, elems), 0)
    elem, corner = cell >> 2, cell & 3
    c_low, c_high = corner & 1, corner >> 1
    home = lax.broadcasted_iota(jnp.int32, (2 * COLS, elems), 1) + elems // 2
    faces = (1 - c_high, c_low, c_high, 1 - c_low)
    everyone = total * elems
    picks = []
    for side in range(4):
        near = nbr_elem_ref[side : side + 1, :] - (me * elems - elems // 2)
        near = jnp.where(near < 0, near + everyone, near)
        near = jnp.where(near >= everyone, near - everyone, near)
        theirs = nbr_side_ref[side : side + 1, :]
        face = jnp.where(
            theirs < 2, jnp.where(theirs == 0, faces[0], faces[1]), jnp.where(theirs == 2, faces[2], faces[3])
        )
        pick = jnp.where(near == elem, face, 0) + jnp.where(home == elem, faces[side], 0)
        picks.append((0.5 * pick.astype(F32)).T.astype(BF16))

    for halo in halos:
        halo.wait()
    table = jnp.concatenate([from_left[...], tend_ref[...], from_right[...]], 0)
    for side in range(4):
        edge_ref[:, side, :] = dot(picks[side], table)
    for relay in relays:
        relay.wait_send()

    others = pl.ds(0, spans - 1)
    mine.wait()
    pltpu.make_async_copy(got.at[others], got.at[others], recv_sem).wait()
    pltpu.make_async_copy(sent.at[others], sent.at[others], send_sem).wait()


def crm_call(shape, column_state, crm_fields, active, density, span_map, nbr_elem, nbr_side):
    constants = [jnp.asarray(a) for a in tables()]
    operands = (column_state, crm_fields, active, density, span_map, nbr_elem.T, nbr_side.T, *constants)
    hbm = pl.BlockSpec(memory_space=pltpu.HBM)
    levels = (NZ, R, LANES)
    spans = shape[1]
    return pl.pallas_call(
        functools.partial(crm_kernel, shape),
        out_shape=(
            jax.ShapeDtypeStruct((COLS, 4 * LEV), BF16),
            jax.ShapeDtypeStruct((COLS, 3 * NZ * NX), BF16),
            jax.ShapeDtypeStruct((spans, 1, LANES), F32),
            jax.ShapeDtypeStruct((COLS // 4, 4, 4 * LEV), F32),
        ),
        in_specs=[hbm] * (7 + len(constants)),
        out_specs=(pl.BlockSpec(memory_space=pltpu.VMEM),) * 4,
        scratch_shapes=[
            pltpu.VMEM((COLS, 4 * LEV), BF16),
            pltpu.VMEM((COLS, 3 * NZ * NX), BF16),
            pltpu.VMEM((COLS,), jnp.int32),
            pltpu.SMEM((NZ,), F32),
            pltpu.VMEM((COLS,), jnp.int32),
            pltpu.VMEM((4, COLS // 4), jnp.int32),
            pltpu.VMEM((4, COLS // 4), jnp.int32),
            *[pltpu.VMEM(a.shape, a.dtype) for a in constants],
            pltpu.VMEM((3, NZ + 2, R, LANES), BF16),
            pltpu.VMEM((3, NZ, R, 2 * LANES), F32),
            pltpu.VMEM((192, LANES), F32),
            pltpu.VMEM((192, R, LANES), BF16),
            pltpu.VMEM(levels, F32),
            pltpu.VMEM(levels, F32),
            pltpu.VMEM(levels, F32),
            pltpu.VMEM(levels, F32),
            pltpu.VMEM((NZ + 1, R, 4 * LANES), BF16),
            pltpu.VMEM(levels, F32),
            pltpu.VMEM((3, NZ, R, 2 * LANES), BF16),
            pltpu.VMEM((NZ + 2, R, LANES), F32),
            pltpu.VMEM((3, 64, R, LANES), F32),
            pltpu.VMEM((3 * NZ, R, LANES), BF16),
            pltpu.VMEM((COLS // 2, 4 * LEV), BF16),
            pltpu.VMEM((COLS // 2, 4 * LEV), BF16),
            pltpu.VMEM((spans, 1, LANES), F32),
            pltpu.VMEM((spans // 4, 1, LANES), F32),
            pltpu.VMEM((spans // 4 - 1, 1, LANES), F32),
            pltpu.SemaphoreType.DMA((15,)),
            pltpu.SemaphoreType.DMA((CHUNKS,)),
            pltpu.SemaphoreType.DMA,
            pltpu.SemaphoreType.DMA,
            pltpu.SemaphoreType.DMA,
            pltpu.SemaphoreType.DMA((2,)),
            pltpu.SemaphoreType.DMA((2,)),
            pltpu.SemaphoreType.DMA((2,)),
            pltpu.SemaphoreType.DMA((2,)),
        ],
        compiler_params=pltpu.CompilerParams(
            collective_id=0, has_side_effects=True, vmem_limit_bytes=40 * 2**20
        ),
    )(*[pltpu.with_memory_space_constraint(a, pltpu.HBM) for a in operands])


def finish_kernel(tend, fresh, got, edge, tend_out, fresh_out, rows_out, edge_out, flat, rows_ref, went):
    pieces = [(tend, tend_out), (edge, edge_out)]
    for top in range(0, COLS, R):
        cut = pl.ds(top, R)
        pieces.append((fresh.at[cut], fresh_out.at[cut]))
    outward = [pltpu.make_async_copy(a, b, went.at[n]) for n, (a, b) in enumerate(pieces)]
    for copy in outward:
        copy.start()

    spans = got.shape[0]
    for i in range(spans):
        flat[i : i + 1] = got[i]
    table = flat[...]
    lower = lax.broadcasted_iota(jnp.int32, (spans, spans), 0) > lax.broadcasted_iota(jnp.int32, (spans, spans), 1)
    start = dot(jnp.where(lower, 1.0, 0.0).astype(BF16), table.astype(BF16))
    one, two = pltpu.roll(table, LANES - 32, 1), pltpu.roll(table, LANES - 64, 1)
    slot = lax.broadcasted_iota(jnp.int32, (spans, LANES), 1).astype(F32)
    rows = jnp.where((start == slot) & (table > 0.5), one, 0.0)
    rows += jnp.where((start + 1.0 == slot) & (table > 1.5), two, 0.0)
    rows_ref[...] = jnp.sum(rows, 0, keepdims=True)[:, : rows_ref.shape[1]]
    last = pltpu.make_async_copy(rows_ref, rows_out, went.at[len(pieces)])
    last.start()
    for copy in outward:
        copy.wait()
    last.wait()


def finish(slots, tendency, fresh, got, edges):
    hbm, vmem = pl.BlockSpec(memory_space=pltpu.HBM), pl.BlockSpec(memory_space=pltpu.VMEM)
    shapes = [jax.ShapeDtypeStruct(a.shape, a.dtype) for a in (tendency, fresh, got, edges)]
    shapes[2] = jax.ShapeDtypeStruct((1, slots), F32)
    return pl.pallas_call(
        finish_kernel,
        out_shape=tuple(shapes),
        in_specs=[vmem] * 4,
        out_specs=(hbm,) * 4,
        scratch_shapes=[
            pltpu.VMEM((got.shape[0], LANES), F32),
            pltpu.VMEM((1, slots), F32),
            pltpu.SemaphoreType.DMA((7,)),
        ],
        compiler_params=pltpu.CompilerParams(vmem_limit_bytes=16 * 2**20),
    )(tendency, fresh, got, edges)


def body(shape, column_state, crm_fields, span_map, active, density, nbr_elem, nbr_side):
    results = crm_call(
        shape, column_state, crm_fields, active, density, span_map, nbr_elem, nbr_side
    )
    tendency, fresh, rows, edge_sums = finish(COLS * 3 // 8, *results)
    return (tendency, fresh, rows[0], edge_sums)


def solution(mesh):
    rows = P(("region", "span"), None)
    line = P(("region", "span"))
    return jax.shard_map(
        functools.partial(body, (mesh.shape["region"], mesh.shape["span"])),
        mesh=mesh,
        in_specs=(rows, rows, line, line, P(), rows, rows),
        out_specs=(rows, rows, line, P(("region", "span"), None, None)),
        check_vma=False,
    )
```

```python
import functools

import jax
import jax.numpy as jnp
import ml_dtypes
import numpy as np
from jax import lax
from jax.experimental import pallas as pl
from jax.experimental.pallas import tpu as pltpu
from jax.sharding import PartitionSpec as P

MESH = pl.DeviceIdType.MESH
LEV, NZ, NX, COLS = 72, 58, 32, 64
G, R, LANES = 4, 16, 128
ROWS = NZ * R
WIDE, CHUNKS = 512, 11
F32, BF16 = jnp.float32, jnp.bfloat16


def split(a):
    high = a.astype(ml_dtypes.bfloat16)
    return high, (a - high.astype(np.float64)).astype(ml_dtypes.bfloat16)


def level_map(count_to, count_from):
    index = np.arange(count_to)
    numerator = (2 * index + 1) * count_from - count_to
    lower = np.clip(numerator // (2 * count_to), 0, count_from - 2)
    fraction = np.clip((numerator - lower * 2 * count_to) / (2 * count_to), 0.0, 1.0)
    target = np.arange(count_from)[None, :]
    return (1 - fraction)[:, None] * (target == lower[:, None]) + fraction[:, None] * (
        target == lower[:, None] + 1
    )


@functools.cache
def tables():
    eye = np.eye(G)
    step = 0.5 * (np.roll(np.eye(NX), 1, 0) - np.roll(np.eye(NX), -1, 0))
    dxm = np.concatenate(
        [np.kron(eye, 0.25 * step), np.kron(eye, np.full((NX, NX), 0.25 / NX))], 1
    ).astype(ml_dtypes.bfloat16)
    mode = np.arange(NX)
    wave = np.where(mode <= NX // 2, mode, mode - NX // 2)
    phase = 2 * np.pi * (wave[:, None] * np.arange(NX)[None, :] % NX) / NX
    norm = np.where((mode == 0) | (mode == NX // 2), np.sqrt(1 / NX), np.sqrt(2 / NX))
    four = norm[:, None] * np.where((mode <= NX // 2)[:, None], np.cos(phase), np.sin(phase))
    eigen = np.tile(2 - 2 * np.cos(2 * np.pi * wave / NX), G)[None, :]
    eigen = np.broadcast_to(eigen, (R, LANES)).astype(np.float32)

    def doubled(a):
        return np.concatenate(split(a), 1)

    to_mode = -four.T
    forward = np.concatenate(
        [doubled(np.kron(eye, a)) for a in (step @ to_mode, step @ to_mode, to_mode, to_mode)], 0
    )
    back = np.concatenate([np.kron(eye, 0.5 * four), np.kron(eye, four @ step)], 1)
    back = np.concatenate([doubled(back)] * 2, 0)
    up = level_map(NZ, LEV)
    zero = np.zeros_like(up)
    blocks = [
        [0.3 * up, zero, zero, zero],
        [zero, 0.25 * up, zero, 0.25 * up],
        [zero, zero, 0.25 * up, zero],
    ]
    rise = np.zeros((192, 4 * LEV))
    for i, row in enumerate(blocks):
        rise[64 * i : 64 * i + NZ] = np.concatenate(row, 1)
    rise = np.stack(split(rise))
    column, lane = np.arange(LANES) % COLS, np.arange(LANES)
    spread = (column[:, None] // R == lane[None, :] // NX).astype(ml_dtypes.bfloat16)
    gather = (lane[:, None] // NX == column[None, :] // R) / NX
    gather = np.concatenate([gather, gather], 0).astype(ml_dtypes.bfloat16)
    tally = np.zeros((64, ROWS))
    for z in range(NZ):
        tally[z, R * z : R * z + R] = 1
    tally = tally.astype(ml_dtypes.bfloat16)
    down = level_map(LEV, NZ)
    fall = np.zeros((4 * LEV, 192))
    for f, (source, gain) in enumerate(((0, 2.0), (1, 4.0), (2, 4.0), (0, 0.5))):
        fall[LEV * f : LEV * f + LEV, 64 * source : 64 * source + NZ] = gain * down
    fall = np.stack(split(fall.T))
    return dxm, forward, back, eigen, rise, spread, gather, tally, fall


def dot(a, b, dims=((1,), (0,)), precision=None):
    return lax.dot_general(a, b, (dims, ((), ())), precision=precision, preferred_element_type=F32)


def halves(a):
    high = a.astype(BF16)
    return high, (a - high.astype(F32)).astype(BF16)


def regroup(parts):
    lane = lax.broadcasted_iota(jnp.int32, (R, LANES), 1)
    low, even = lane < 64, (lane & 32) == 0
    a, b, c, d = parts
    a, c = jnp.where(low, a, pltpu.roll(c, 64, 1)), jnp.where(low, pltpu.roll(a, 64, 1), c)
    b, d = jnp.where(low, b, pltpu.roll(d, 64, 1)), jnp.where(low, pltpu.roll(b, 64, 1), d)
    a, b = jnp.where(even, a, pltpu.roll(b, 32, 1)), jnp.where(even, pltpu.roll(a, 96, 1), b)
    c, d = jnp.where(even, c, pltpu.roll(d, 32, 1)), jnp.where(even, pltpu.roll(c, 96, 1), d)
    return a, b, c, d


def crm_kernel(
    shape,
    state_hbm, fields_hbm, active_hbm, density_hbm, span_map_hbm, nbr_elem_hbm, nbr_side_hbm,
    dxm_hbm, forward_hbm, back_hbm, eigen_hbm, rise_hbm, spread_hbm, gather_hbm, tally_hbm, fall_hbm,
    tend_ref, fresh_ref, got, edge_ref,
    state_ref, fields_ref, active_ref, density_ref, span_map_ref, nbr_elem_ref, nbr_side_ref,
    dxm_ref, forward_ref, back_ref, eigen_ref, rise_ref, spread_ref, gather_ref, tally_ref, fall_ref,
    raw, dxm, prof_wide, prof_rows, inv, coup, u1, w1, left, sol, cells, pres, means, fresh,
    from_left, from_right, sent, from_lower, from_upper,
    in_sem, field_sem, out_sem, send_sem, recv_sem, pass_sem, halo_send, halo_recv, relay_send, relay_recv,
):
    regions, spans = shape
    reach = spans // 4
    region, span = lax.axis_index("region"), lax.axis_index("span")
    me = region * spans + span
    total = regions * spans
    next_device, left_device = lax.rem(me + 1, total), lax.rem(me + total - 1, total)
    next_device = (lax.div(next_device, spans), lax.rem(next_device, spans))
    left_device = (lax.div(left_device, spans), lax.rem(left_device, spans))

    parity = lax.rem(region, 2)
    lead = region + 1 - parity

    def along(offset, where=region):
        return (where, lax.rem(span + offset, spans))

    barrier = pltpu.get_barrier_semaphore()

    def greet(i, _):
        for offset in (reach - i, spans - reach + i):
            pl.semaphore_signal(barrier, inc=1, device_id=along(offset), device_id_type=MESH)
        return _

    def greet_lead(i, _):
        for offset in (reach - i, spans - reach + i):
            pl.semaphore_signal(barrier, inc=1, device_id=along(offset, lead), device_id_type=MESH)
        return _

    @pl.when(parity == 0)
    def _():
        lax.fori_loop(0, reach, greet_lead, 0)

    @pl.when(parity == 1)
    def _():
        for offset in (reach, spans - reach):
            pl.semaphore_signal(
                barrier, inc=1, device_id=along(offset, region - 1), device_id_type=MESH
            )

    lax.fori_loop(0, reach, greet, 0)
    for other in (left_device, next_device):
        pl.semaphore_signal(barrier, inc=1, device_id=other, device_id_type=MESH)

    copies = {}
    pairs = dict(
        state=(state_hbm, state_ref), rise=(rise_hbm, rise_ref), active=(active_hbm, active_ref),
        spread=(spread_hbm, spread_ref), dxm=(dxm_hbm, dxm_ref), density=(density_hbm, density_ref),
        eigen=(eigen_hbm, eigen_ref), forward=(forward_hbm, forward_ref), back=(back_hbm, back_ref),
        gather=(gather_hbm, gather_ref), tally=(tally_hbm, tally_ref), fall=(fall_hbm, fall_ref),
        span_map=(span_map_hbm, span_map_ref), nbr_elem=(nbr_elem_hbm, nbr_elem_ref),
        nbr_side=(nbr_side_hbm, nbr_side_ref),
    )
    for n, (name, (source, target)) in enumerate(pairs.items()):
        copies[name] = pltpu.make_async_copy(source, target, in_sem.at[n])
        if n == 6:
            for k in range(CHUNKS):
                cut = slice(WIDE * k, min(WIDE * k + WIDE, NZ * NX * 3))
                copies[k] = pltpu.make_async_copy(
                    fields_hbm.at[:, cut], fields_ref.at[:, cut], field_sem.at[k]
                )
                copies[k].start()
        copies[name].start()

    lane = lax.broadcasted_iota(jnp.int32, (R, LANES), 1)
    row = lax.broadcasted_iota(jnp.int32, (R, LANES), 0)
    own = (lane & (R - 1)) == row
    zero16 = jnp.zeros((R, LANES), BF16)

    copies["state"].wait()
    copies["rise"].wait()
    copies["active"].wait()
    state = state_ref[...]
    profile = dot(rise_ref[0], state, ((1,), (1,))) + dot(rise_ref[1], state, ((1,), (1,)))
    flags = active_ref[...].reshape(1, COLS).astype(F32)
    p_high, p_low = halves(jnp.concatenate([jnp.exp(profile[:64]), profile[64:]], 0))
    prof_wide[...] = jnp.concatenate([p_high, p_low], 1).astype(F32)
    keep = jnp.concatenate([flags, flags], 1)
    prof_wide[63:64] = jnp.where(lane[:1] < COLS, keep, 0.0)
    wanted = [64 * f + z for f in range(3) for z in range(NZ)] + [63]
    for k in range(0, len(wanted), 8):
        lines = [prof_wide[i : i + 1] for i in wanted[k : k + 8]]
        lines = [jnp.where(own, jnp.broadcast_to(v, (R, LANES)), 0.0).astype(BF16) for v in lines]
        for i, v in zip(wanted[k : k + 8], lines):
            prof_rows[i] = v
    copies["spread"].wait()
    for f in range(3):
        top = 64 if f == 0 else NZ
        block = dot(prof_rows[64 * f : 64 * f + top].reshape(top * R, LANES), spread_ref[...])
        means[f, :top] = block.reshape(top, R, LANES)
    mask = means[0, 63] > 0.5

    for f in range(3):
        raw[f, 0] = zero16
        raw[f, NZ + 1] = zero16
    for k in range(CHUNKS):
        copies[k].wait()
        blocks = []
        for j in range(4 * k, 4 * k + 4):
            if j < 43:
                tiles = [fields_ref[R * g : R * g + R, LANES * j : LANES * j + LANES] for g in range(G)]
            else:
                tiles = [
                    jnp.concatenate([fields_ref[R * g : R * g + R, LANES * j :], zero16[:, :64]], 1)
                    for g in range(G)
                ]
            blocks.append(regroup(tiles))
        for j, block in enumerate(blocks):
            for part, level in zip(block, range(16 * k + 4 * j, min(16 * k + 4 * j + 4, 3 * NZ))):
                f, z = divmod(level, NZ)
                raw[f, z + 1] = part
    copies["dxm"].wait()
    for f in range(3):
        block = dot(raw[f, 1 : NZ + 1].reshape(ROWS, LANES), dxm_ref[...])
        dxm[f] = block.reshape(NZ, R, 2 * LANES)

    copies["density"].wait()
    copies["eigen"].wait()
    eigen = eigen_ref[...]
    inv[0] = jnp.zeros((R, LANES), F32)
    zero = inv[0]

    def factor(t, last):
        low, high, _ = last
        z = NZ - 1 - t
        rho, above = density_ref[t], density_ref[t + 1]
        below = jnp.where(t > 0, density_ref[jnp.maximum(t - 1, 0)], rho)
        f_up, f_down = 0.5 * (rho + above), 0.5 * (rho + below)
        i_low = 1.0 / ((eigen * rho + (f_up + f_down)) - f_down * low)
        e_low = f_up * i_low
        rho, below = density_ref[z], density_ref[z - 1]
        above = jnp.where(t > 0, density_ref[jnp.minimum(z + 1, NZ - 1)], rho)
        f_up, f_down = 0.5 * (rho + above), 0.5 * (rho + below)
        diag = (eigen * rho + (f_up + f_down)) - f_up * high
        i_high = 1.0 / diag
        e_high = f_down * i_high
        stores = [(inv, t, i_low), (coup, t, e_low), (inv, z, i_high), (coup, z, e_high)]
        return stores, (e_low, e_high, diag)

    def advect(z, carry):
        (u_m, u), (w_m, w), (q_m, q), (rw_mm, rw_m), rain = carry
        u_p, w_p, q_p = [raw[f, z + 2].astype(F32) for f in range(3)]
        rho = density_ref[z]
        half = 0.125 * w
        du, mean_u = dxm[0, z, :, :LANES], dxm[0, z, :, LANES:]
        dw = dxm[1, z, :, :LANES]
        dq, mean_q = dxm[2, z, :, :LANES], dxm[2, z, :, LANES:]
        new_u = u - u * du - half * (u_p - u_m) + (means[2, z] - mean_u)
        new_w = w - u * dw - half * (w_p - w_m) + (0.125 * q - 0.5 * mean_q)
        new_q = q - u * dq - half * (q_p - q_m) + (means[1, z] - mean_q)
        x = new_q - means[0, z]
        cond = jnp.maximum(x, 0.0) + jnp.log(1.0 + jnp.exp(-jnp.abs(x)))
        q2 = new_q - 0.5 * cond
        rw = rho * new_w
        stores = [
            (u1, z, new_u),
            (w1, z, new_w),
            (fresh, 2 * NZ + z, jnp.where(mask, q2, q).astype(BF16)),
            (cells.at[0], z, jnp.concatenate(halves(cond), 1)),
            (cells.at[1], z, jnp.concatenate(halves(q2 - q), 1)),
            (left.at[:, :, : 2 * LANES], z + 1, jnp.concatenate(halves(rho * new_u), 1)),
            (left.at[:, :, 2 * LANES :], z, jnp.concatenate(halves(0.5 * (rw - rw_mm)), 1)),
        ]
        return stores, ((u, u_p), (w, w_p), (q, q_p), (rw_m, rw), rain + rho * cond)

    def both_passes(t, carry):
        stores, last = factor(t, carry[0])
        more, levels = advect(2 * t, carry[1])
        most, levels = advect(2 * t + 1, levels)
        for ref, z, value in stores + more + most:
            ref[z] = value
        return last, levels

    first = tuple((zero, raw[f, 1].astype(F32)) for f in range(3)) + ((zero, zero), zero)
    last, levels = lax.fori_loop(0, NZ // 2, both_passes, ((zero, zero, zero), first))
    left[NZ, :, 2 * LANES :] = jnp.concatenate(halves(-0.5 * levels[3][0]), 1)
    mid = NZ // 2
    centre = 1.0 / (last[2] - 0.5 * (density_ref[mid - 1] + density_ref[mid]) * last[0])

    copies["gather"].wait()
    parts = dot(jnp.concatenate(halves(levels[4] * (2.0 / NZ)), 1), gather_ref[...])
    precip = jnp.sum(jnp.where(own, parts, 0.0), 0, keepdims=True)[:, :COLS]
    copies["span_map"].wait()
    order = lax.broadcasted_iota(jnp.int32, (spans, COLS), 0) + span
    target = jnp.where(order >= spans, order - spans, order)
    hot = jnp.where((span_map_ref[...].reshape(1, COLS) == target) & (flags > 0.5), 1.0, 0.0)
    upper = lax.broadcasted_iota(jnp.int32, (COLS, COLS), 0) < lax.broadcasted_iota(jnp.int32, (COLS, COLS), 1)
    before = dot(hot.astype(BF16), jnp.where(upper, 1.0, 0.0).astype(BF16))
    one = jnp.sum(jnp.where(before < 0.5, hot, 0.0) * precip, 1, keepdims=True)
    two = jnp.sum(jnp.where(before > 0.5, hot, 0.0) * precip, 1, keepdims=True)
    load = jnp.sum(hot, 1, keepdims=True)
    place = lax.broadcasted_iota(jnp.int32, (spans, LANES), 1)
    block = jnp.where(place < 32, load, jnp.where(place < 64, one, two))
    for i in range(spans):
        sent[i] = block[i : i + 1]
    mine = pltpu.make_async_copy(sent.at[0], got.at[span], out_sem)
    mine.start()

    pl.semaphore_wait(barrier, jnp.where(parity == 0, 2 * reach + 4, 4 * reach + 2))
    relays = [
        pltpu.make_async_remote_copy(
            src_ref=sent.at[pl.ds(first_row, count)], dst_ref=slot.at[parity], send_sem=relay_send.at[n],
            recv_sem=relay_recv.at[n, parity], device_id=along(offset, lead), device_id_type=MESH,
        )
        for n, (first_row, count, slot, offset) in enumerate(
            (
                (reach + 1, reach, from_lower, reach),
                (2 * reach + 1, reach - 1, from_upper, spans - reach),
            )
        )
    ]
    for relay in relays:
        relay.start()

    def give(source, slot, offset, sem=send_sem, where=region):
        pltpu.make_async_remote_copy(
            src_ref=source, dst_ref=got.at[slot], send_sem=sem, recv_sem=recv_sem,
            device_id=along(offset, where), device_id_type=MESH,
        ).start()

    def give_near(i, _):
        for offset in (reach - i, spans - reach + i):
            give(sent.at[offset], span, offset)
        return _

    lax.fori_loop(0, reach, give_near, 0)

    def give_back(k):
        blocks = []
        for j in range(4 * k, 4 * k + 4):
            blocks.append(
                regroup([fresh[v] if v < 3 * NZ else zero16 for v in range(4 * j, 4 * j + 4)])
            )
        for j, block in enumerate(blocks):
            j += 4 * k
            for g, part in enumerate(block):
                if j < 43:
                    fresh_ref[R * g : R * g + R, LANES * j : LANES * j + LANES] = part
                else:
                    fresh_ref[R * g : R * g + R, LANES * j :] = part[:, :64]

    for k in range(8, CHUNKS):
        give_back(k)

    copies["forward"].wait()
    right = dot(left[1:].reshape(ROWS, 4 * LANES), forward_ref[...])
    sol[...] = (right[:, :LANES] + right[:, LANES:]).reshape(NZ, R, LANES)
    low, high = sol[0], sol[NZ - 1]
    for t in range(1, mid):
        z = NZ - 1 - t
        low = sol[t] + coup[t - 1] * low
        high = sol[z] + coup[z + 1] * high
        sol[t], sol[z] = low, high
    high = centre * (high + coup[mid - 1] * low)
    low = inv[mid - 1] * low + coup[mid - 1] * high
    left[mid - 1, :, : 2 * LANES] = jnp.concatenate(halves(low), 1)
    left[mid, :, : 2 * LANES] = jnp.concatenate(halves(high), 1)
    for t in range(mid - 2, -1, -1):
        z = NZ - 1 - t
        low = inv[t] * sol[t] + coup[t] * low
        high = inv[z] * sol[z] + coup[z] * high
        left[t, :, : 2 * LANES] = jnp.concatenate(halves(low), 1)
        left[z, :, : 2 * LANES] = jnp.concatenate(halves(high), 1)
    copies["back"].wait()
    both = dot(left[:NZ, :, : 2 * LANES].reshape(ROWS, 2 * LANES), back_ref[...])
    pres[0] = zero
    pres[NZ + 1] = zero
    pres[1 : NZ + 1] = (both[:, :LANES] + both[:, 2 * LANES : 3 * LANES]).reshape(NZ, R, LANES)
    sol[...] = (both[:, LANES : 2 * LANES] + both[:, 3 * LANES :]).reshape(NZ, R, LANES)

    @pl.loop(0, NZ // 2)
    def _(t):
        z = 2 * t
        here = pl.ds(z, 2)
        u, w = raw[0, pl.ds(z + 1, 2)].astype(F32), raw[1, pl.ds(z + 1, 2)].astype(F32)
        u2 = u1[here] - sol[here]
        w2 = w1[here] - (pres[pl.ds(z + 2, 2)] - pres[here])
        u_out = jnp.where(mask[None], u2, u).astype(BF16)
        w_out = jnp.where(mask[None], w2, w).astype(BF16)
        change = jnp.concatenate(halves(u2 - u), 2)
        fresh[here] = u_out
        fresh[pl.ds(NZ + z, 2)] = w_out
        cells[2, here] = change

    for f in range(3):
        block = dot(cells[f].reshape(ROWS, 2 * LANES), gather_ref[...])
        means[f, :NZ] = block.reshape(NZ, R, LANES)
    lane_high = lane < COLS

    @pl.loop(0, NZ // 2)
    def _(t):
        here = pl.ds(2 * t, 2)
        values = []
        for f in range(3):
            value = jnp.where(own[None], means[f, here], 0.0)
            high = value.astype(BF16).astype(F32)
            values.append(jnp.where(lane_high[None], high, value - high).astype(BF16))
        left[here, :, : 3 * LANES] = jnp.concatenate(values, 2)

    copies["tally"].wait()
    sums = dot(tally_ref[...], left[:NZ, :, : 3 * LANES].reshape(ROWS, 3 * LANES))
    sums = jnp.concatenate([sums[:, LANES * f : LANES * f + LANES] for f in range(3)], 0)
    t_high, t_low = halves(jnp.where(keep > 0.5, sums, 0.0).T)
    copies["fall"].wait()
    tend = dot(t_high, fall_ref[0]) + dot(t_low, fall_ref[0]) + dot(t_high, fall_ref[1])
    tend_ref[...] = (tend[:COLS] + tend[COLS:]).astype(BF16)
    half = COLS // 2
    halos = [
        pltpu.make_async_remote_copy(
            src_ref=tend_ref.at[part], dst_ref=slot, send_sem=halo_send.at[n], recv_sem=halo_recv.at[n],
            device_id=other, device_id_type=MESH,
        )
        for n, (part, slot, other) in enumerate(
            ((pl.ds(half, half), from_left, next_device), (pl.ds(0, half), from_right, left_device))
        )
    ]
    for halo in halos:
        halo.start()

    passed = pl.ds(0, 4 * reach - 2)

    @pl.when(parity == 1)
    def _():
        for n, slot in enumerate((from_lower, from_upper)):
            for p in range(2):
                pltpu.make_async_copy(slot.at[p], slot.at[p], relay_recv.at[n, p]).wait()
        below, above = lax.rem(span + spans - reach, spans), lax.rem(span + reach, spans)

        def pass_up(i):
            for p in range(2):
                give(from_lower.at[p, i], below, i + 1, pass_sem, region - 1 + p)

        def pass_on(i, _):
            pass_up(reach - 1 - i)
            for p in range(2):
                give(from_upper.at[p, i], above, spans - reach + 1 + i, pass_sem, region - 1 + p)
            return _

        lax.fori_loop(0, reach - 1, pass_on, 0)
        pass_up(0)

    for k in range(8):
        give_back(k)

    copies["nbr_elem"].wait()
    copies["nbr_side"].wait()
    elems = COLS // 4
    cell = lax.broadcasted_iota(jnp.int32, (2 * COLS, elems), 0)
    elem, corner = cell >> 2, cell & 3
    c_low, c_high = corner & 1, corner >> 1
    home = lax.broadcasted_iota(jnp.int32, (2 * COLS, elems), 1) + elems // 2
    faces = (1 - c_high, c_low, c_high, 1 - c_low)
    everyone = total * elems
    picks = []
    for side in range(4):
        near = nbr_elem_ref[side : side + 1, :] - (me * elems - elems // 2)
        near = jnp.where(near < 0, near + everyone, near)
        near = jnp.where(near >= everyone, near - everyone, near)
        theirs = nbr_side_ref[side : side + 1, :]
        face = jnp.where(
            theirs < 2, jnp.where(theirs == 0, faces[0], faces[1]), jnp.where(theirs == 2, faces[2], faces[3])
        )
        pick = jnp.where(near == elem, face, 0) + jnp.where(home == elem, faces[side], 0)
        picks.append((0.5 * pick.astype(F32)).T.astype(BF16))

    for halo in halos:
        halo.wait()
    table = jnp.concatenate([from_left[...], tend_ref[...], from_right[...]], 0)
    for side in range(4):
        edge_ref[:, side, :] = dot(picks[side], table)
    for relay in relays:
        relay.wait_send()

    others = pl.ds(0, spans - 1)
    mine.wait()
    pltpu.make_async_copy(got.at[others], got.at[others], recv_sem).wait()
    near = pl.ds(0, 2 * reach)
    pltpu.make_async_copy(sent.at[near], sent.at[near], send_sem).wait()

    @pl.when(parity == 1)
    def _():
        pltpu.make_async_copy(sent.at[passed], sent.at[passed], pass_sem).wait()


def crm_call(shape, column_state, crm_fields, active, density, span_map, nbr_elem, nbr_side):
    constants = [jnp.asarray(a) for a in tables()]
    operands = (column_state, crm_fields, active, density, span_map, nbr_elem.T, nbr_side.T, *constants)
    hbm = pl.BlockSpec(memory_space=pltpu.HBM)
    levels = (NZ, R, LANES)
    spans = shape[1]
    return pl.pallas_call(
        functools.partial(crm_kernel, shape),
        out_shape=(
            jax.ShapeDtypeStruct((COLS, 4 * LEV), BF16),
            jax.ShapeDtypeStruct((COLS, 3 * NZ * NX), BF16),
            jax.ShapeDtypeStruct((spans, 1, LANES), F32),
            jax.ShapeDtypeStruct((COLS // 4, 4, 4 * LEV), F32),
        ),
        in_specs=[hbm] * (7 + len(constants)),
        out_specs=(pl.BlockSpec(memory_space=pltpu.VMEM),) * 4,
        scratch_shapes=[
            pltpu.VMEM((COLS, 4 * LEV), BF16),
            pltpu.VMEM((COLS, 3 * NZ * NX), BF16),
            pltpu.VMEM((COLS,), jnp.int32),
            pltpu.SMEM((NZ,), F32),
            pltpu.VMEM((COLS,), jnp.int32),
            pltpu.VMEM((4, COLS // 4), jnp.int32),
            pltpu.VMEM((4, COLS // 4), jnp.int32),
            *[pltpu.VMEM(a.shape, a.dtype) for a in constants],
            pltpu.VMEM((3, NZ + 2, R, LANES), BF16),
            pltpu.VMEM((3, NZ, R, 2 * LANES), F32),
            pltpu.VMEM((192, LANES), F32),
            pltpu.VMEM((192, R, LANES), BF16),
            pltpu.VMEM(levels, F32),
            pltpu.VMEM(levels, F32),
            pltpu.VMEM(levels, F32),
            pltpu.VMEM(levels, F32),
            pltpu.VMEM((NZ + 1, R, 4 * LANES), BF16),
            pltpu.VMEM(levels, F32),
            pltpu.VMEM((3, NZ, R, 2 * LANES), BF16),
            pltpu.VMEM((NZ + 2, R, LANES), F32),
            pltpu.VMEM((3, 64, R, LANES), F32),
            pltpu.VMEM((3 * NZ, R, LANES), BF16),
            pltpu.VMEM((COLS // 2, 4 * LEV), BF16),
            pltpu.VMEM((COLS // 2, 4 * LEV), BF16),
            pltpu.VMEM((spans, 1, LANES), F32),
            pltpu.VMEM((2, spans // 4, 1, LANES), F32),
            pltpu.VMEM((2, spans // 4 - 1, 1, LANES), F32),
            pltpu.SemaphoreType.DMA((15,)),
            pltpu.SemaphoreType.DMA((CHUNKS,)),
            pltpu.SemaphoreType.DMA,
            pltpu.SemaphoreType.DMA,
            pltpu.SemaphoreType.DMA,
            pltpu.SemaphoreType.DMA,
            pltpu.SemaphoreType.DMA((2,)),
            pltpu.SemaphoreType.DMA((2,)),
            pltpu.SemaphoreType.DMA((2,)),
            pltpu.SemaphoreType.DMA((2, 2)),
        ],
        compiler_params=pltpu.CompilerParams(
            collective_id=0, has_side_effects=True, vmem_limit_bytes=40 * 2**20
        ),
    )(*[pltpu.with_memory_space_constraint(a, pltpu.HBM) for a in operands])


def finish_kernel(tend, fresh, got, edge, tend_out, fresh_out, rows_out, edge_out, flat, rows_ref, went):
    pieces = [(tend, tend_out), (edge, edge_out)]
    for top in range(0, COLS, R):
        cut = pl.ds(top, R)
        pieces.append((fresh.at[cut], fresh_out.at[cut]))
    outward = [pltpu.make_async_copy(a, b, went.at[n]) for n, (a, b) in enumerate(pieces)]
    for copy in outward:
        copy.start()

    spans = got.shape[0]
    for i in range(spans):
        flat[i : i + 1] = got[i]
    table = flat[...]
    lower = lax.broadcasted_iota(jnp.int32, (spans, spans), 0) > lax.broadcasted_iota(jnp.int32, (spans, spans), 1)
    start = dot(jnp.where(lower, 1.0, 0.0).astype(BF16), table.astype(BF16))
    one, two = pltpu.roll(table, LANES - 32, 1), pltpu.roll(table, LANES - 64, 1)
    slot = lax.broadcasted_iota(jnp.int32, (spans, LANES), 1).astype(F32)
    rows = jnp.where((start == slot) & (table > 0.5), one, 0.0)
    rows += jnp.where((start + 1.0 == slot) & (table > 1.5), two, 0.0)
    rows_ref[...] = jnp.sum(rows, 0, keepdims=True)[:, : rows_ref.shape[1]]
    last = pltpu.make_async_copy(rows_ref, rows_out, went.at[len(pieces)])
    last.start()
    for copy in outward:
        copy.wait()
    last.wait()


def finish(slots, tendency, fresh, got, edges):
    hbm, vmem = pl.BlockSpec(memory_space=pltpu.HBM), pl.BlockSpec(memory_space=pltpu.VMEM)
    shapes = [jax.ShapeDtypeStruct(a.shape, a.dtype) for a in (tendency, fresh, got, edges)]
    shapes[2] = jax.ShapeDtypeStruct((1, slots), F32)
    return pl.pallas_call(
        finish_kernel,
        out_shape=tuple(shapes),
        in_specs=[vmem] * 4,
        out_specs=(hbm,) * 4,
        scratch_shapes=[
            pltpu.VMEM((got.shape[0], LANES), F32),
            pltpu.VMEM((1, slots), F32),
            pltpu.SemaphoreType.DMA((7,)),
        ],
        compiler_params=pltpu.CompilerParams(vmem_limit_bytes=16 * 2**20),
    )(tendency, fresh, got, edges)


def body(shape, column_state, crm_fields, span_map, active, density, nbr_elem, nbr_side):
    results = crm_call(
        shape, column_state, crm_fields, active, density, span_map, nbr_elem, nbr_side
    )
    tendency, fresh, rows, edge_sums = finish(COLS * 3 // 8, *results)
    return (tendency, fresh, rows[0], edge_sums)


def solution(mesh):
    rows = P(("region", "span"), None)
    line = P(("region", "span"))
    return jax.shard_map(
        functools.partial(body, (mesh.shape["region"], mesh.shape["span"])),
        mesh=mesh,
        in_specs=(rows, rows, line, line, P(), rows, rows),
        out_specs=(rows, rows, line, P(("region", "span"), None, None)),
        check_vma=False,
    )
```

```python
import functools

import jax
import jax.numpy as jnp
import ml_dtypes
import numpy as np
from jax import lax
from jax.experimental import pallas as pl
from jax.experimental.pallas import tpu as pltpu
from jax.sharding import PartitionSpec as P

MESH = pl.DeviceIdType.MESH
LEV, NZ, NX, COLS = 72, 58, 32, 64
G, R, LANES = 4, 16, 128
ROWS = NZ * R
WIDE, CHUNKS = 512, 11
F32, BF16 = jnp.float32, jnp.bfloat16


def split(a):
    high = a.astype(ml_dtypes.bfloat16)
    return high, (a - high.astype(np.float64)).astype(ml_dtypes.bfloat16)


def level_map(count_to, count_from):
    index = np.arange(count_to)
    numerator = (2 * index + 1) * count_from - count_to
    lower = np.clip(numerator // (2 * count_to), 0, count_from - 2)
    fraction = np.clip((numerator - lower * 2 * count_to) / (2 * count_to), 0.0, 1.0)
    target = np.arange(count_from)[None, :]
    return (1 - fraction)[:, None] * (target == lower[:, None]) + fraction[:, None] * (
        target == lower[:, None] + 1
    )


@functools.cache
def tables():
    eye = np.eye(G)
    step = 0.5 * (np.roll(np.eye(NX), 1, 0) - np.roll(np.eye(NX), -1, 0))
    dxm = np.concatenate(
        [np.kron(eye, 0.25 * step), np.kron(eye, np.full((NX, NX), 0.25 / NX))], 1
    ).astype(ml_dtypes.bfloat16)
    mode = np.arange(NX)
    wave = np.where(mode <= NX // 2, mode, mode - NX // 2)
    phase = 2 * np.pi * (wave[:, None] * np.arange(NX)[None, :] % NX) / NX
    norm = np.where((mode == 0) | (mode == NX // 2), np.sqrt(1 / NX), np.sqrt(2 / NX))
    four = norm[:, None] * np.where((mode <= NX // 2)[:, None], np.cos(phase), np.sin(phase))
    eigen = np.tile(2 - 2 * np.cos(2 * np.pi * wave / NX), G)[None, :]
    eigen = np.broadcast_to(eigen, (R, LANES)).astype(np.float32)

    def doubled(a):
        return np.concatenate(split(a), 1)

    to_mode = -four.T
    forward = np.concatenate(
        [doubled(np.kron(eye, a)) for a in (step @ to_mode, step @ to_mode, to_mode, to_mode)], 0
    )
    back = np.concatenate([np.kron(eye, 0.5 * four), np.kron(eye, four @ step)], 1)
    back = np.concatenate([doubled(back)] * 2, 0)
    up = level_map(NZ, LEV)
    zero = np.zeros_like(up)
    blocks = [
        [0.3 * up, zero, zero, zero],
        [zero, 0.25 * up, zero, 0.25 * up],
        [zero, zero, 0.25 * up, zero],
    ]
    rise = np.zeros((192, 4 * LEV))
    for i, row in enumerate(blocks):
        rise[64 * i : 64 * i + NZ] = np.concatenate(row, 1)
    rise = np.stack(split(rise))
    column, lane = np.arange(LANES) % COLS, np.arange(LANES)
    spread = (column[:, None] // R == lane[None, :] // NX).astype(ml_dtypes.bfloat16)
    gather = (lane[:, None] // NX == column[None, :] // R) / NX
    gather = np.concatenate([gather, gather], 0).astype(ml_dtypes.bfloat16)
    tally = np.zeros((64, ROWS))
    for z in range(NZ):
        tally[z, R * z : R * z + R] = 1
    tally = tally.astype(ml_dtypes.bfloat16)
    down = level_map(LEV, NZ)
    fall = np.zeros((4 * LEV, 192))
    for f, (source, gain) in enumerate(((0, 2.0), (1, 4.0), (2, 4.0), (0, 0.5))):
        fall[LEV * f : LEV * f + LEV, 64 * source : 64 * source + NZ] = gain * down
    fall = np.stack(split(fall.T))
    return dxm, forward, back, eigen, rise, spread, gather, tally, fall


def dot(a, b, dims=((1,), (0,)), precision=None):
    return lax.dot_general(a, b, (dims, ((), ())), precision=precision, preferred_element_type=F32)


def halves(a):
    high = a.astype(BF16)
    return high, (a - high.astype(F32)).astype(BF16)


def regroup(parts):
    lane = lax.broadcasted_iota(jnp.int32, (R, LANES), 1)
    low, even = lane < 64, (lane & 32) == 0
    a, b, c, d = parts
    a, c = jnp.where(low, a, pltpu.roll(c, 64, 1)), jnp.where(low, pltpu.roll(a, 64, 1), c)
    b, d = jnp.where(low, b, pltpu.roll(d, 64, 1)), jnp.where(low, pltpu.roll(b, 64, 1), d)
    a, b = jnp.where(even, a, pltpu.roll(b, 32, 1)), jnp.where(even, pltpu.roll(a, 96, 1), b)
    c, d = jnp.where(even, c, pltpu.roll(d, 32, 1)), jnp.where(even, pltpu.roll(c, 96, 1), d)
    return a, b, c, d


def crm_kernel(
    shape,
    state_hbm, fields_hbm, active_hbm, density_hbm, span_map_hbm, nbr_elem_hbm, nbr_side_hbm,
    dxm_hbm, forward_hbm, back_hbm, eigen_hbm, rise_hbm, spread_hbm, gather_hbm, tally_hbm, fall_hbm,
    tend_ref, fresh_ref, got, edge_ref,
    state_ref, fields_ref, active_ref, density_ref, span_map_ref, nbr_elem_ref, nbr_side_ref,
    dxm_ref, forward_ref, back_ref, eigen_ref, rise_ref, spread_ref, gather_ref, tally_ref, fall_ref,
    raw, dxm, prof_wide, prof_rows, inv, coup, u1, w1, left, sol, cells, pres, means, fresh,
    from_left, from_right, sent, from_lower, from_upper,
    in_sem, field_sem, out_sem, send_sem, recv_sem, pass_sem, halo_send, halo_recv, relay_send, relay_recv,
):
    regions, spans = shape
    reach = spans // 4
    region, span = lax.axis_index("region"), lax.axis_index("span")
    me = region * spans + span
    total = regions * spans
    next_device, left_device = lax.rem(me + 1, total), lax.rem(me + total - 1, total)
    next_device = (lax.div(next_device, spans), lax.rem(next_device, spans))
    left_device = (lax.div(left_device, spans), lax.rem(left_device, spans))

    parity = lax.rem(region, 2)
    lead = region + 1 - parity

    def along(offset, where=region):
        return (where, lax.rem(span + offset, spans))

    barrier = pltpu.get_barrier_semaphore()

    def greet(i, _):
        for offset in (reach - i, spans - reach + i):
            pl.semaphore_signal(barrier, inc=1, device_id=along(offset), device_id_type=MESH)
        return _

    def greet_lead(i, _):
        for offset in (reach - i, spans - reach + i):
            pl.semaphore_signal(barrier, inc=1, device_id=along(offset, lead), device_id_type=MESH)
        return _

    @pl.when(parity == 0)
    def _():
        lax.fori_loop(0, reach, greet_lead, 0)

    @pl.when(parity == 1)
    def _():
        for offset in (reach, spans - reach):
            pl.semaphore_signal(
                barrier, inc=1, device_id=along(offset, region - 1), device_id_type=MESH
            )

    lax.fori_loop(0, reach, greet, 0)
    for other in (left_device, next_device):
        pl.semaphore_signal(barrier, inc=1, device_id=other, device_id_type=MESH)

    copies = {}
    pairs = dict(
        state=(state_hbm, state_ref), rise=(rise_hbm, rise_ref), active=(active_hbm, active_ref),
        spread=(spread_hbm, spread_ref), dxm=(dxm_hbm, dxm_ref), density=(density_hbm, density_ref),
        eigen=(eigen_hbm, eigen_ref), forward=(forward_hbm, forward_ref), back=(back_hbm, back_ref),
        gather=(gather_hbm, gather_ref), tally=(tally_hbm, tally_ref), fall=(fall_hbm, fall_ref),
        span_map=(span_map_hbm, span_map_ref), nbr_elem=(nbr_elem_hbm, nbr_elem_ref),
        nbr_side=(nbr_side_hbm, nbr_side_ref),
    )
    for n, (name, (source, target)) in enumerate(pairs.items()):
        copies[name] = pltpu.make_async_copy(source, target, in_sem.at[n])
        if n == 6:
            for k in range(CHUNKS):
                cut = slice(WIDE * k, min(WIDE * k + WIDE, NZ * NX * 3))
                copies[k] = pltpu.make_async_copy(
                    fields_hbm.at[:, cut], fields_ref.at[:, cut], field_sem.at[k]
                )
                copies[k].start()
        copies[name].start()

    lane = lax.broadcasted_iota(jnp.int32, (R, LANES), 1)
    row = lax.broadcasted_iota(jnp.int32, (R, LANES), 0)
    own = (lane & (R - 1)) == row
    zero16 = jnp.zeros((R, LANES), BF16)

    copies["state"].wait()
    copies["rise"].wait()
    copies["active"].wait()
    state = state_ref[...]
    profile = dot(rise_ref[0], state, ((1,), (1,))) + dot(rise_ref[1], state, ((1,), (1,)))
    flags = active_ref[...].reshape(1, COLS).astype(F32)
    p_high, p_low = halves(jnp.concatenate([jnp.exp(profile[:64]), profile[64:]], 0))
    prof_wide[...] = jnp.concatenate([p_high, p_low], 1).astype(F32)
    keep = jnp.concatenate([flags, flags], 1)
    prof_wide[63:64] = jnp.where(lane[:1] < COLS, keep, 0.0)
    wanted = [64 * f + z for f in range(3) for z in range(NZ)] + [63]
    for k in range(0, len(wanted), 8):
        lines = [prof_wide[i : i + 1] for i in wanted[k : k + 8]]
        lines = [jnp.where(own, jnp.broadcast_to(v, (R, LANES)), 0.0).astype(BF16) for v in lines]
        for i, v in zip(wanted[k : k + 8], lines):
            prof_rows[i] = v
    copies["spread"].wait()
    for f in range(3):
        top = 64 if f == 0 else NZ
        block = dot(prof_rows[64 * f : 64 * f + top].reshape(top * R, LANES), spread_ref[...])
        means[f, :top] = block.reshape(top, R, LANES)
    mask = means[0, 63] > 0.5

    for f in range(3):
        raw[f, 0] = zero16
        raw[f, NZ + 1] = zero16
    for k in range(CHUNKS):
        copies[k].wait()
        blocks = []
        for j in range(4 * k, 4 * k + 4):
            if j < 43:
                tiles = [fields_ref[R * g : R * g + R, LANES * j : LANES * j + LANES] for g in range(G)]
            else:
                tiles = [
                    jnp.concatenate([fields_ref[R * g : R * g + R, LANES * j :], zero16[:, :64]], 1)
                    for g in range(G)
                ]
            blocks.append(regroup(tiles))
        for j, block in enumerate(blocks):
            for part, level in zip(block, range(16 * k + 4 * j, min(16 * k + 4 * j + 4, 3 * NZ))):
                f, z = divmod(level, NZ)
                raw[f, z + 1] = part
    copies["dxm"].wait()
    for f in range(3):
        block = dot(raw[f, 1 : NZ + 1].reshape(ROWS, LANES), dxm_ref[...])
        dxm[f] = block.reshape(NZ, R, 2 * LANES)

    copies["density"].wait()
    copies["eigen"].wait()
    eigen = eigen_ref[...]
    inv[0] = jnp.zeros((R, LANES), F32)
    zero = inv[0]

    def factor(t, last):
        low, high, _ = last
        z = NZ - 1 - t
        rho, above = density_ref[t], density_ref[t + 1]
        below = jnp.where(t > 0, density_ref[jnp.maximum(t - 1, 0)], rho)
        f_up, f_down = 0.5 * (rho + above), 0.5 * (rho + below)
        i_low = 1.0 / ((eigen * rho + (f_up + f_down)) - f_down * low)
        e_low = f_up * i_low
        rho, below = density_ref[z], density_ref[z - 1]
        above = jnp.where(t > 0, density_ref[jnp.minimum(z + 1, NZ - 1)], rho)
        f_up, f_down = 0.5 * (rho + above), 0.5 * (rho + below)
        diag = (eigen * rho + (f_up + f_down)) - f_up * high
        i_high = 1.0 / diag
        e_high = f_down * i_high
        stores = [(inv, t, i_low), (coup, t, e_low), (inv, z, i_high), (coup, z, e_high)]
        return stores, (e_low, e_high, diag)

    def advect(z, carry):
        (u_m, u), (w_m, w), (q_m, q), (rw_mm, rw_m), rain = carry
        u_p, w_p, q_p = [raw[f, z + 2].astype(F32) for f in range(3)]
        rho = density_ref[z]
        half = 0.125 * w
        du, mean_u = dxm[0, z, :, :LANES], dxm[0, z, :, LANES:]
        dw = dxm[1, z, :, :LANES]
        dq, mean_q = dxm[2, z, :, :LANES], dxm[2, z, :, LANES:]
        new_u = u - u * du - half * (u_p - u_m) + (means[2, z] - mean_u)
        new_w = w - u * dw - half * (w_p - w_m) + (0.125 * q - 0.5 * mean_q)
        new_q = q - u * dq - half * (q_p - q_m) + (means[1, z] - mean_q)
        x = new_q - means[0, z]
        cond = jnp.maximum(x, 0.0) + jnp.log(1.0 + jnp.exp(-jnp.abs(x)))
        q2 = new_q - 0.5 * cond
        rw = rho * new_w
        stores = [
            (u1, z, new_u),
            (w1, z, new_w),
            (fresh, 2 * NZ + z, jnp.where(mask, q2, q).astype(BF16)),
            (cells.at[0], z, jnp.concatenate(halves(cond), 1)),
            (cells.at[1], z, jnp.concatenate(halves(q2 - q), 1)),
            (left.at[:, :, : 2 * LANES], z + 1, jnp.concatenate(halves(rho * new_u), 1)),
            (left.at[:, :, 2 * LANES :], z, jnp.concatenate(halves(0.5 * (rw - rw_mm)), 1)),
        ]
        return stores, ((u, u_p), (w, w_p), (q, q_p), (rw_m, rw), rain + rho * cond)

    def both_passes(t, carry):
        stores, last = factor(t, carry[0])
        more, levels = advect(2 * t, carry[1])
        most, levels = advect(2 * t + 1, levels)
        for ref, z, value in stores + more + most:
            ref[z] = value
        return last, levels

    first = tuple((zero, raw[f, 1].astype(F32)) for f in range(3)) + ((zero, zero), zero)
    last, levels = lax.fori_loop(0, NZ // 2, both_passes, ((zero, zero, zero), first))
    left[NZ, :, 2 * LANES :] = jnp.concatenate(halves(-0.5 * levels[3][0]), 1)
    mid = NZ // 2
    centre = 1.0 / (last[2] - 0.5 * (density_ref[mid - 1] + density_ref[mid]) * last[0])

    copies["gather"].wait()
    parts = dot(jnp.concatenate(halves(levels[4] * (2.0 / NZ)), 1), gather_ref[...])
    precip = jnp.sum(jnp.where(own, parts, 0.0), 0, keepdims=True)[:, :COLS]
    copies["span_map"].wait()
    order = lax.broadcasted_iota(jnp.int32, (spans, COLS), 0) + span
    target = jnp.where(order >= spans, order - spans, order)
    hot = jnp.where((span_map_ref[...].reshape(1, COLS) == target) & (flags > 0.5), 1.0, 0.0)
    upper = lax.broadcasted_iota(jnp.int32, (COLS, COLS), 0) < lax.broadcasted_iota(jnp.int32, (COLS, COLS), 1)
    before = dot(hot.astype(BF16), jnp.where(upper, 1.0, 0.0).astype(BF16))
    one = jnp.sum(jnp.where(before < 0.5, hot, 0.0) * precip, 1, keepdims=True)
    two = jnp.sum(jnp.where(before > 0.5, hot, 0.0) * precip, 1, keepdims=True)
    load = jnp.sum(hot, 1, keepdims=True)
    place = lax.broadcasted_iota(jnp.int32, (spans, LANES), 1)
    block = jnp.where(place < 32, load, jnp.where(place < 64, one, two))
    for i in range(spans):
        sent[i] = block[i : i + 1]
    mine = pltpu.make_async_copy(sent.at[0], got.at[span], out_sem)
    mine.start()

    pl.semaphore_wait(barrier, jnp.where(parity == 0, 2 * reach + 4, 4 * reach + 2))
    relays = [
        pltpu.make_async_remote_copy(
            src_ref=sent.at[pl.ds(first_row, count)], dst_ref=slot.at[parity], send_sem=relay_send.at[n],
            recv_sem=relay_recv.at[n, parity], device_id=along(offset, lead), device_id_type=MESH,
        )
        for n, (first_row, count, slot, offset) in enumerate(
            (
                (reach + 1, reach, from_lower, reach),
                (2 * reach + 1, reach - 1, from_upper, spans - reach),
            )
        )
    ]
    for relay in relays:
        relay.start()

    def give(source, slot, offset, sem=send_sem, where=region):
        pltpu.make_async_remote_copy(
            src_ref=source, dst_ref=got.at[slot], send_sem=sem, recv_sem=recv_sem,
            device_id=along(offset, where), device_id_type=MESH,
        ).start()

    def give_near(i, _):
        for offset in (reach - i, spans - reach + i):
            give(sent.at[offset], span, offset)
        return _

    lax.fori_loop(0, reach, give_near, 0)

    def give_back(k):
        blocks = []
        for j in range(4 * k, 4 * k + 4):
            blocks.append(
                regroup([fresh[v] if v < 3 * NZ else zero16 for v in range(4 * j, 4 * j + 4)])
            )
        for j, block in enumerate(blocks):
            j += 4 * k
            for g, part in enumerate(block):
                if j < 43:
                    fresh_ref[R * g : R * g + R, LANES * j : LANES * j + LANES] = part
                else:
                    fresh_ref[R * g : R * g + R, LANES * j :] = part[:, :64]

    for k in range(8, CHUNKS):
        give_back(k)

    copies["forward"].wait()
    right = dot(left[1:].reshape(ROWS, 4 * LANES), forward_ref[...])
    sol[...] = (right[:, :LANES] + right[:, LANES:]).reshape(NZ, R, LANES)
    low, high = sol[0], sol[NZ - 1]
    for t in range(1, mid):
        z = NZ - 1 - t
        low = sol[t] + coup[t - 1] * low
        high = sol[z] + coup[z + 1] * high
        sol[t], sol[z] = low, high
    high = centre * (high + coup[mid - 1] * low)
    low = inv[mid - 1] * low + coup[mid - 1] * high
    left[mid - 1, :, : 2 * LANES] = jnp.concatenate(halves(low), 1)
    left[mid, :, : 2 * LANES] = jnp.concatenate(halves(high), 1)
    for t in range(mid - 2, -1, -1):
        z = NZ - 1 - t
        low = inv[t] * sol[t] + coup[t] * low
        high = inv[z] * sol[z] + coup[z] * high
        left[t, :, : 2 * LANES] = jnp.concatenate(halves(low), 1)
        left[z, :, : 2 * LANES] = jnp.concatenate(halves(high), 1)
    copies["back"].wait()
    both = dot(left[:NZ, :, : 2 * LANES].reshape(ROWS, 2 * LANES), back_ref[...])
    pres[0] = zero
    pres[NZ + 1] = zero
    pres[1 : NZ + 1] = (both[:, :LANES] + both[:, 2 * LANES : 3 * LANES]).reshape(NZ, R, LANES)
    sol[...] = (both[:, LANES : 2 * LANES] + both[:, 3 * LANES :]).reshape(NZ, R, LANES)

    @pl.loop(0, NZ // 2)
    def _(t):
        z = 2 * t
        here = pl.ds(z, 2)
        u, w = raw[0, pl.ds(z + 1, 2)].astype(F32), raw[1, pl.ds(z + 1, 2)].astype(F32)
        u2 = u1[here] - sol[here]
        w2 = w1[here] - (pres[pl.ds(z + 2, 2)] - pres[here])
        u_out = jnp.where(mask[None], u2, u).astype(BF16)
        w_out = jnp.where(mask[None], w2, w).astype(BF16)
        change = jnp.concatenate(halves(u2 - u), 2)
        fresh[here] = u_out
        fresh[pl.ds(NZ + z, 2)] = w_out
        cells[2, here] = change

    for f in range(3):
        block = dot(cells[f].reshape(ROWS, 2 * LANES), gather_ref[...])
        means[f, :NZ] = block.reshape(NZ, R, LANES)
    lane_high = lane < COLS

    @pl.loop(0, NZ // 2)
    def _(t):
        here = pl.ds(2 * t, 2)
        values = []
        for f in range(3):
            value = jnp.where(own[None], means[f, here], 0.0)
            high = value.astype(BF16).astype(F32)
            values.append(jnp.where(lane_high[None], high, value - high).astype(BF16))
        left[here, :, : 3 * LANES] = jnp.concatenate(values, 2)

    copies["tally"].wait()
    sums = dot(tally_ref[...], left[:NZ, :, : 3 * LANES].reshape(ROWS, 3 * LANES))
    sums = jnp.concatenate([sums[:, LANES * f : LANES * f + LANES] for f in range(3)], 0)
    t_high, t_low = halves(jnp.where(keep > 0.5, sums, 0.0).T)
    copies["fall"].wait()
    tend = dot(t_high, fall_ref[0]) + dot(t_low, fall_ref[0]) + dot(t_high, fall_ref[1])
    tend_ref[...] = (tend[:COLS] + tend[COLS:]).astype(BF16)
    half = COLS // 2
    halos = [
        pltpu.make_async_remote_copy(
            src_ref=tend_ref.at[part], dst_ref=slot, send_sem=halo_send.at[n], recv_sem=halo_recv.at[n],
            device_id=other, device_id_type=MESH,
        )
        for n, (part, slot, other) in enumerate(
            ((pl.ds(half, half), from_left, next_device), (pl.ds(0, half), from_right, left_device))
        )
    ]
    for halo in halos:
        halo.start()

    passed = pl.ds(0, 4 * reach - 2)

    @pl.when(parity == 1)
    def _():
        for p in (1, 0):
            for n, slot in enumerate((from_lower, from_upper)):
                pltpu.make_async_copy(slot.at[p], slot.at[p], relay_recv.at[n, p]).wait()

            def pass_up(i, p=p):
                origin = lax.rem(span + spans - reach, spans)
                give(from_lower.at[p, i], origin, i + 1, pass_sem, region - 1 + p)

            def pass_on(i, _, p=p):
                pass_up(reach - 1 - i)
                origin = lax.rem(span + reach, spans)
                give(from_upper.at[p, i], origin, spans - reach + 1 + i, pass_sem, region - 1 + p)
                return _

            lax.fori_loop(0, reach - 1, pass_on, 0)
            pass_up(0)

    for k in range(8):
        give_back(k)

    copies["nbr_elem"].wait()
    copies["nbr_side"].wait()
    elems = COLS // 4
    cell = lax.broadcasted_iota(jnp.int32, (2 * COLS, elems), 0)
    elem, corner = cell >> 2, cell & 3
    c_low, c_high = corner & 1, corner >> 1
    home = lax.broadcasted_iota(jnp.int32, (2 * COLS, elems), 1) + elems // 2
    faces = (1 - c_high, c_low, c_high, 1 - c_low)
    everyone = total * elems
    picks = []
    for side in range(4):
        near = nbr_elem_ref[side : side + 1, :] - (me * elems - elems // 2)
        near = jnp.where(near < 0, near + everyone, near)
        near = jnp.where(near >= everyone, near - everyone, near)
        theirs = nbr_side_ref[side : side + 1, :]
        face = jnp.where(
            theirs < 2, jnp.where(theirs == 0, faces[0], faces[1]), jnp.where(theirs == 2, faces[2], faces[3])
        )
        pick = jnp.where(near == elem, face, 0) + jnp.where(home == elem, faces[side], 0)
        picks.append((0.5 * pick.astype(F32)).T.astype(BF16))

    for halo in halos:
        halo.wait()
    table = jnp.concatenate([from_left[...], tend_ref[...], from_right[...]], 0)
    for side in range(4):
        edge_ref[:, side, :] = dot(picks[side], table)
    for relay in relays:
        relay.wait_send()

    others = pl.ds(0, spans - 1)
    mine.wait()
    pltpu.make_async_copy(got.at[others], got.at[others], recv_sem).wait()
    near = pl.ds(0, 2 * reach)
    pltpu.make_async_copy(sent.at[near], sent.at[near], send_sem).wait()

    @pl.when(parity == 1)
    def _():
        pltpu.make_async_copy(sent.at[passed], sent.at[passed], pass_sem).wait()


def crm_call(shape, column_state, crm_fields, active, density, span_map, nbr_elem, nbr_side):
    constants = [jnp.asarray(a) for a in tables()]
    operands = (column_state, crm_fields, active, density, span_map, nbr_elem.T, nbr_side.T, *constants)
    hbm = pl.BlockSpec(memory_space=pltpu.HBM)
    levels = (NZ, R, LANES)
    spans = shape[1]
    return pl.pallas_call(
        functools.partial(crm_kernel, shape),
        out_shape=(
            jax.ShapeDtypeStruct((COLS, 4 * LEV), BF16),
            jax.ShapeDtypeStruct((COLS, 3 * NZ * NX), BF16),
            jax.ShapeDtypeStruct((spans, 1, LANES), F32),
            jax.ShapeDtypeStruct((COLS // 4, 4, 4 * LEV), F32),
        ),
        in_specs=[hbm] * (7 + len(constants)),
        out_specs=(pl.BlockSpec(memory_space=pltpu.VMEM),) * 4,
        scratch_shapes=[
            pltpu.VMEM((COLS, 4 * LEV), BF16),
            pltpu.VMEM((COLS, 3 * NZ * NX), BF16),
            pltpu.VMEM((COLS,), jnp.int32),
            pltpu.SMEM((NZ,), F32),
            pltpu.VMEM((COLS,), jnp.int32),
            pltpu.VMEM((4, COLS // 4), jnp.int32),
            pltpu.VMEM((4, COLS // 4), jnp.int32),
            *[pltpu.VMEM(a.shape, a.dtype) for a in constants],
            pltpu.VMEM((3, NZ + 2, R, LANES), BF16),
            pltpu.VMEM((3, NZ, R, 2 * LANES), F32),
            pltpu.VMEM((192, LANES), F32),
            pltpu.VMEM((192, R, LANES), BF16),
            pltpu.VMEM(levels, F32),
            pltpu.VMEM(levels, F32),
            pltpu.VMEM(levels, F32),
            pltpu.VMEM(levels, F32),
            pltpu.VMEM((NZ + 1, R, 4 * LANES), BF16),
            pltpu.VMEM(levels, F32),
            pltpu.VMEM((3, NZ, R, 2 * LANES), BF16),
            pltpu.VMEM((NZ + 2, R, LANES), F32),
            pltpu.VMEM((3, 64, R, LANES), F32),
            pltpu.VMEM((3 * NZ, R, LANES), BF16),
            pltpu.VMEM((COLS // 2, 4 * LEV), BF16),
            pltpu.VMEM((COLS // 2, 4 * LEV), BF16),
            pltpu.VMEM((spans, 1, LANES), F32),
            pltpu.VMEM((2, spans // 4, 1, LANES), F32),
            pltpu.VMEM((2, spans // 4 - 1, 1, LANES), F32),
            pltpu.SemaphoreType.DMA((15,)),
            pltpu.SemaphoreType.DMA((CHUNKS,)),
            pltpu.SemaphoreType.DMA,
            pltpu.SemaphoreType.DMA,
            pltpu.SemaphoreType.DMA,
            pltpu.SemaphoreType.DMA,
            pltpu.SemaphoreType.DMA((2,)),
            pltpu.SemaphoreType.DMA((2,)),
            pltpu.SemaphoreType.DMA((2,)),
            pltpu.SemaphoreType.DMA((2, 2)),
        ],
        compiler_params=pltpu.CompilerParams(
            collective_id=0, has_side_effects=True, vmem_limit_bytes=40 * 2**20
        ),
    )(*[pltpu.with_memory_space_constraint(a, pltpu.HBM) for a in operands])


def finish_kernel(tend, fresh, got, edge, tend_out, fresh_out, rows_out, edge_out, flat, rows_ref, went):
    pieces = [(tend, tend_out), (edge, edge_out)]
    for top in range(0, COLS, R):
        cut = pl.ds(top, R)
        pieces.append((fresh.at[cut], fresh_out.at[cut]))
    outward = [pltpu.make_async_copy(a, b, went.at[n]) for n, (a, b) in enumerate(pieces)]
    for copy in outward:
        copy.start()

    spans = got.shape[0]
    for i in range(spans):
        flat[i : i + 1] = got[i]
    table = flat[...]
    lower = lax.broadcasted_iota(jnp.int32, (spans, spans), 0) > lax.broadcasted_iota(jnp.int32, (spans, spans), 1)
    start = dot(jnp.where(lower, 1.0, 0.0).astype(BF16), table.astype(BF16))
    one, two = pltpu.roll(table, LANES - 32, 1), pltpu.roll(table, LANES - 64, 1)
    slot = lax.broadcasted_iota(jnp.int32, (spans, LANES), 1).astype(F32)
    rows = jnp.where((start == slot) & (table > 0.5), one, 0.0)
    rows += jnp.where((start + 1.0 == slot) & (table > 1.5), two, 0.0)
    rows_ref[...] = jnp.sum(rows, 0, keepdims=True)[:, : rows_ref.shape[1]]
    last = pltpu.make_async_copy(rows_ref, rows_out, went.at[len(pieces)])
    last.start()
    for copy in outward:
        copy.wait()
    last.wait()


def finish(slots, tendency, fresh, got, edges):
    hbm, vmem = pl.BlockSpec(memory_space=pltpu.HBM), pl.BlockSpec(memory_space=pltpu.VMEM)
    shapes = [jax.ShapeDtypeStruct(a.shape, a.dtype) for a in (tendency, fresh, got, edges)]
    shapes[2] = jax.ShapeDtypeStruct((1, slots), F32)
    return pl.pallas_call(
        finish_kernel,
        out_shape=tuple(shapes),
        in_specs=[vmem] * 4,
        out_specs=(hbm,) * 4,
        scratch_shapes=[
            pltpu.VMEM((got.shape[0], LANES), F32),
            pltpu.VMEM((1, slots), F32),
            pltpu.SemaphoreType.DMA((7,)),
        ],
        compiler_params=pltpu.CompilerParams(vmem_limit_bytes=16 * 2**20),
    )(tendency, fresh, got, edges)


def body(shape, column_state, crm_fields, span_map, active, density, nbr_elem, nbr_side):
    results = crm_call(
        shape, column_state, crm_fields, active, density, span_map, nbr_elem, nbr_side
    )
    tendency, fresh, rows, edge_sums = finish(COLS * 3 // 8, *results)
    return (tendency, fresh, rows[0], edge_sums)


def solution(mesh):
    rows = P(("region", "span"), None)
    line = P(("region", "span"))
    return jax.shard_map(
        functools.partial(body, (mesh.shape["region"], mesh.shape["span"])),
        mesh=mesh,
        in_specs=(rows, rows, line, line, P(), rows, rows),
        out_specs=(rows, rows, line, P(("region", "span"), None, None)),
        check_vma=False,
    )
```

```python
import functools

import jax
import jax.numpy as jnp
import ml_dtypes
import numpy as np
from jax import lax
from jax.experimental import pallas as pl
from jax.experimental.pallas import tpu as pltpu
from jax.sharding import PartitionSpec as P

MESH = pl.DeviceIdType.MESH
LEV, NZ, NX, COLS = 72, 58, 32, 64
G, R, LANES = 4, 16, 128
ROWS = NZ * R
WIDE, CHUNKS = 512, 11
F32, BF16 = jnp.float32, jnp.bfloat16


def split(a):
    high = a.astype(ml_dtypes.bfloat16)
    return high, (a - high.astype(np.float64)).astype(ml_dtypes.bfloat16)


def level_map(count_to, count_from):
    index = np.arange(count_to)
    numerator = (2 * index + 1) * count_from - count_to
    lower = np.clip(numerator // (2 * count_to), 0, count_from - 2)
    fraction = np.clip((numerator - lower * 2 * count_to) / (2 * count_to), 0.0, 1.0)
    target = np.arange(count_from)[None, :]
    return (1 - fraction)[:, None] * (target == lower[:, None]) + fraction[:, None] * (
        target == lower[:, None] + 1
    )


@functools.cache
def tables():
    eye = np.eye(G)
    step = 0.5 * (np.roll(np.eye(NX), 1, 0) - np.roll(np.eye(NX), -1, 0))
    dxm = np.concatenate(
        [np.kron(eye, 0.25 * step), np.kron(eye, np.full((NX, NX), 0.25 / NX))], 1
    ).astype(ml_dtypes.bfloat16)
    mode = np.arange(NX)
    wave = np.where(mode <= NX // 2, mode, mode - NX // 2)
    phase = 2 * np.pi * (wave[:, None] * np.arange(NX)[None, :] % NX) / NX
    norm = np.where((mode == 0) | (mode == NX // 2), np.sqrt(1 / NX), np.sqrt(2 / NX))
    four = norm[:, None] * np.where((mode <= NX // 2)[:, None], np.cos(phase), np.sin(phase))
    eigen = np.tile(2 - 2 * np.cos(2 * np.pi * wave / NX), G)[None, :]
    eigen = np.broadcast_to(eigen, (R, LANES)).astype(np.float32)

    def doubled(a):
        return np.concatenate(split(a), 1)

    to_mode = -four.T
    forward = np.concatenate(
        [doubled(np.kron(eye, a)) for a in (step @ to_mode, step @ to_mode, to_mode, to_mode)], 0
    )
    back = np.concatenate([np.kron(eye, 0.5 * four), np.kron(eye, four @ step)], 1)
    back = np.concatenate([doubled(back)] * 2, 0)
    up = level_map(NZ, LEV)
    zero = np.zeros_like(up)
    blocks = [
        [0.3 * up, zero, zero, zero],
        [zero, 0.25 * up, zero, 0.25 * up],
        [zero, zero, 0.25 * up, zero],
    ]
    rise = np.zeros((192, 4 * LEV))
    for i, row in enumerate(blocks):
        rise[64 * i : 64 * i + NZ] = np.concatenate(row, 1)
    rise = np.stack(split(rise))
    column, lane = np.arange(LANES) % COLS, np.arange(LANES)
    spread = (column[:, None] // R == lane[None, :] // NX).astype(ml_dtypes.bfloat16)
    gather = (lane[:, None] // NX == column[None, :] // R) / NX
    gather = np.concatenate([gather, gather], 0).astype(ml_dtypes.bfloat16)
    tally = np.zeros((64, ROWS))
    for z in range(NZ):
        tally[z, R * z : R * z + R] = 1
    tally = tally.astype(ml_dtypes.bfloat16)
    down = level_map(LEV, NZ)
    fall = np.zeros((4 * LEV, 192))
    for f, (source, gain) in enumerate(((0, 2.0), (1, 4.0), (2, 4.0), (0, 0.5))):
        fall[LEV * f : LEV * f + LEV, 64 * source : 64 * source + NZ] = gain * down
    fall = np.stack(split(fall.T))
    return dxm, forward, back, eigen, rise, spread, gather, tally, fall


def dot(a, b, dims=((1,), (0,)), precision=None):
    return lax.dot_general(a, b, (dims, ((), ())), precision=precision, preferred_element_type=F32)


def halves(a):
    high = a.astype(BF16)
    return high, (a - high.astype(F32)).astype(BF16)


def regroup(parts):
    lane = lax.broadcasted_iota(jnp.int32, (R, LANES), 1)
    low, even = lane < 64, (lane & 32) == 0
    a, b, c, d = parts
    a, c = jnp.where(low, a, pltpu.roll(c, 64, 1)), jnp.where(low, pltpu.roll(a, 64, 1), c)
    b, d = jnp.where(low, b, pltpu.roll(d, 64, 1)), jnp.where(low, pltpu.roll(b, 64, 1), d)
    a, b = jnp.where(even, a, pltpu.roll(b, 32, 1)), jnp.where(even, pltpu.roll(a, 96, 1), b)
    c, d = jnp.where(even, c, pltpu.roll(d, 32, 1)), jnp.where(even, pltpu.roll(c, 96, 1), d)
    return a, b, c, d


def crm_kernel(
    shape,
    state_hbm, fields_hbm, active_hbm, density_hbm, span_map_hbm, nbr_elem_hbm, nbr_side_hbm,
    dxm_hbm, forward_hbm, back_hbm, eigen_hbm, rise_hbm, spread_hbm, gather_hbm, tally_hbm, fall_hbm,
    tend_ref, fresh_ref, got, edge_ref,
    state_ref, fields_ref, active_ref, density_ref, span_map_ref, nbr_elem_ref, nbr_side_ref,
    dxm_ref, forward_ref, back_ref, eigen_ref, rise_ref, spread_ref, gather_ref, tally_ref, fall_ref,
    raw, dxm, prof_wide, prof_rows, inv, coup, u1, w1, left, sol, cells, pres, means, fresh,
    from_left, from_right, sent, from_lower, from_upper,
    in_sem, field_sem, out_sem, send_sem, recv_sem, pass_sem, halo_send, halo_recv, relay_send, relay_recv,
):
    regions, spans = shape
    reach = spans // 4
    region, span = lax.axis_index("region"), lax.axis_index("span")
    me = region * spans + span
    total = regions * spans
    next_device, left_device = lax.rem(me + 1, total), lax.rem(me + total - 1, total)
    next_device = (lax.div(next_device, spans), lax.rem(next_device, spans))
    left_device = (lax.div(left_device, spans), lax.rem(left_device, spans))

    parity = lax.rem(region, 2)
    lead = region + 1 - parity

    def along(offset, where=region):
        return (where, lax.rem(span + offset, spans))

    barrier = pltpu.get_barrier_semaphore()

    def greet(i, _):
        for offset in (reach - i, spans - reach + i):
            pl.semaphore_signal(barrier, inc=1, device_id=along(offset), device_id_type=MESH)
        return _

    lax.fori_loop(0, reach, greet, 0)

    def greet_lead(i, _):
        for offset in (reach - i, spans - reach + i):
            pl.semaphore_signal(barrier, inc=1, device_id=along(offset, lead), device_id_type=MESH)
        return _

    @pl.when(parity == 0)
    def _():
        lax.fori_loop(0, reach, greet_lead, 0)

    @pl.when(parity == 1)
    def _():
        for offset in (reach, spans - reach):
            pl.semaphore_signal(
                barrier, inc=1, device_id=along(offset, region - 1), device_id_type=MESH
            )

    for other in (left_device, next_device):
        pl.semaphore_signal(barrier, inc=1, device_id=other, device_id_type=MESH)

    copies = {}
    pairs = dict(
        state=(state_hbm, state_ref), rise=(rise_hbm, rise_ref), active=(active_hbm, active_ref),
        spread=(spread_hbm, spread_ref), dxm=(dxm_hbm, dxm_ref), density=(density_hbm, density_ref),
        eigen=(eigen_hbm, eigen_ref), forward=(forward_hbm, forward_ref), back=(back_hbm, back_ref),
        gather=(gather_hbm, gather_ref), tally=(tally_hbm, tally_ref), fall=(fall_hbm, fall_ref),
        span_map=(span_map_hbm, span_map_ref), nbr_elem=(nbr_elem_hbm, nbr_elem_ref),
        nbr_side=(nbr_side_hbm, nbr_side_ref),
    )
    for n, (name, (source, target)) in enumerate(pairs.items()):
        copies[name] = pltpu.make_async_copy(source, target, in_sem.at[n])
        if n == 6:
            for k in range(CHUNKS):
                cut = slice(WIDE * k, min(WIDE * k + WIDE, NZ * NX * 3))
                copies[k] = pltpu.make_async_copy(
                    fields_hbm.at[:, cut], fields_ref.at[:, cut], field_sem.at[k]
                )
                copies[k].start()
        copies[name].start()

    lane = lax.broadcasted_iota(jnp.int32, (R, LANES), 1)
    row = lax.broadcasted_iota(jnp.int32, (R, LANES), 0)
    own = (lane & (R - 1)) == row
    zero16 = jnp.zeros((R, LANES), BF16)

    copies["state"].wait()
    copies["rise"].wait()
    copies["active"].wait()
    state = state_ref[...]
    profile = dot(rise_ref[0], state, ((1,), (1,))) + dot(rise_ref[1], state, ((1,), (1,)))
    flags = active_ref[...].reshape(1, COLS).astype(F32)
    p_high, p_low = halves(jnp.concatenate([jnp.exp(profile[:64]), profile[64:]], 0))
    prof_wide[...] = jnp.concatenate([p_high, p_low], 1).astype(F32)
    keep = jnp.concatenate([flags, flags], 1)
    prof_wide[63:64] = jnp.where(lane[:1] < COLS, keep, 0.0)
    wanted = [64 * f + z for f in range(3) for z in range(NZ)] + [63]
    for k in range(0, len(wanted), 8):
        lines = [prof_wide[i : i + 1] for i in wanted[k : k + 8]]
        lines = [jnp.where(own, jnp.broadcast_to(v, (R, LANES)), 0.0).astype(BF16) for v in lines]
        for i, v in zip(wanted[k : k + 8], lines):
            prof_rows[i] = v
    copies["spread"].wait()
    for f in range(3):
        top = 64 if f == 0 else NZ
        block = dot(prof_rows[64 * f : 64 * f + top].reshape(top * R, LANES), spread_ref[...])
        means[f, :top] = block.reshape(top, R, LANES)
    mask = means[0, 63] > 0.5

    for f in range(3):
        raw[f, 0] = zero16
        raw[f, NZ + 1] = zero16
    for k in range(CHUNKS):
        copies[k].wait()
        blocks = []
        for j in range(4 * k, 4 * k + 4):
            if j < 43:
                tiles = [fields_ref[R * g : R * g + R, LANES * j : LANES * j + LANES] for g in range(G)]
            else:
                tiles = [
                    jnp.concatenate([fields_ref[R * g : R * g + R, LANES * j :], zero16[:, :64]], 1)
                    for g in range(G)
                ]
            blocks.append(regroup(tiles))
        for j, block in enumerate(blocks):
            for part, level in zip(block, range(16 * k + 4 * j, min(16 * k + 4 * j + 4, 3 * NZ))):
                f, z = divmod(level, NZ)
                raw[f, z + 1] = part
    copies["dxm"].wait()
    for f in range(3):
        block = dot(raw[f, 1 : NZ + 1].reshape(ROWS, LANES), dxm_ref[...])
        dxm[f] = block.reshape(NZ, R, 2 * LANES)

    copies["density"].wait()
    copies["eigen"].wait()
    eigen = eigen_ref[...]
    inv[0] = jnp.zeros((R, LANES), F32)
    zero = inv[0]

    def factor(t, last):
        low, high, _ = last
        z = NZ - 1 - t
        rho, above = density_ref[t], density_ref[t + 1]
        below = jnp.where(t > 0, density_ref[jnp.maximum(t - 1, 0)], rho)
        f_up, f_down = 0.5 * (rho + above), 0.5 * (rho + below)
        i_low = 1.0 / ((eigen * rho + (f_up + f_down)) - f_down * low)
        e_low = f_up * i_low
        rho, below = density_ref[z], density_ref[z - 1]
        above = jnp.where(t > 0, density_ref[jnp.minimum(z + 1, NZ - 1)], rho)
        f_up, f_down = 0.5 * (rho + above), 0.5 * (rho + below)
        diag = (eigen * rho + (f_up + f_down)) - f_up * high
        i_high = 1.0 / diag
        e_high = f_down * i_high
        stores = [(inv, t, i_low), (coup, t, e_low), (inv, z, i_high), (coup, z, e_high)]
        return stores, (e_low, e_high, diag)

    def advect(z, carry):
        (u_m, u), (w_m, w), (q_m, q), (rw_mm, rw_m), rain = carry
        u_p, w_p, q_p = [raw[f, z + 2].astype(F32) for f in range(3)]
        rho = density_ref[z]
        half = 0.125 * w
        du, mean_u = dxm[0, z, :, :LANES], dxm[0, z, :, LANES:]
        dw = dxm[1, z, :, :LANES]
        dq, mean_q = dxm[2, z, :, :LANES], dxm[2, z, :, LANES:]
        new_u = u - u * du - half * (u_p - u_m) + (means[2, z] - mean_u)
        new_w = w - u * dw - half * (w_p - w_m) + (0.125 * q - 0.5 * mean_q)
        new_q = q - u * dq - half * (q_p - q_m) + (means[1, z] - mean_q)
        x = new_q - means[0, z]
        cond = jnp.maximum(x, 0.0) + jnp.log(1.0 + jnp.exp(-jnp.abs(x)))
        q2 = new_q - 0.5 * cond
        rw = rho * new_w
        stores = [
            (u1, z, new_u),
            (w1, z, new_w),
            (fresh, 2 * NZ + z, jnp.where(mask, q2, q).astype(BF16)),
            (cells.at[0], z, jnp.concatenate(halves(cond), 1)),
            (cells.at[1], z, jnp.concatenate(halves(q2 - q), 1)),
            (left.at[:, :, : 2 * LANES], z + 1, jnp.concatenate(halves(rho * new_u), 1)),
            (left.at[:, :, 2 * LANES :], z, jnp.concatenate(halves(0.5 * (rw - rw_mm)), 1)),
        ]
        return stores, ((u, u_p), (w, w_p), (q, q_p), (rw_m, rw), rain + rho * cond)

    def both_passes(t, carry):
        stores, last = factor(t, carry[0])
        more, levels = advect(2 * t, carry[1])
        most, levels = advect(2 * t + 1, levels)
        for ref, z, value in stores + more + most:
            ref[z] = value
        return last, levels

    first = tuple((zero, raw[f, 1].astype(F32)) for f in range(3)) + ((zero, zero), zero)
    last, levels = lax.fori_loop(0, NZ // 2, both_passes, ((zero, zero, zero), first))
    left[NZ, :, 2 * LANES :] = jnp.concatenate(halves(-0.5 * levels[3][0]), 1)
    mid = NZ // 2
    centre = 1.0 / (last[2] - 0.5 * (density_ref[mid - 1] + density_ref[mid]) * last[0])

    copies["gather"].wait()
    parts = dot(jnp.concatenate(halves(levels[4] * (2.0 / NZ)), 1), gather_ref[...])
    precip = jnp.sum(jnp.where(own, parts, 0.0), 0, keepdims=True)[:, :COLS]
    copies["span_map"].wait()
    order = lax.broadcasted_iota(jnp.int32, (spans, COLS), 0) + span
    target = jnp.where(order >= spans, order - spans, order)
    hot = jnp.where((span_map_ref[...].reshape(1, COLS) == target) & (flags > 0.5), 1.0, 0.0)
    upper = lax.broadcasted_iota(jnp.int32, (COLS, COLS), 0) < lax.broadcasted_iota(jnp.int32, (COLS, COLS), 1)
    before = dot(hot.astype(BF16), jnp.where(upper, 1.0, 0.0).astype(BF16))
    one = jnp.sum(jnp.where(before < 0.5, hot, 0.0) * precip, 1, keepdims=True)
    two = jnp.sum(jnp.where(before > 0.5, hot, 0.0) * precip, 1, keepdims=True)
    load = jnp.sum(hot, 1, keepdims=True)
    place = lax.broadcasted_iota(jnp.int32, (spans, LANES), 1)
    block = jnp.where(place < 32, load, jnp.where(place < 64, one, two))
    for i in range(spans):
        sent[i] = block[i : i + 1]
    mine = pltpu.make_async_copy(sent.at[0], got.at[span], out_sem)
    mine.start()

    pl.semaphore_wait(barrier, jnp.where(parity == 0, 2 * reach + 4, 4 * reach + 2))
    relays = [
        pltpu.make_async_remote_copy(
            src_ref=sent.at[pl.ds(first_row, count)], dst_ref=slot.at[parity], send_sem=relay_send.at[n],
            recv_sem=relay_recv.at[n, parity], device_id=along(offset, lead), device_id_type=MESH,
        )
        for n, (first_row, count, slot, offset) in enumerate(
            (
                (reach + 1, reach, from_lower, reach),
                (2 * reach + 1, reach - 1, from_upper, spans - reach),
            )
        )
    ]
    for relay in relays:
        relay.start()

    def give(source, slot, offset, sem=send_sem, where=region):
        pltpu.make_async_remote_copy(
            src_ref=source, dst_ref=got.at[slot], send_sem=sem, recv_sem=recv_sem,
            device_id=along(offset, where), device_id_type=MESH,
        ).start()

    def give_near(i, _):
        for offset in (reach - i, spans - reach + i):
            give(sent.at[offset], span, offset)
        return _

    lax.fori_loop(0, reach, give_near, 0)

    def give_back(k):
        blocks = []
        for j in range(4 * k, 4 * k + 4):
            blocks.append(
                regroup([fresh[v] if v < 3 * NZ else zero16 for v in range(4 * j, 4 * j + 4)])
            )
        for j, block in enumerate(blocks):
            j += 4 * k
            for g, part in enumerate(block):
                if j < 43:
                    fresh_ref[R * g : R * g + R, LANES * j : LANES * j + LANES] = part
                else:
                    fresh_ref[R * g : R * g + R, LANES * j :] = part[:, :64]

    for k in range(8, CHUNKS):
        give_back(k)

    copies["forward"].wait()
    right = dot(left[1:].reshape(ROWS, 4 * LANES), forward_ref[...])
    sol[...] = (right[:, :LANES] + right[:, LANES:]).reshape(NZ, R, LANES)
    low, high = sol[0], sol[NZ - 1]
    for t in range(1, mid):
        z = NZ - 1 - t
        low = sol[t] + coup[t - 1] * low
        high = sol[z] + coup[z + 1] * high
        sol[t], sol[z] = low, high
    high = centre * (high + coup[mid - 1] * low)
    low = inv[mid - 1] * low + coup[mid - 1] * high
    left[mid - 1, :, : 2 * LANES] = jnp.concatenate(halves(low), 1)
    left[mid, :, : 2 * LANES] = jnp.concatenate(halves(high), 1)
    for t in range(mid - 2, -1, -1):
        z = NZ - 1 - t
        low = inv[t] * sol[t] + coup[t] * low
        high = inv[z] * sol[z] + coup[z] * high
        left[t, :, : 2 * LANES] = jnp.concatenate(halves(low), 1)
        left[z, :, : 2 * LANES] = jnp.concatenate(halves(high), 1)
    copies["back"].wait()
    both = dot(left[:NZ, :, : 2 * LANES].reshape(ROWS, 2 * LANES), back_ref[...])
    pres[0] = zero
    pres[NZ + 1] = zero
    pres[1 : NZ + 1] = (both[:, :LANES] + both[:, 2 * LANES : 3 * LANES]).reshape(NZ, R, LANES)
    sol[...] = (both[:, LANES : 2 * LANES] + both[:, 3 * LANES :]).reshape(NZ, R, LANES)

    @pl.loop(0, NZ // 2)
    def _(t):
        z = 2 * t
        here = pl.ds(z, 2)
        u, w = raw[0, pl.ds(z + 1, 2)].astype(F32), raw[1, pl.ds(z + 1, 2)].astype(F32)
        u2 = u1[here] - sol[here]
        w2 = w1[here] - (pres[pl.ds(z + 2, 2)] - pres[here])
        u_out = jnp.where(mask[None], u2, u).astype(BF16)
        w_out = jnp.where(mask[None], w2, w).astype(BF16)
        change = jnp.concatenate(halves(u2 - u), 2)
        fresh[here] = u_out
        fresh[pl.ds(NZ + z, 2)] = w_out
        cells[2, here] = change

    for f in range(3):
        block = dot(cells[f].reshape(ROWS, 2 * LANES), gather_ref[...])
        means[f, :NZ] = block.reshape(NZ, R, LANES)
    lane_high = lane < COLS

    @pl.loop(0, NZ // 2)
    def _(t):
        here = pl.ds(2 * t, 2)
        values = []
        for f in range(3):
            value = jnp.where(own[None], means[f, here], 0.0)
            high = value.astype(BF16).astype(F32)
            values.append(jnp.where(lane_high[None], high, value - high).astype(BF16))
        left[here, :, : 3 * LANES] = jnp.concatenate(values, 2)

    copies["tally"].wait()
    sums = dot(tally_ref[...], left[:NZ, :, : 3 * LANES].reshape(ROWS, 3 * LANES))
    sums = jnp.concatenate([sums[:, LANES * f : LANES * f + LANES] for f in range(3)], 0)
    t_high, t_low = halves(jnp.where(keep > 0.5, sums, 0.0).T)
    copies["fall"].wait()
    tend = dot(t_high, fall_ref[0]) + dot(t_low, fall_ref[0]) + dot(t_high, fall_ref[1])
    tend_ref[...] = (tend[:COLS] + tend[COLS:]).astype(BF16)
    half = COLS // 2
    halos = [
        pltpu.make_async_remote_copy(
            src_ref=tend_ref.at[part], dst_ref=slot, send_sem=halo_send.at[n], recv_sem=halo_recv.at[n],
            device_id=other, device_id_type=MESH,
        )
        for n, (part, slot, other) in enumerate(
            ((pl.ds(half, half), from_left, next_device), (pl.ds(0, half), from_right, left_device))
        )
    ]
    for halo in halos:
        halo.start()

    passed = pl.ds(0, 4 * reach - 2)

    @pl.when(parity == 1)
    def _():
        for p in (1, 0):
            for n, slot in enumerate((from_lower, from_upper)):
                pltpu.make_async_copy(slot.at[p], slot.at[p], relay_recv.at[n, p]).wait()

            def pass_up(i, p=p):
                origin = lax.rem(span + spans - reach, spans)
                give(from_lower.at[p, i], origin, i + 1, pass_sem, region - 1 + p)

            def pass_on(i, _, p=p):
                pass_up(reach - 1 - i)
                origin = lax.rem(span + reach, spans)
                give(from_upper.at[p, i], origin, spans - reach + 1 + i, pass_sem, region - 1 + p)
                return _

            lax.fori_loop(0, reach - 1, pass_on, 0)
            pass_up(0)

    for k in range(8):
        give_back(k)

    copies["nbr_elem"].wait()
    copies["nbr_side"].wait()
    elems = COLS // 4
    cell = lax.broadcasted_iota(jnp.int32, (2 * COLS, elems), 0)
    elem, corner = cell >> 2, cell & 3
    c_low, c_high = corner & 1, corner >> 1
    home = lax.broadcasted_iota(jnp.int32, (2 * COLS, elems), 1) + elems // 2
    faces = (1 - c_high, c_low, c_high, 1 - c_low)
    everyone = total * elems
    picks = []
    for side in range(4):
        near = nbr_elem_ref[side : side + 1, :] - (me * elems - elems // 2)
        near = jnp.where(near < 0, near + everyone, near)
        near = jnp.where(near >= everyone, near - everyone, near)
        theirs = nbr_side_ref[side : side + 1, :]
        face = jnp.where(
            theirs < 2, jnp.where(theirs == 0, faces[0], faces[1]), jnp.where(theirs == 2, faces[2], faces[3])
        )
        pick = jnp.where(near == elem, face, 0) + jnp.where(home == elem, faces[side], 0)
        picks.append((0.5 * pick.astype(F32)).T.astype(BF16))

    for halo in halos:
        halo.wait()
    table = jnp.concatenate([from_left[...], tend_ref[...], from_right[...]], 0)
    for side in range(4):
        edge_ref[:, side, :] = dot(picks[side], table)
    for relay in relays:
        relay.wait_send()

    others = pl.ds(0, spans - 1)
    mine.wait()
    pltpu.make_async_copy(got.at[others], got.at[others], recv_sem).wait()
    near = pl.ds(0, 2 * reach)
    pltpu.make_async_copy(sent.at[near], sent.at[near], send_sem).wait()

    @pl.when(parity == 1)
    def _():
        pltpu.make_async_copy(sent.at[passed], sent.at[passed], pass_sem).wait()


def crm_call(shape, column_state, crm_fields, active, density, span_map, nbr_elem, nbr_side):
    constants = [jnp.asarray(a) for a in tables()]
    operands = (column_state, crm_fields, active, density, span_map, nbr_elem.T, nbr_side.T, *constants)
    hbm = pl.BlockSpec(memory_space=pltpu.HBM)
    levels = (NZ, R, LANES)
    spans = shape[1]
    return pl.pallas_call(
        functools.partial(crm_kernel, shape),
        out_shape=(
            jax.ShapeDtypeStruct((COLS, 4 * LEV), BF16),
            jax.ShapeDtypeStruct((COLS, 3 * NZ * NX), BF16),
            jax.ShapeDtypeStruct((spans, 1, LANES), F32),
            jax.ShapeDtypeStruct((COLS // 4, 4, 4 * LEV), F32),
        ),
        in_specs=[hbm] * (7 + len(constants)),
        out_specs=(pl.BlockSpec(memory_space=pltpu.VMEM),) * 4,
        scratch_shapes=[
            pltpu.VMEM((COLS, 4 * LEV), BF16),
            pltpu.VMEM((COLS, 3 * NZ * NX), BF16),
            pltpu.VMEM((COLS,), jnp.int32),
            pltpu.SMEM((NZ,), F32),
            pltpu.VMEM((COLS,), jnp.int32),
            pltpu.VMEM((4, COLS // 4), jnp.int32),
            pltpu.VMEM((4, COLS // 4), jnp.int32),
            *[pltpu.VMEM(a.shape, a.dtype) for a in constants],
            pltpu.VMEM((3, NZ + 2, R, LANES), BF16),
            pltpu.VMEM((3, NZ, R, 2 * LANES), F32),
            pltpu.VMEM((192, LANES), F32),
            pltpu.VMEM((192, R, LANES), BF16),
            pltpu.VMEM(levels, F32),
            pltpu.VMEM(levels, F32),
            pltpu.VMEM(levels, F32),
            pltpu.VMEM(levels, F32),
            pltpu.VMEM((NZ + 1, R, 4 * LANES), BF16),
            pltpu.VMEM(levels, F32),
            pltpu.VMEM((3, NZ, R, 2 * LANES), BF16),
            pltpu.VMEM((NZ + 2, R, LANES), F32),
            pltpu.VMEM((3, 64, R, LANES), F32),
            pltpu.VMEM((3 * NZ, R, LANES), BF16),
            pltpu.VMEM((COLS // 2, 4 * LEV), BF16),
            pltpu.VMEM((COLS // 2, 4 * LEV), BF16),
            pltpu.VMEM((spans, 1, LANES), F32),
            pltpu.VMEM((2, spans // 4, 1, LANES), F32),
            pltpu.VMEM((2, spans // 4 - 1, 1, LANES), F32),
            pltpu.SemaphoreType.DMA((15,)),
            pltpu.SemaphoreType.DMA((CHUNKS,)),
            pltpu.SemaphoreType.DMA,
            pltpu.SemaphoreType.DMA,
            pltpu.SemaphoreType.DMA,
            pltpu.SemaphoreType.DMA,
            pltpu.SemaphoreType.DMA((2,)),
            pltpu.SemaphoreType.DMA((2,)),
            pltpu.SemaphoreType.DMA((2,)),
            pltpu.SemaphoreType.DMA((2, 2)),
        ],
        compiler_params=pltpu.CompilerParams(
            collective_id=0, has_side_effects=True, vmem_limit_bytes=40 * 2**20
        ),
    )(*[pltpu.with_memory_space_constraint(a, pltpu.HBM) for a in operands])


def finish_kernel(tend, fresh, got, edge, tend_out, fresh_out, rows_out, edge_out, flat, rows_ref, went):
    pieces = [(tend, tend_out), (edge, edge_out)]
    for top in range(0, COLS, R):
        cut = pl.ds(top, R)
        pieces.append((fresh.at[cut], fresh_out.at[cut]))
    outward = [pltpu.make_async_copy(a, b, went.at[n]) for n, (a, b) in enumerate(pieces)]
    for copy in outward:
        copy.start()

    spans = got.shape[0]
    for i in range(spans):
        flat[i : i + 1] = got[i]
    table = flat[...]
    lower = lax.broadcasted_iota(jnp.int32, (spans, spans), 0) > lax.broadcasted_iota(jnp.int32, (spans, spans), 1)
    start = dot(jnp.where(lower, 1.0, 0.0).astype(BF16), table.astype(BF16))
    one, two = pltpu.roll(table, LANES - 32, 1), pltpu.roll(table, LANES - 64, 1)
    slot = lax.broadcasted_iota(jnp.int32, (spans, LANES), 1).astype(F32)
    rows = jnp.where((start == slot) & (table > 0.5), one, 0.0)
    rows += jnp.where((start + 1.0 == slot) & (table > 1.5), two, 0.0)
    rows_ref[...] = jnp.sum(rows, 0, keepdims=True)[:, : rows_ref.shape[1]]
    last = pltpu.make_async_copy(rows_ref, rows_out, went.at[len(pieces)])
    last.start()
    for copy in outward:
        copy.wait()
    last.wait()


def finish(slots, tendency, fresh, got, edges):
    hbm, vmem = pl.BlockSpec(memory_space=pltpu.HBM), pl.BlockSpec(memory_space=pltpu.VMEM)
    shapes = [jax.ShapeDtypeStruct(a.shape, a.dtype) for a in (tendency, fresh, got, edges)]
    shapes[2] = jax.ShapeDtypeStruct((1, slots), F32)
    return pl.pallas_call(
        finish_kernel,
        out_shape=tuple(shapes),
        in_specs=[vmem] * 4,
        out_specs=(hbm,) * 4,
        scratch_shapes=[
            pltpu.VMEM((got.shape[0], LANES), F32),
            pltpu.VMEM((1, slots), F32),
            pltpu.SemaphoreType.DMA((7,)),
        ],
        compiler_params=pltpu.CompilerParams(vmem_limit_bytes=16 * 2**20),
    )(tendency, fresh, got, edges)


def body(shape, column_state, crm_fields, span_map, active, density, nbr_elem, nbr_side):
    results = crm_call(
        shape, column_state, crm_fields, active, density, span_map, nbr_elem, nbr_side
    )
    tendency, fresh, rows, edge_sums = finish(COLS * 3 // 8, *results)
    return (tendency, fresh, rows[0], edge_sums)


def solution(mesh):
    rows = P(("region", "span"), None)
    line = P(("region", "span"))
    return jax.shard_map(
        functools.partial(body, (mesh.shape["region"], mesh.shape["span"])),
        mesh=mesh,
        in_specs=(rows, rows, line, line, P(), rows, rows),
        out_specs=(rows, rows, line, P(("region", "span"), None, None)),
        check_vma=False,
    )
```
